32 devices in a mesh: ctx: 8 (over z, core), head: 4 (over y, x).
Axes of the slice: x: 2, y: 2, z: 4, core: 2. Of those that a mesh axis runs over, the one named last changes fastest.
Arguments:
- queries: bfloat16 [2, 12288, 4096], P(None, 'ctx', 'head')
- layer_keys_input: bfloat16 [2, 12288, 2048], P(None, 'ctx', 'head')
- layer_values_input: bfloat16 [2, 12288, 2048], P(None, 'ctx', 'head')
- attn_out: bfloat16 [2, 12288, 4096], P(None, 'ctx', 'head'), as said below
- grad_out: bfloat16 [2, 12288, 4096], P(None, 'ctx', 'head'), may hold values from -6 to 6
- log_norm: float32 [2, 32, 12288], P(None, 'head', 'ctx'), as said below
- window: int32 [2], replicated, may hold values from 512 to 1024, as said below
Outputs:
- grad_query: bfloat16 [2, 12288, 4096], P(None, ('ctx', 'head'))
- grad_key: bfloat16 [2, 12288, 2048], P(None, ('ctx', 'head'))
- grad_value: bfloat16 [2, 12288, 2048], P(None, ('ctx', 'head'))
The draws below stay inside these ranges and needn't reach their ends.
Inputs may be any that keep to these rules, and one draw needn't show every extreme that they name: Each layer's window is 512 to 1024 tokens; one of the layers has exactly 1024. log_norm is the log of the sum, over each query's window, of exp of its scaled scores against layer_keys_input. attn_out is the attention output that these weights give from layer_values_input.
All inputs are finite; a program needn't handle non-finite values.
Results may differ from the reference program's by a relative error of at most 0.005.
Values may be sent and summed in bfloat16 or wider, within the bound.
No kernel may reach another device: no remote copies, remote signals or barrier semaphores. Data moves between devices by JAX's collectives and lax.ppermute only.
A program may use at most 256 MiB of HBM per device.

```python
import jax
import jax.numpy as jnp
from jax import lax

QUERY_HEADS = 32
KEY_VALUE_HEADS = 16
HEAD_SIZE = 128
WINDOW_LENGTH = 1024
QUERY_PRE = 168
SLIDING_LAYERS = 2
BLOCK = 512
SPAN_TOKENS = 12288


def shared_draws(key):
    which_layer = jax.random.randint(jax.random.fold_in(key, 11), (), 0, SLIDING_LAYERS)
    other_width = jax.random.randint(jax.random.fold_in(key, 12), (SLIDING_LAYERS,), WINDOW_LENGTH // 2, WINDOW_LENGTH + 1)
    widths = jnp.where(jnp.arange(SLIDING_LAYERS) == which_layer, WINDOW_LENGTH, other_width).astype(jnp.int32)
    q_shape = (SLIDING_LAYERS, SPAN_TOKENS, QUERY_HEADS * HEAD_SIZE)
    key_value_shape = (SLIDING_LAYERS, SPAN_TOKENS, KEY_VALUE_HEADS * HEAD_SIZE)
    q_draw = jax.random.normal(jax.random.fold_in(key, 13), q_shape, jnp.float32)
    k_draw = jax.random.normal(jax.random.fold_in(key, 14), key_value_shape, jnp.float32)
    v_draw = jax.random.normal(jax.random.fold_in(key, 15), key_value_shape, jnp.float32)
    return (widths, q_draw.astype(jnp.bfloat16), k_draw.astype(jnp.bfloat16), v_draw.astype(jnp.bfloat16))


def forward_layer(layer_query_rows, layer_key_rows, layer_value_rows, win):
    query_group_count = QUERY_HEADS // KEY_VALUE_HEADS
    score_scale = QUERY_PRE ** (-0.5)
    query_head_count = layer_query_rows.astype(jnp.float32).reshape(SPAN_TOKENS, KEY_VALUE_HEADS, query_group_count, HEAD_SIZE)
    padding_rows = jnp.zeros((WINDOW_LENGTH, KEY_VALUE_HEADS, HEAD_SIZE), jnp.float32)
    padded_keys = jnp.concatenate([padding_rows, layer_key_rows.astype(jnp.float32).reshape(SPAN_TOKENS, KEY_VALUE_HEADS, HEAD_SIZE)], 0)
    padded_values = jnp.concatenate([padding_rows, layer_value_rows.astype(jnp.float32).reshape(SPAN_TOKENS, KEY_VALUE_HEADS, HEAD_SIZE)], 0)

    def one_block(block_idx):
        start_row = block_idx * BLOCK
        q_block = lax.dynamic_slice_in_dim(query_head_count, start_row, BLOCK, 0)
        k_block = lax.dynamic_slice_in_dim(padded_keys, start_row, WINDOW_LENGTH + BLOCK, 0)
        v_block = lax.dynamic_slice_in_dim(padded_values, start_row, WINDOW_LENGTH + BLOCK, 0)
        scores = jnp.einsum('rkgd,ckd->kgrc', q_block, k_block) * score_scale
        q_pos = start_row + jnp.arange(BLOCK, dtype=jnp.int32)
        k_pos = start_row - WINDOW_LENGTH + jnp.arange(WINDOW_LENGTH + BLOCK, dtype=jnp.int32)
        visible = (k_pos[None, :] <= q_pos[:, None]) & (q_pos[:, None] - k_pos[None, :] < win) & (k_pos[None, :] >= 0)
        masked = jnp.where(visible, scores, -1e+30)
        top_score = jnp.max(masked, axis=-1, keepdims=True)
        weights = jnp.where(visible, jnp.exp(masked - top_score), 0.0)
        totals = jnp.sum(weights, axis=-1)
        lse_block = top_score[..., 0] + jnp.log(totals)
        out_block = jnp.einsum('kgrc,ckd->rkgd', weights, v_block) / jnp.transpose(totals, (2, 0, 1))[..., None]
        return (out_block.reshape(BLOCK, QUERY_HEADS * HEAD_SIZE), lse_block.reshape(QUERY_HEADS, BLOCK))
    out_blocks, lse_blocks = lax.map(one_block, jnp.arange(SPAN_TOKENS // BLOCK, dtype=jnp.int32))
    return (out_blocks.reshape(SPAN_TOKENS, QUERY_HEADS * HEAD_SIZE), jnp.transpose(lse_blocks, (1, 0, 2)).reshape(QUERY_HEADS, SPAN_TOKENS))


def forward_all(key):
    widths, q_all, k_all, v_all = shared_draws(key)
    out_list = []
    lse_list = []
    for layer_number in range(SLIDING_LAYERS):
        out_layer, lse_layer = forward_layer(q_all[layer_number], k_all[layer_number], v_all[layer_number], widths[layer_number])
        out_list.append(out_layer)
        lse_list.append(lse_layer)
    return (jnp.stack(out_list, 0), jnp.stack(lse_list, 0))


def draw_window(key, part):
    return shared_draws(key)[0]


def draw_queries(key, part):
    return shared_draws(key)[1]


def draw_layer_keys_input(key, part):
    return shared_draws(key)[2]


def draw_layer_values_input(key, part):
    return shared_draws(key)[3]


def draw_attn_out(key, part):
    return forward_all(key)[0].astype(jnp.bfloat16)


def draw_log_norm(key, part):
    return forward_all(key)[1].astype(jnp.float32)


def block_scale(key, shape, shards, low, high):
    level = 1.0
    for dim, blocks in shards:
        heights = jax.random.uniform(jax.random.fold_in(jax.random.fold_in(key, 6), dim), (blocks,), jnp.float32, low / len(shards), high / len(shards))
        level = level * jnp.repeat(jnp.exp(heights), shape[dim] // blocks).reshape((-1,) + (1,) * (len(shape) - 1 - dim))
    return level


def scatter_about(key, shape, width, most, split=(), kind=jnp.bfloat16):
    values = jax.random.normal(key, shape, jnp.float32) * width
    if len(split) > 0:
        values = block_scale(key, shape, split, -0.22, 0.18) * values
    return jnp.clip(values, min=-most, max=most).astype(kind)


def setup_inputs(seed: int = 0) -> dict:
    key_list = jax.random.split(jax.random.key(seed), 8)
    return {
        "queries": draw_queries(jax.random.fold_in(key_list[7], 71), 0),
        "layer_keys_input": draw_layer_keys_input(jax.random.fold_in(key_list[7], 71), 0),
        "layer_values_input": draw_layer_values_input(jax.random.fold_in(key_list[7], 71), 0),
        "attn_out": draw_attn_out(jax.random.fold_in(key_list[7], 71), 0),
        "grad_out": scatter_about(key_list[4], (SLIDING_LAYERS, SPAN_TOKENS, QUERY_HEADS * HEAD_SIZE), 1.0, 6.0, ((1, 8), (2, 4))),
        "log_norm": draw_log_norm(jax.random.fold_in(key_list[7], 71), 0),
        "window": draw_window(jax.random.fold_in(key_list[7], 71), 0),
    }


def block_grads(q_block, do_block, lse_block, dlt_block, k_block, v_block, q_pos, k_pos, win):
    row_count, head_count, head_dim = q_block.shape
    kv_count = k_block.shape[1]
    query_group_count = head_count // kv_count
    score_scale = QUERY_PRE ** -0.5
    query_head_count = q_block.reshape(row_count, kv_count, query_group_count, head_dim).astype(jnp.float32)
    do_heads = do_block.reshape(row_count, kv_count, query_group_count, head_dim).astype(jnp.float32)
    k_float = k_block.astype(jnp.float32)
    v_float = v_block.astype(jnp.float32)
    scores = jnp.einsum("rkgd,ckd->kgrc", query_head_count, k_float) * score_scale
    lse_heads = lse_block.reshape(kv_count, query_group_count, row_count)
    dlt_heads = dlt_block.reshape(kv_count, query_group_count, row_count)
    visible = (k_pos[None, :] <= q_pos[:, None]) & (q_pos[:, None] - k_pos[None, :] < win) & (k_pos[None, :] >= 0)
    attn_prob = jnp.where(visible, jnp.exp(scores - lse_heads[..., None]), 0.0)
    prob_low = lax.optimization_barrier(attn_prob.astype(jnp.bfloat16)).astype(jnp.float32)
    grad_prob = jnp.einsum("rkgd,ckd->kgrc", do_heads, v_float)
    grad_score = attn_prob * (grad_prob - dlt_heads[..., None])
    score_low = lax.optimization_barrier(grad_score.astype(jnp.bfloat16)).astype(jnp.float32)
    dv_part = jnp.einsum("kgrc,rkgd->ckd", prob_low, do_heads)
    dk_part = jnp.einsum("kgrc,rkgd->ckd", score_low, query_head_count) * score_scale
    dq_part = jnp.einsum("kgrc,ckd->rkgd", score_low, k_float) * score_scale
    return dq_part.reshape(row_count, head_count, head_dim), dk_part, dv_part


def reference(queries, layer_keys_input, layer_values_input, attn_out, grad_out, log_norm, window):
    dq_list = []
    key_gradient_parts = []
    value_gradient_parts = []
    for layer_number in range(SLIDING_LAYERS):
        q_all = queries[layer_number].reshape(SPAN_TOKENS, QUERY_HEADS, HEAD_SIZE)
        do_all = grad_out[layer_number].reshape(SPAN_TOKENS, QUERY_HEADS, HEAD_SIZE)
        delta = jnp.sum(do_all.astype(jnp.float32) * attn_out[layer_number].reshape(SPAN_TOKENS, QUERY_HEADS, HEAD_SIZE).astype(jnp.float32), axis=-1).T
        padding_rows = jnp.zeros((WINDOW_LENGTH, KEY_VALUE_HEADS, HEAD_SIZE), layer_keys_input.dtype)
        padded_keys = jnp.concatenate([padding_rows, layer_keys_input[layer_number].reshape(SPAN_TOKENS, KEY_VALUE_HEADS, HEAD_SIZE)], 0)
        padded_values = jnp.concatenate([padding_rows, layer_values_input[layer_number].reshape(SPAN_TOKENS, KEY_VALUE_HEADS, HEAD_SIZE)], 0)
        win = window[layer_number]
        lse_all = log_norm[layer_number]

        def sweep(block_idx, carry, q_all=q_all, do_all=do_all, delta=delta, padded_keys=padded_keys, padded_values=padded_values, win=win, lse_all=lse_all):
            dq_all, key_gradient_total, value_gradient_total = carry
            start_row = (block_idx * BLOCK).astype(jnp.int32)
            q_block = lax.dynamic_slice_in_dim(q_all, start_row, BLOCK, 0)
            do_block = lax.dynamic_slice_in_dim(do_all, start_row, BLOCK, 0)
            lse_block = lax.dynamic_slice_in_dim(lse_all, start_row, BLOCK, 1)
            dlt_block = lax.dynamic_slice_in_dim(delta, start_row, BLOCK, 1)
            k_block = lax.dynamic_slice_in_dim(padded_keys, start_row, WINDOW_LENGTH + BLOCK, 0)
            v_block = lax.dynamic_slice_in_dim(padded_values, start_row, WINDOW_LENGTH + BLOCK, 0)
            q_pos = start_row + jnp.arange(BLOCK, dtype=jnp.int32)
            k_pos = start_row - WINDOW_LENGTH + jnp.arange(WINDOW_LENGTH + BLOCK, dtype=jnp.int32)
            dq_part, dk_part, dv_part = block_grads(q_block, do_block, lse_block, dlt_block, k_block, v_block, q_pos, k_pos, win)
            dq_all = lax.dynamic_update_slice_in_dim(dq_all, dq_part.astype(jnp.bfloat16), start_row, 0)
            dk_old = lax.dynamic_slice_in_dim(key_gradient_total, start_row, WINDOW_LENGTH + BLOCK, 0)
            dv_old = lax.dynamic_slice_in_dim(value_gradient_total, start_row, WINDOW_LENGTH + BLOCK, 0)
            key_gradient_total = lax.dynamic_update_slice_in_dim(key_gradient_total, dk_old + dk_part, start_row, 0)
            value_gradient_total = lax.dynamic_update_slice_in_dim(value_gradient_total, dv_old + dv_part, start_row, 0)
            return dq_all, key_gradient_total, value_gradient_total

        initial_state = (jnp.zeros((SPAN_TOKENS, QUERY_HEADS, HEAD_SIZE), jnp.bfloat16), jnp.zeros((WINDOW_LENGTH + SPAN_TOKENS, KEY_VALUE_HEADS, HEAD_SIZE), jnp.float32), jnp.zeros((WINDOW_LENGTH + SPAN_TOKENS, KEY_VALUE_HEADS, HEAD_SIZE), jnp.float32))
        dq_all, key_gradient_total, value_gradient_total = lax.fori_loop(0, SPAN_TOKENS // BLOCK, sweep, initial_state)
        dq_list.append(dq_all.reshape(SPAN_TOKENS, QUERY_HEADS * HEAD_SIZE))
        key_gradient_parts.append(key_gradient_total[WINDOW_LENGTH:].astype(jnp.bfloat16).reshape(SPAN_TOKENS, KEY_VALUE_HEADS * HEAD_SIZE))
        value_gradient_parts.append(value_gradient_total[WINDOW_LENGTH:].astype(jnp.bfloat16).reshape(SPAN_TOKENS, KEY_VALUE_HEADS * HEAD_SIZE))
    return jnp.stack(dq_list, 0), jnp.stack(key_gradient_parts, 0), jnp.stack(value_gradient_parts, 0)
```

```python
import functools
import math

import jax
import jax.numpy as jnp
from jax import lax
from jax.experimental import pallas as pl
from jax.experimental.pallas import tpu as pltpu
from jax.sharding import PartitionSpec as P

HEAD_SIZE = 128
WINDOW_LENGTH = 1024
QUERY_PRE = 168
SLIDING_LAYERS = 2
TILE = 256
SCALE = QUERY_PRE ** (-0.5)
LOG2E = math.log2(math.e)
FAR = 1 << 20

NT = (((1,), (1,)), ((), ()))
NN = (((1,), (0,)), ((), ()))


def dot(a, b, dims=NN):
    return lax.dot_general(a, b, dims, preferred_element_type=jnp.float32)


def shifted(value, axis, steps):
    count = lax.axis_size(axis)
    first, last = (max(0, -steps), min(count, count - steps))
    return lax.ppermute(value, axis, [(source, source + steps) for source in range(first, last)])


def swapped(value, axis, flip):
    count = lax.axis_size(axis)
    return lax.ppermute(value, axis, [(source, source ^ flip) for source in range(count)])


def band_kernel(
    layer, kv_first, kv_count, owners, scal, q_ref, do_ref, out_ref, lse_ref, k_ref, v_ref, halo_ref, *rest
):
    dq_bufs = rest[:owners]
    back_ref, part_ref, kx, vx, kt, acc, dq_scr, sems = rest[owners:]
    tok_local = q_ref.shape[1]
    group = q_ref.shape[2] // HEAD_SIZE
    chunk = tok_local // owners
    step = pl.program_id(0)
    me = scal[0]
    first_shard = scal[1]
    win = scal[2 + layer]
    wide = group * TILE

    kx[0:WINDOW_LENGTH] = halo_ref[:, 0:HEAD_SIZE]
    vx[0:WINDOW_LENGTH] = halo_ref[:, HEAD_SIZE : 2 * HEAD_SIZE]
    kx[WINDOW_LENGTH:] = k_ref[0]
    vx[WINDOW_LENGTH:] = v_ref[0]
    kt[...] = kx[...].T
    acc[...] = jnp.zeros_like(acc)

    rows = lax.broadcasted_iota(jnp.int32, (TILE, wide), 0)
    lanes = lax.broadcasted_iota(jnp.int32, (1, wide), 1) % TILE

    def stacked(ref, start):
        block = ref[0, pl.ds(start, TILE), :]
        return jnp.concatenate(
            [block[:, h * HEAD_SIZE : (h + 1) * HEAD_SIZE] for h in range(group)], 0
        )

    def one_block(block, carry):
        start = pl.multiple_of(block * TILE, TILE)
        q2 = stacked(q_ref, start)
        do2 = stacked(do_ref, start)
        prod = do2.astype(jnp.float32) * stacked(out_ref, start).astype(jnp.float32)
        high = prod.astype(jnp.bfloat16)
        low = (prod - high.astype(jnp.float32)).astype(jnp.bfloat16)
        ones = jnp.ones((8, HEAD_SIZE), jnp.bfloat16)
        delta = (dot(ones, high, NT) + dot(ones, low, NT))[0:1]
        head = (kv_first + step) * group
        lse = jnp.concatenate(
            [lse_ref[0, pl.ds(head + h, 1), pl.ds(start, TILE)] for h in range(group)], 1
        )
        lse2 = lse * LOG2E
        dq_t = jnp.zeros((HEAD_SIZE, wide), jnp.float32)
        tiles = WINDOW_LENGTH // TILE + 1
        for tile in range(tiles):
            begin = pl.multiple_of(start + tile * TILE, TILE)
            span = pl.ds(begin, TILE)
            scores = dot(kx[span, :], q2, NT)
            prob = jnp.exp2(scores * (SCALE * LOG2E) - lse2)
            if tile == tiles - 1:
                seen = rows <= lanes
            else:
                bound = WINDOW_LENGTH - win - tile * TILE
                outside = jnp.logical_and(first_shard == 1, begin < WINDOW_LENGTH)
                seen = rows > lanes + jnp.where(outside, FAR, bound)
            prob = jnp.where(seen, prob, 0.0)
            grad_prob = dot(vx[span, :], do2, NT)
            grad_score = prob * (grad_prob - delta)
            prob_low = prob.astype(jnp.bfloat16)
            score_low = grad_score.astype(jnp.bfloat16)
            acc[span, HEAD_SIZE:] += dot(prob_low, do2)
            acc[span, :HEAD_SIZE] += dot(score_low, q2)
            dq_t += dot(kt[:, span], score_low)
        dq = (dq_t.T * SCALE).astype(jnp.bfloat16)
        for h in range(group):
            dq_scr[step, pl.ds(start, TILE), h * HEAD_SIZE : (h + 1) * HEAD_SIZE] = dq[
                h * TILE : (h + 1) * TILE
            ]
        return carry

    lax.fori_loop(0, tok_local // TILE, one_block, 0)

    back_ref[:, :HEAD_SIZE] = (acc[0:WINDOW_LENGTH, :HEAD_SIZE] * SCALE).astype(jnp.bfloat16)
    back_ref[:, HEAD_SIZE:] = acc[0:WINDOW_LENGTH, HEAD_SIZE:].astype(jnp.bfloat16)
    part_ref[:, :HEAD_SIZE] = acc[WINDOW_LENGTH:, :HEAD_SIZE] * SCALE
    part_ref[:, HEAD_SIZE:] = acc[WINDOW_LENGTH:, HEAD_SIZE:]

    def copies(index):
        result = []
        for flip in range(owners):
            owner = jnp.bitwise_xor(me, flip)
            source = dq_scr.at[index, pl.ds(pl.multiple_of(owner * chunk, chunk), chunk), :]
            target = dq_bufs[flip].at[:, pl.ds(index * group * HEAD_SIZE, group * HEAD_SIZE)]
            result.append(pltpu.make_async_copy(source, target, sems.at[index, flip]))
        return result

    for index in range(kv_count):

        @pl.when(step == index)
        def _(index=index):
            for copy in copies(index):
                copy.start()

    @pl.when(step == kv_count - 1)
    def _():
        for index in range(kv_count):
            for copy in copies(index):
                copy.wait()


def band_call(piece, extra, owners, scal, queries, grad_out, attn_out, log_norm, keys, values, halo):
    layer, kv_first, kv_count = piece
    tok_local = queries.shape[1]
    group = queries.shape[2] // keys.shape[2]
    span = WINDOW_LENGTH + tok_local
    chunk = tok_local // owners
    q_spec = pl.BlockSpec((1, tok_local, group * HEAD_SIZE), lambda g: (layer, 0, kv_first + g))
    kv_spec = pl.BlockSpec((1, tok_local, HEAD_SIZE), lambda g: (layer, 0, kv_first + g))
    pairs = tok_local * (WINDOW_LENGTH + TILE) * group * kv_count
    outs = pl.pallas_call(
        functools.partial(band_kernel, layer, kv_first, kv_count, owners),
        grid=(kv_count,),
        in_specs=[
            pl.BlockSpec(memory_space=pltpu.SMEM),
            q_spec,
            q_spec,
            q_spec,
            pl.BlockSpec((1,) + log_norm.shape[1:], lambda g: (layer, 0, 0)),
            kv_spec,
            kv_spec,
            pl.BlockSpec((WINDOW_LENGTH, 2 * HEAD_SIZE), lambda g: (0, g)),
        ],
        out_specs=[pl.BlockSpec(memory_space=pl.ANY)] * owners
        + [
            pl.BlockSpec((WINDOW_LENGTH, 2 * HEAD_SIZE), lambda g: (0, g)),
            pl.BlockSpec((tok_local, 2 * HEAD_SIZE), lambda g: (0, g)),
        ],
        out_shape=[
            jax.ShapeDtypeStruct((chunk, (kv_count * group + extra) * HEAD_SIZE), jnp.bfloat16)
        ]
        * owners
        + [
            jax.ShapeDtypeStruct((WINDOW_LENGTH, kv_count * 2 * HEAD_SIZE), jnp.bfloat16),
            jax.ShapeDtypeStruct((tok_local, kv_count * 2 * HEAD_SIZE), jnp.float32),
        ],
        scratch_shapes=[
            pltpu.VMEM((span, HEAD_SIZE), jnp.bfloat16),
            pltpu.VMEM((span, HEAD_SIZE), jnp.bfloat16),
            pltpu.VMEM((HEAD_SIZE, span), jnp.bfloat16),
            pltpu.VMEM((span, 2 * HEAD_SIZE), jnp.float32),
            pltpu.VMEM((kv_count, tok_local, group * HEAD_SIZE), jnp.bfloat16),
            pltpu.SemaphoreType.DMA((kv_count, owners)),
        ],
        compiler_params=pltpu.CompilerParams(vmem_limit_bytes=40 * 1024 * 1024),
        cost_estimate=pl.CostEstimate(
            flops=pairs * 2 * HEAD_SIZE * 5 * 2,
            bytes_accessed=8 * tok_local * group * kv_count * HEAD_SIZE,
            transcendentals=pairs,
        ),
        name="band",
    )(scal, queries, grad_out, attn_out, log_norm, keys, values, halo)
    return outs[:owners], outs[owners], outs[owners + 1]


def finish_kernel(kv_count, owners, column, aliased, scal, part_ref, back_ref, *rest):
    bufs = rest[owners if aliased else 0 :][:owners]
    scr, sems = rest[-2:]
    tok_local = part_ref.shape[0]
    chunk = tok_local // owners
    step = pl.program_id(0)
    me = scal[0]
    plain = tok_local - WINDOW_LENGTH
    scr[step, :plain] = part_ref[:plain].astype(jnp.bfloat16)
    scr[step, plain:] = (part_ref[plain:] + back_ref[...].astype(jnp.float32)).astype(jnp.bfloat16)

    def copies(index):
        result = []
        for flip in range(owners):
            owner = jnp.bitwise_xor(me, flip)
            rows = pl.ds(pl.multiple_of(owner * chunk, chunk), chunk)
            for kind in range(2):
                place = column + (kind * kv_count + index) * HEAD_SIZE
                result.append(
                    pltpu.make_async_copy(
                        scr.at[index, rows, pl.ds(kind * HEAD_SIZE, HEAD_SIZE)],
                        bufs[flip].at[:, pl.ds(place, HEAD_SIZE)],
                        sems.at[index, flip, kind],
                    )
                )
        return result

    for index in range(kv_count):

        @pl.when(step == index)
        def _(index=index):
            for copy in copies(index):
                copy.start()

    @pl.when(step == kv_count - 1)
    def _():
        for index in range(kv_count):
            for copy in copies(index):
                copy.wait()


def finish_call(kv_count, owners, column, scal, part, back, bufs):
    tok_local = part.shape[0]
    chunk = tok_local // owners
    aliased = bufs is not None
    shape = jax.ShapeDtypeStruct((chunk, column + kv_count * 2 * HEAD_SIZE), jnp.bfloat16)
    any_spec = pl.BlockSpec(memory_space=pl.ANY)
    return pl.pallas_call(
        functools.partial(finish_kernel, kv_count, owners, column, aliased),
        grid=(kv_count,),
        in_specs=[
            pl.BlockSpec(memory_space=pltpu.SMEM),
            pl.BlockSpec((tok_local, 2 * HEAD_SIZE), lambda g: (0, g)),
            pl.BlockSpec((WINDOW_LENGTH, 2 * HEAD_SIZE), lambda g: (0, g)),
        ]
        + ([any_spec] * owners if aliased else []),
        out_specs=[any_spec] * owners,
        out_shape=[shape] * owners,
        input_output_aliases={3 + i: i for i in range(owners)} if aliased else {},
        scratch_shapes=[
            pltpu.VMEM((kv_count, tok_local, 2 * HEAD_SIZE), jnp.bfloat16),
            pltpu.SemaphoreType.DMA((kv_count, owners, 2)),
        ],
        compiler_params=pltpu.CompilerParams(vmem_limit_bytes=32 * 1024 * 1024),
        cost_estimate=pl.CostEstimate(
            flops=0, bytes_accessed=16 * tok_local * kv_count * HEAD_SIZE, transcendentals=0
        ),
        name="finish",
    )(scal, part, back, *(bufs if aliased else ()))


def place_kernel(plan, owners, group, kv_local, aliased, scal, *rest):
    blocks = rest[:owners]
    outs = rest[owners + (3 if aliased else 0) :][:3]
    sems = rest[-1]
    me = scal[0]
    copies = []
    for flip in range(owners):
        source = jnp.bitwise_xor(me, flip)
        column = 0
        for which, (layer, kv_first, kv_count) in plan:
            heads = kv_count * group if which == 0 else kv_count
            home = kv_local * group if which == 0 else kv_local
            first = kv_first * group if which == 0 else kv_first
            place = pl.multiple_of((source * home + first) * HEAD_SIZE, HEAD_SIZE)
            copies.append(
                pltpu.make_async_copy(
                    blocks[flip].at[:, pl.ds(column, heads * HEAD_SIZE)],
                    outs[which].at[layer, :, pl.ds(place, heads * HEAD_SIZE)],
                    sems.at[len(copies)],
                )
            )
            column += heads * HEAD_SIZE
    for copy in copies:
        copy.start()
    for copy in copies:
        copy.wait()


def place_call(plan, owners, group, kv_local, scal, blocks, outs):
    chunk, width = blocks[0].shape
    aliased = outs is not None
    any_spec = pl.BlockSpec(memory_space=pl.ANY)
    shapes = [
        jax.ShapeDtypeStruct(
            (SLIDING_LAYERS, chunk, owners * heads * HEAD_SIZE), jnp.bfloat16
        )
        for heads in (kv_local * group, kv_local, kv_local)
    ]
    return pl.pallas_call(
        functools.partial(place_kernel, plan, owners, group, kv_local, aliased),
        in_specs=[pl.BlockSpec(memory_space=pltpu.SMEM)]
        + [any_spec] * (owners + (3 if aliased else 0)),
        out_specs=[any_spec] * 3,
        out_shape=shapes,
        input_output_aliases={1 + owners + i: i for i in range(3)} if aliased else {},
        scratch_shapes=[pltpu.SemaphoreType.DMA((owners * len(plan),))],
        cost_estimate=pl.CostEstimate(
            flops=0, bytes_accessed=owners * chunk * width * 4, transcendentals=0
        ),
        name="place",
    )(scal, *blocks, *(outs if aliased else ()))


def shards(queries, layer_keys_input, layer_values_input, attn_out, grad_out, log_norm, window):
    tok_local = queries.shape[1]
    kv_local = layer_keys_input.shape[2] // HEAD_SIZE
    group = queries.shape[2] // layer_keys_input.shape[2]
    owners = lax.axis_size("head")
    shard = lax.axis_index("ctx")
    scal = jnp.concatenate(
        [
            jnp.stack([lax.axis_index("head"), (shard == 0).astype(jnp.int32)]).astype(jnp.int32),
            window.astype(jnp.int32),
        ]
    )
    each = min(2, kv_local)
    pieces = [
        (layer, kv_first, each)
        for layer in range(SLIDING_LAYERS)
        for kv_first in range(0, kv_local, each)
    ]

    halos = []
    for layer, kv_first, kv_count in pieces:
        parts = []
        for kv in range(kv_first, kv_first + kv_count):
            columns = slice(kv * HEAD_SIZE, (kv + 1) * HEAD_SIZE)
            parts.append(layer_keys_input[layer, tok_local - WINDOW_LENGTH :, columns])
            parts.append(layer_values_input[layer, tok_local - WINDOW_LENGTH :, columns])
        halos.append(shifted(jnp.concatenate(parts, 1), "ctx", 1))

    outs = None
    waiting = None

    def send(plan, bufs, outs):
        blocks = [bufs[0]] + [swapped(bufs[flip], "head", flip) for flip in range(1, owners)]
        return place_call(plan, owners, group, kv_local, scal, blocks, outs)

    for piece, halo in zip(pieces, halos):
        kv_count = piece[2]
        extra = 0 if waiting is None else 2 * waiting[0][2]
        bufs, back, part = band_call(
            piece,
            extra,
            owners,
            scal,
            queries,
            grad_out,
            attn_out,
            log_norm,
            layer_keys_input,
            layer_values_input,
            halo,
        )
        back = shifted(back, "ctx", -1)
        plan = [(0, piece)]
        if waiting is not None:
            old, old_part, old_back = waiting
            bufs = finish_call(
                old[2], owners, kv_count * group * HEAD_SIZE, scal, old_part, old_back, bufs
            )
            plan += [(1, old), (2, old)]
        outs = send(plan, bufs, outs)
        waiting = (piece, part, back)
    old, old_part, old_back = waiting
    bufs = finish_call(old[2], owners, 0, scal, old_part, old_back, None)
    outs = send([(1, old), (2, old)], bufs, outs)
    return tuple(outs)


def solution(mesh):
    in_specs = (
        P(None, "ctx", "head"),
        P(None, "ctx", "head"),
        P(None, "ctx", "head"),
        P(None, "ctx", "head"),
        P(None, "ctx", "head"),
        P(None, "head", "ctx"),
        P(),
    )
    out_specs = (
        P(None, ("ctx", "head"), None),
        P(None, ("ctx", "head"), None),
        P(None, ("ctx", "head"), None),
    )
    return jax.shard_map(shards, mesh=mesh, in_specs=in_specs, out_specs=out_specs, check_vma=False)
```

```python
import functools
import math

import jax
import jax.numpy as jnp
from jax import lax
from jax.experimental import pallas as pl
from jax.experimental.pallas import tpu as pltpu
from jax.sharding import PartitionSpec as P

HEAD_SIZE = 128
WINDOW_LENGTH = 1024
QUERY_PRE = 168
SLIDING_LAYERS = 2
TILE = 256
SCALE = QUERY_PRE ** (-0.5)
LOG2E = math.log2(math.e)
FAR = 1 << 20

NT = (((1,), (1,)), ((), ()))
NN = (((1,), (0,)), ((), ()))


def dot(a, b, dims=NN):
    return lax.dot_general(a, b, dims, preferred_element_type=jnp.float32)


def shifted(value, axis, steps):
    count = lax.axis_size(axis)
    first, last = (max(0, -steps), min(count, count - steps))
    return lax.ppermute(value, axis, [(source, source + steps) for source in range(first, last)])


def swapped(value, axis, flip):
    count = lax.axis_size(axis)
    return lax.ppermute(value, axis, [(source, source ^ flip) for source in range(count)])


def band_kernel(
    layer, kv_first, kv_count, owners, scal, q_ref, do_ref, out_ref, lse_ref, k_ref, v_ref, halo_ref, after, *rest
):
    dq_bufs = rest[:owners]
    back_ref, part_ref, kx, vx, kt, acc, lse2_scr, delta_scr, dq_scr, sems = rest[owners:]
    tok_local = q_ref.shape[1]
    group = q_ref.shape[2] // HEAD_SIZE
    chunk = tok_local // owners
    step = pl.program_id(0)
    me = scal[0]
    first_shard = scal[1]
    win = scal[2 + layer]
    wide = group * TILE

    kx[0:WINDOW_LENGTH] = halo_ref[:, 0:HEAD_SIZE]
    vx[0:WINDOW_LENGTH] = halo_ref[:, HEAD_SIZE : 2 * HEAD_SIZE]
    kx[WINDOW_LENGTH:] = k_ref[0]
    vx[WINDOW_LENGTH:] = v_ref[0]
    kt[...] = kx[...].T
    acc[...] = jnp.zeros_like(acc)

    rows = lax.broadcasted_iota(jnp.int32, (TILE, wide), 0)
    lanes = lax.broadcasted_iota(jnp.int32, (1, wide), 1) % TILE

    def stacked(ref, start):
        block = ref[0, pl.ds(start, TILE), :]
        return jnp.concatenate(
            [block[:, h * HEAD_SIZE : (h + 1) * HEAD_SIZE] for h in range(group)], 0
        )

    ones = jnp.ones((8, HEAD_SIZE), jnp.bfloat16)
    head = (kv_first + step) * group
    for block in range(tok_local // TILE):
        start = block * TILE
        columns = slice(block * wide, (block + 1) * wide)
        prod = stacked(do_ref, start).astype(jnp.float32) * stacked(out_ref, start).astype(jnp.float32)
        high = prod.astype(jnp.bfloat16)
        low = (prod - high.astype(jnp.float32)).astype(jnp.bfloat16)
        delta_scr[:, columns] = dot(ones, high, NT) + dot(ones, low, NT)
        for h in range(group):
            lse2_scr[0:1, block * wide + h * TILE : block * wide + (h + 1) * TILE] = (
                lse_ref[0, pl.ds(head + h, 1), start : start + TILE] * LOG2E
            )

    def one_block(block, carry):
        start = pl.multiple_of(block * TILE, TILE)
        columns = pl.ds(pl.multiple_of(block * wide, wide), wide)
        q2 = stacked(q_ref, start)
        do2 = stacked(do_ref, start)
        delta = delta_scr[0:1, columns]
        lse2 = lse2_scr[0:1, columns]
        tiles = WINDOW_LENGTH // TILE + 1
        span = pl.ds(start, tiles * TILE)
        scores = dot(kx[span, :], q2, NT)
        grad_prob = dot(vx[span, :], do2, NT)
        prob_low = []
        score_low = []
        for tile in range(tiles):
            part = slice(tile * TILE, (tile + 1) * TILE)
            prob = jnp.exp2(scores[part] * (SCALE * LOG2E) - lse2)
            if tile == tiles - 1:
                seen = rows <= lanes
            else:
                bound = WINDOW_LENGTH - win - tile * TILE
                outside = jnp.logical_and(first_shard == 1, start + tile * TILE < WINDOW_LENGTH)
                seen = rows > lanes + jnp.where(outside, FAR, bound)
            prob = jnp.where(seen, prob, 0.0)
            prob_low.append(prob.astype(jnp.bfloat16))
            score_low.append((prob * (grad_prob[part] - delta)).astype(jnp.bfloat16))
        prob_low = jnp.concatenate(prob_low, 0)
        score_low = jnp.concatenate(score_low, 0)
        acc[span, HEAD_SIZE:] += dot(prob_low, do2)
        acc[span, :HEAD_SIZE] += dot(score_low, q2)
        dq_t = dot(kt[:, span], score_low)
        dq = (dq_t.T * SCALE).astype(jnp.bfloat16)
        for h in range(group):
            dq_scr[step, pl.ds(start, TILE), h * HEAD_SIZE : (h + 1) * HEAD_SIZE] = dq[
                h * TILE : (h + 1) * TILE
            ]
        return carry

    lax.fori_loop(0, tok_local // TILE, one_block, 0)

    back_ref[:, :HEAD_SIZE] = (acc[0:WINDOW_LENGTH, :HEAD_SIZE] * SCALE).astype(jnp.bfloat16)
    back_ref[:, HEAD_SIZE:] = acc[0:WINDOW_LENGTH, HEAD_SIZE:].astype(jnp.bfloat16)
    part_ref[:, :HEAD_SIZE] = acc[WINDOW_LENGTH:, :HEAD_SIZE] * SCALE
    part_ref[:, HEAD_SIZE:] = acc[WINDOW_LENGTH:, HEAD_SIZE:]

    def copies(index):
        result = []
        for flip in range(owners):
            owner = jnp.bitwise_xor(me, flip)
            source = dq_scr.at[index, pl.ds(pl.multiple_of(owner * chunk, chunk), chunk), :]
            target = dq_bufs[flip].at[:, pl.ds(index * group * HEAD_SIZE, group * HEAD_SIZE)]
            result.append(pltpu.make_async_copy(source, target, sems.at[index, flip]))
        return result

    for index in range(kv_count):

        @pl.when(step == index)
        def _(index=index):
            for copy in copies(index):
                copy.start()

    @pl.when(step == kv_count - 1)
    def _():
        for index in range(kv_count):
            for copy in copies(index):
                copy.wait()


def band_call(piece, extra, owners, scal, queries, grad_out, attn_out, log_norm, keys, values, halo, column, after):
    layer, kv_first, kv_count = piece
    tok_local = queries.shape[1]
    group = queries.shape[2] // keys.shape[2]
    span = WINDOW_LENGTH + tok_local
    chunk = tok_local // owners
    q_spec = pl.BlockSpec((1, tok_local, group * HEAD_SIZE), lambda g: (layer, 0, kv_first + g))
    kv_spec = pl.BlockSpec((1, tok_local, HEAD_SIZE), lambda g: (layer, 0, kv_first + g))
    pairs = tok_local * (WINDOW_LENGTH + TILE) * group * kv_count
    outs = pl.pallas_call(
        functools.partial(band_kernel, layer, kv_first, kv_count, owners),
        grid=(kv_count,),
        in_specs=[
            pl.BlockSpec(memory_space=pltpu.SMEM),
            q_spec,
            q_spec,
            q_spec,
            pl.BlockSpec((1,) + log_norm.shape[1:], lambda g: (layer, 0, 0)),
            kv_spec,
            kv_spec,
            pl.BlockSpec((WINDOW_LENGTH, 2 * HEAD_SIZE), lambda g: (0, column + g)),
            pl.BlockSpec(memory_space=pl.ANY),
        ],
        out_specs=[pl.BlockSpec(memory_space=pl.ANY)] * owners
        + [
            pl.BlockSpec((WINDOW_LENGTH, 2 * HEAD_SIZE), lambda g: (0, g)),
            pl.BlockSpec((tok_local, 2 * HEAD_SIZE), lambda g: (0, g)),
        ],
        out_shape=[
            jax.ShapeDtypeStruct((chunk, (kv_count * group + extra) * HEAD_SIZE), jnp.bfloat16)
        ]
        * owners
        + [
            jax.ShapeDtypeStruct((WINDOW_LENGTH, kv_count * 2 * HEAD_SIZE), jnp.bfloat16),
            jax.ShapeDtypeStruct((tok_local, kv_count * 2 * HEAD_SIZE), jnp.float32),
        ],
        scratch_shapes=[
            pltpu.VMEM((span, HEAD_SIZE), jnp.bfloat16),
            pltpu.VMEM((span, HEAD_SIZE), jnp.bfloat16),
            pltpu.VMEM((HEAD_SIZE, span), jnp.bfloat16),
            pltpu.VMEM((span, 2 * HEAD_SIZE), jnp.float32),
            pltpu.VMEM((8, tok_local * group), jnp.float32),
            pltpu.VMEM((8, tok_local * group), jnp.float32),
            pltpu.VMEM((kv_count, tok_local, group * HEAD_SIZE), jnp.bfloat16),
            pltpu.SemaphoreType.DMA((kv_count, owners)),
        ],
        compiler_params=pltpu.CompilerParams(vmem_limit_bytes=40 * 1024 * 1024),
        cost_estimate=pl.CostEstimate(
            flops=pairs * 2 * HEAD_SIZE * 5 * 2,
            bytes_accessed=8 * tok_local * group * kv_count * HEAD_SIZE,
            transcendentals=pairs,
        ),
        name="band",
    )(scal, queries, grad_out, attn_out, log_norm, keys, values, halo, after)
    return outs[:owners], outs[owners], outs[owners + 1]


def finish_kernel(kv_count, owners, column, aliased, scal, part_ref, back_ref, *rest):
    bufs = rest[owners if aliased else 0 :][:owners]
    scr, sems = rest[-2:]
    tok_local = part_ref.shape[0]
    chunk = tok_local // owners
    step = pl.program_id(0)
    me = scal[0]
    plain = tok_local - WINDOW_LENGTH
    scr[step, :plain] = part_ref[:plain].astype(jnp.bfloat16)
    scr[step, plain:] = (part_ref[plain:] + back_ref[...].astype(jnp.float32)).astype(jnp.bfloat16)

    def copies(index):
        result = []
        for flip in range(owners):
            owner = jnp.bitwise_xor(me, flip)
            rows = pl.ds(pl.multiple_of(owner * chunk, chunk), chunk)
            for kind in range(2):
                place = column + (kind * kv_count + index) * HEAD_SIZE
                result.append(
                    pltpu.make_async_copy(
                        scr.at[index, rows, pl.ds(kind * HEAD_SIZE, HEAD_SIZE)],
                        bufs[flip].at[:, pl.ds(place, HEAD_SIZE)],
                        sems.at[index, flip, kind],
                    )
                )
        return result

    for index in range(kv_count):

        @pl.when(step == index)
        def _(index=index):
            for copy in copies(index):
                copy.start()

    @pl.when(step == kv_count - 1)
    def _():
        for index in range(kv_count):
            for copy in copies(index):
                copy.wait()


def finish_call(kv_count, owners, column, scal, part, back, bufs):
    tok_local = part.shape[0]
    chunk = tok_local // owners
    aliased = bufs is not None
    shape = jax.ShapeDtypeStruct((chunk, column + kv_count * 2 * HEAD_SIZE), jnp.bfloat16)
    any_spec = pl.BlockSpec(memory_space=pl.ANY)
    return pl.pallas_call(
        functools.partial(finish_kernel, kv_count, owners, column, aliased),
        grid=(kv_count,),
        in_specs=[
            pl.BlockSpec(memory_space=pltpu.SMEM),
            pl.BlockSpec((tok_local, 2 * HEAD_SIZE), lambda g: (0, g)),
            pl.BlockSpec((WINDOW_LENGTH, 2 * HEAD_SIZE), lambda g: (0, g)),
        ]
        + ([any_spec] * owners if aliased else []),
        out_specs=[any_spec] * owners,
        out_shape=[shape] * owners,
        input_output_aliases={3 + i: i for i in range(owners)} if aliased else {},
        scratch_shapes=[
            pltpu.VMEM((kv_count, tok_local, 2 * HEAD_SIZE), jnp.bfloat16),
            pltpu.SemaphoreType.DMA((kv_count, owners, 2)),
        ],
        compiler_params=pltpu.CompilerParams(vmem_limit_bytes=32 * 1024 * 1024),
        cost_estimate=pl.CostEstimate(
            flops=0, bytes_accessed=16 * tok_local * kv_count * HEAD_SIZE, transcendentals=0
        ),
        name="finish",
    )(scal, part, back, *(bufs if aliased else ()))


def place_kernel(plan, owners, group, kv_local, aliased, scal, *rest):
    blocks = rest[:owners]
    outs = rest[owners + (3 if aliased else 0) :][:3]
    scr, in_sems, out_sems = rest[-3:]
    me = scal[0]
    loads = [
        pltpu.make_async_copy(blocks[flip], scr.at[flip], in_sems.at[flip])
        for flip in range(owners)
    ]
    for load in loads:
        load.start()
    stores = []
    for flip in range(owners):
        loads[flip].wait()
        source = jnp.bitwise_xor(me, flip)
        column = 0
        for which, (layer, kv_first, kv_count) in plan:
            heads = kv_count * group if which == 0 else kv_count
            home = kv_local * group if which == 0 else kv_local
            first = kv_first * group if which == 0 else kv_first
            place = pl.multiple_of((source * home + first) * HEAD_SIZE, HEAD_SIZE)
            store = pltpu.make_async_copy(
                scr.at[flip, :, pl.ds(column, heads * HEAD_SIZE)],
                outs[which].at[layer, :, pl.ds(place, heads * HEAD_SIZE)],
                out_sems.at[len(stores)],
            )
            store.start()
            stores.append(store)
            column += heads * HEAD_SIZE
    for store in stores:
        store.wait()


def place_call(plan, owners, group, kv_local, scal, blocks, outs):
    chunk, width = blocks[0].shape
    aliased = outs is not None
    any_spec = pl.BlockSpec(memory_space=pl.ANY)
    shapes = [
        jax.ShapeDtypeStruct(
            (SLIDING_LAYERS, chunk, owners * heads * HEAD_SIZE), jnp.bfloat16
        )
        for heads in (kv_local * group, kv_local, kv_local)
    ]
    return pl.pallas_call(
        functools.partial(place_kernel, plan, owners, group, kv_local, aliased),
        in_specs=[pl.BlockSpec(memory_space=pltpu.SMEM)]
        + [any_spec] * (owners + (3 if aliased else 0)),
        out_specs=[any_spec] * 3,
        out_shape=shapes,
        input_output_aliases={1 + owners + i: i for i in range(3)} if aliased else {},
        scratch_shapes=[
            pltpu.VMEM((owners, chunk, width), jnp.bfloat16),
            pltpu.SemaphoreType.DMA((owners,)),
            pltpu.SemaphoreType.DMA((owners * len(plan),)),
        ],
        compiler_params=pltpu.CompilerParams(vmem_limit_bytes=16 * 1024 * 1024),
        cost_estimate=pl.CostEstimate(
            flops=0, bytes_accessed=owners * chunk * width * 4, transcendentals=0
        ),
        name="place",
    )(scal, *blocks, *(outs if aliased else ()))


def shards(queries, layer_keys_input, layer_values_input, attn_out, grad_out, log_norm, window):
    tok_local = queries.shape[1]
    kv_local = layer_keys_input.shape[2] // HEAD_SIZE
    group = queries.shape[2] // layer_keys_input.shape[2]
    owners = lax.axis_size("head")
    shard = lax.axis_index("ctx")
    scal = jnp.concatenate(
        [
            jnp.stack([lax.axis_index("head"), (shard == 0).astype(jnp.int32)]).astype(jnp.int32),
            window.astype(jnp.int32),
        ]
    )
    each = min(2, kv_local)
    pieces = [
        (layer, kv_first, each)
        for layer in range(SLIDING_LAYERS)
        for kv_first in range(0, kv_local, each)
    ]

    def halo_of(some):
        parts = []
        for layer, kv_first, kv_count in some:
            for kv in range(kv_first, kv_first + kv_count):
                columns = slice(kv * HEAD_SIZE, (kv + 1) * HEAD_SIZE)
                parts.append(layer_keys_input[layer, tok_local - WINDOW_LENGTH :, columns])
                parts.append(layer_values_input[layer, tok_local - WINDOW_LENGTH :, columns])
        return shifted(jnp.concatenate(parts, 1), "ctx", 1)

    first_halo = halo_of(pieces[:1])
    other_halo = halo_of(pieces[1:])
    halos = [(first_halo, 0)] + [(other_halo, index * each) for index in range(len(pieces) - 1)]

    outs = None
    waiting = None

    def send(plan, bufs, outs):
        blocks = [bufs[0]] + [swapped(bufs[flip], "head", flip) for flip in range(1, owners)]
        return place_call(plan, owners, group, kv_local, scal, blocks, outs)

    after = scal
    for piece, (halo, column) in zip(pieces, halos):
        kv_count = piece[2]
        extra = 0 if waiting is None else 2 * waiting[0][2]
        bufs, back, part = band_call(
            piece,
            extra,
            owners,
            scal,
            queries,
            grad_out,
            attn_out,
            log_norm,
            layer_keys_input,
            layer_values_input,
            halo,
            column,
            after,
        )
        after = part
        back = shifted(back, "ctx", -1)
        plan = [(0, piece)]
        if waiting is not None:
            old, old_part, old_back = waiting
            bufs = finish_call(
                old[2], owners, kv_count * group * HEAD_SIZE, scal, old_part, old_back, bufs
            )
            after = bufs[0]
            plan += [(1, old), (2, old)]
        outs = send(plan, bufs, outs)
        waiting = (piece, part, back)
    old, old_part, old_back = waiting
    bufs = finish_call(old[2], owners, 0, scal, old_part, old_back, None)
    outs = send([(1, old), (2, old)], bufs, outs)
    return tuple(outs)


def solution(mesh):
    in_specs = (
        P(None, "ctx", "head"),
        P(None, "ctx", "head"),
        P(None, "ctx", "head"),
        P(None, "ctx", "head"),
        P(None, "ctx", "head"),
        P(None, "head", "ctx"),
        P(),
    )
    out_specs = (
        P(None, ("ctx", "head"), None),
        P(None, ("ctx", "head"), None),
        P(None, ("ctx", "head"), None),
    )
    return jax.shard_map(shards, mesh=mesh, in_specs=in_specs, out_specs=out_specs, check_vma=False)
```

```python
import functools
import math

import jax
import jax.numpy as jnp
from jax import lax
from jax.experimental import pallas as pl
from jax.experimental.pallas import tpu as pltpu
from jax.sharding import PartitionSpec as P

HEAD_SIZE = 128
WINDOW_LENGTH = 1024
QUERY_PRE = 168
SLIDING_LAYERS = 2
TILE = 256
SCALE = QUERY_PRE ** (-0.5)
LOG2E = math.log2(math.e)
FAR = 1 << 20

NT = (((1,), (1,)), ((), ()))
NN = (((1,), (0,)), ((), ()))


def dot(a, b, dims=NN):
    return lax.dot_general(a, b, dims, preferred_element_type=jnp.float32)


def shifted(value, axis, steps):
    count = lax.axis_size(axis)
    first, last = (max(0, -steps), min(count, count - steps))
    return lax.ppermute(value, axis, [(source, source + steps) for source in range(first, last)])


def swapped(value, axis, flip):
    count = lax.axis_size(axis)
    return lax.ppermute(value, axis, [(source, source ^ flip) for source in range(count)])


def pack_kernel(plan, rows, *rest):
    count = len(plan)
    keys, values = rest[:2]
    outs = rest[2 : 2 + count]
    scrs = rest[2 + count : 2 + 2 * count]
    in_sems, out_sems = rest[2 + 2 * count :]
    loads = []
    for index, (layer, kv_first, kv_count) in enumerate(plan):
        width = kv_count * HEAD_SIZE
        for kind, array in enumerate((keys, values)):
            loads.append(
                pltpu.make_async_copy(
                    array.at[layer, rows, pl.ds(kv_first * HEAD_SIZE, width)],
                    scrs[index].at[:, pl.ds(kind * width, width)],
                    in_sems.at[index, kind],
                )
            )
    for load in loads:
        load.start()
    stores = []
    for index in range(count):
        loads[2 * index].wait()
        loads[2 * index + 1].wait()
        store = pltpu.make_async_copy(scrs[index], outs[index], out_sems.at[index])
        store.start()
        stores.append(store)
    for store in stores:
        store.wait()


def pack_call(plan, keys, values):
    tok_local = keys.shape[1]
    any_spec = pl.BlockSpec(memory_space=pl.ANY)
    sizes = [(WINDOW_LENGTH, 2 * kv_count * HEAD_SIZE) for _, _, kv_count in plan]
    return pl.pallas_call(
        functools.partial(pack_kernel, plan, pl.ds(tok_local - WINDOW_LENGTH, WINDOW_LENGTH)),
        in_specs=[any_spec] * 2,
        out_specs=[any_spec] * len(plan),
        out_shape=[jax.ShapeDtypeStruct(size, jnp.bfloat16) for size in sizes],
        scratch_shapes=[pltpu.VMEM(size, jnp.bfloat16) for size in sizes]
        + [pltpu.SemaphoreType.DMA((len(plan), 2)), pltpu.SemaphoreType.DMA((len(plan),))],
        compiler_params=pltpu.CompilerParams(vmem_limit_bytes=16 * 1024 * 1024),
        cost_estimate=pl.CostEstimate(
            flops=0, bytes_accessed=4 * sum(size[0] * size[1] for size in sizes), transcendentals=0
        ),
        name="pack",
    )(keys, values)


def band_kernel(
    layer,
    kv_first,
    kv_count,
    owners,
    scal,
    q_ref,
    do_ref,
    out_ref,
    lse_ref,
    k_ref,
    v_ref,
    k_halo,
    v_halo,
    after,
    *rest,
):
    dq_bufs = rest[:owners]
    back_ref, part_ref, kx, vx, kt, acc, lse2_scr, delta_scr, dq_scr, sems = rest[owners:]
    tok_local = q_ref.shape[1]
    group = q_ref.shape[2] // HEAD_SIZE
    chunk = tok_local // owners
    step = pl.program_id(0)
    me = scal[0]
    first_shard = scal[1]
    win = scal[2 + layer]
    wide = group * TILE

    kx[0:WINDOW_LENGTH] = k_halo[...]
    vx[0:WINDOW_LENGTH] = v_halo[...]
    kx[WINDOW_LENGTH:] = k_ref[0]
    vx[WINDOW_LENGTH:] = v_ref[0]
    kt[...] = kx[...].T
    acc[...] = jnp.zeros_like(acc)

    rows = lax.broadcasted_iota(jnp.int32, (TILE, wide), 0)
    lanes = lax.broadcasted_iota(jnp.int32, (1, wide), 1) % TILE

    def stacked(ref, start):
        block = ref[0, pl.ds(start, TILE), :]
        return jnp.concatenate(
            [block[:, h * HEAD_SIZE : (h + 1) * HEAD_SIZE] for h in range(group)], 0
        )

    ones = jnp.ones((8, HEAD_SIZE), jnp.bfloat16)
    head = (kv_first + step) * group
    for block in range(tok_local // TILE):
        start = block * TILE
        columns = slice(block * wide, (block + 1) * wide)
        prod = stacked(do_ref, start).astype(jnp.float32) * stacked(out_ref, start).astype(jnp.float32)
        high = prod.astype(jnp.bfloat16)
        low = (prod - high.astype(jnp.float32)).astype(jnp.bfloat16)
        delta_scr[:, columns] = dot(ones, high, NT) + dot(ones, low, NT)
        for h in range(group):
            lse2_scr[0:1, block * wide + h * TILE : block * wide + (h + 1) * TILE] = (
                lse_ref[0, pl.ds(head + h, 1), start : start + TILE] * LOG2E
            )

    tiles = WINDOW_LENGTH // TILE + 1

    def weights(start, tile, half, scores, grad_prob, lse2, delta):
        place = tile - half
        prob = jnp.exp2(scores * (SCALE * LOG2E) - lse2)
        if place == tiles - 1:
            seen = rows <= lanes
        else:
            bound = WINDOW_LENGTH - win - place * TILE
            outside = jnp.logical_and(first_shard == 1, start + tile * TILE < WINDOW_LENGTH)
            seen = rows > lanes + jnp.where(outside, FAR, bound)
        prob = jnp.where(seen, prob, 0.0)
        return prob.astype(jnp.bfloat16), (prob * (grad_prob - delta)).astype(jnp.bfloat16)

    def one_pair(pair, carry):
        start = pl.multiple_of(pair * 2 * TILE, 2 * TILE)
        columns = pl.ds(pl.multiple_of(pair * 2 * wide, 2 * wide), 2 * wide)
        q4 = jnp.concatenate([stacked(q_ref, start), stacked(q_ref, start + TILE)], 0)
        do4 = jnp.concatenate([stacked(do_ref, start), stacked(do_ref, start + TILE)], 0)
        delta = delta_scr[0:1, columns]
        lse2 = lse2_scr[0:1, columns]
        score_lows = ([], [])

        def finish(tile, halves, scores, grad_prob):
            low = halves[0] * wide
            high = (halves[-1] + 1) * wide
            probs, grads = [], []
            for half in halves:
                mine = slice(half * wide - low, (half + 1) * wide - low)
                ours = slice(half * wide, (half + 1) * wide)
                prob_low, score_low = weights(
                    start, tile, half, scores[:, mine], grad_prob[:, mine], lse2[:, ours], delta[:, ours]
                )
                probs.append(prob_low)
                grads.append(score_low)
                score_lows[half].append(score_low)
            span = pl.ds(start + tile * TILE, TILE)
            acc[span, HEAD_SIZE:] += dot(jnp.concatenate(probs, 1), do4[low:high])
            acc[span, :HEAD_SIZE] += dot(jnp.concatenate(grads, 1), q4[low:high])

        held = None
        for tile in range(tiles + 1):
            halves = [half for half in (0, 1) if 0 <= tile - half < tiles]
            low = halves[0] * wide
            high = (halves[-1] + 1) * wide
            span = pl.ds(start + tile * TILE, TILE)
            scores = dot(kx[span, :], q4[low:high], NT)
            grad_prob = dot(vx[span, :], do4[low:high], NT)
            if held is not None:
                finish(*held)
            held = (tile, halves, scores, grad_prob)
        finish(*held)
        for half in (0, 1):
            begin = start + half * TILE
            keys_t = kt[:, pl.ds(pl.multiple_of(begin, TILE), tiles * TILE)]
            dq_t = dot(keys_t, jnp.concatenate(score_lows[half], 0))
            dq = (dq_t.T * SCALE).astype(jnp.bfloat16)
            for h in range(group):
                dq_scr[step, pl.ds(begin, TILE), h * HEAD_SIZE : (h + 1) * HEAD_SIZE] = dq[
                    h * TILE : (h + 1) * TILE
                ]
        return carry

    lax.fori_loop(0, tok_local // (2 * TILE), one_pair, 0)

    back_ref[:, :HEAD_SIZE] = (acc[0:WINDOW_LENGTH, :HEAD_SIZE] * SCALE).astype(jnp.bfloat16)
    back_ref[:, HEAD_SIZE:] = acc[0:WINDOW_LENGTH, HEAD_SIZE:].astype(jnp.bfloat16)
    part_ref[:, :HEAD_SIZE] = acc[WINDOW_LENGTH:, :HEAD_SIZE] * SCALE
    part_ref[:, HEAD_SIZE:] = acc[WINDOW_LENGTH:, HEAD_SIZE:]

    def copies(index):
        result = []
        for flip in range(owners):
            owner = jnp.bitwise_xor(me, flip)
            source = dq_scr.at[index, pl.ds(pl.multiple_of(owner * chunk, chunk), chunk), :]
            target = dq_bufs[flip].at[:, pl.ds(index * group * HEAD_SIZE, group * HEAD_SIZE)]
            result.append(pltpu.make_async_copy(source, target, sems.at[index, flip]))
        return result

    for index in range(kv_count):

        @pl.when(step == index)
        def _(index=index):
            for copy in copies(index):
                copy.start()

    @pl.when(step == kv_count - 1)
    def _():
        for index in range(kv_count):
            for copy in copies(index):
                copy.wait()


def band_call(piece, extra, owners, scal, queries, grad_out, attn_out, log_norm, keys, values, halo, column, after):
    layer, kv_first, kv_count = piece
    tok_local = queries.shape[1]
    group = queries.shape[2] // keys.shape[2]
    span = WINDOW_LENGTH + tok_local
    chunk = tok_local // owners
    halo_kv = halo.shape[1] // (2 * HEAD_SIZE)
    q_spec = pl.BlockSpec((1, tok_local, group * HEAD_SIZE), lambda g: (layer, 0, kv_first + g))
    kv_spec = pl.BlockSpec((1, tok_local, HEAD_SIZE), lambda g: (layer, 0, kv_first + g))
    pairs = tok_local * (WINDOW_LENGTH + TILE) * group * kv_count
    outs = pl.pallas_call(
        functools.partial(band_kernel, layer, kv_first, kv_count, owners),
        grid=(kv_count,),
        in_specs=[
            pl.BlockSpec(memory_space=pltpu.SMEM),
            q_spec,
            q_spec,
            q_spec,
            pl.BlockSpec((1,) + log_norm.shape[1:], lambda g: (layer, 0, 0)),
            kv_spec,
            kv_spec,
            pl.BlockSpec((WINDOW_LENGTH, HEAD_SIZE), lambda g: (0, column + g)),
            pl.BlockSpec((WINDOW_LENGTH, HEAD_SIZE), lambda g: (0, halo_kv + column + g)),
            pl.BlockSpec(memory_space=pl.ANY),
        ],
        out_specs=[pl.BlockSpec(memory_space=pl.ANY)] * owners
        + [
            pl.BlockSpec((WINDOW_LENGTH, 2 * HEAD_SIZE), lambda g: (0, g)),
            pl.BlockSpec((tok_local, 2 * HEAD_SIZE), lambda g: (0, g)),
        ],
        out_shape=[
            jax.ShapeDtypeStruct((chunk, (kv_count * group + extra) * HEAD_SIZE), jnp.bfloat16)
        ]
        * owners
        + [
            jax.ShapeDtypeStruct((WINDOW_LENGTH, kv_count * 2 * HEAD_SIZE), jnp.bfloat16),
            jax.ShapeDtypeStruct((tok_local, kv_count * 2 * HEAD_SIZE), jnp.float32),
        ],
        scratch_shapes=[
            pltpu.VMEM((span, HEAD_SIZE), jnp.bfloat16),
            pltpu.VMEM((span, HEAD_SIZE), jnp.bfloat16),
            pltpu.VMEM((HEAD_SIZE, span), jnp.bfloat16),
            pltpu.VMEM((span, 2 * HEAD_SIZE), jnp.float32),
            pltpu.VMEM((8, tok_local * group), jnp.float32),
            pltpu.VMEM((8, tok_local * group), jnp.float32),
            pltpu.VMEM((kv_count, tok_local, group * HEAD_SIZE), jnp.bfloat16),
            pltpu.SemaphoreType.DMA((kv_count, owners)),
        ],
        compiler_params=pltpu.CompilerParams(vmem_limit_bytes=44 * 1024 * 1024),
        cost_estimate=pl.CostEstimate(
            flops=pairs * 2 * HEAD_SIZE * 5 * 4,
            bytes_accessed=8 * tok_local * group * kv_count * HEAD_SIZE,
            transcendentals=pairs,
        ),
        name="band",
    )(scal, queries, grad_out, attn_out, log_norm, keys, values, halo, halo, after)
    return outs[:owners], outs[owners], outs[owners + 1]


def finish_kernel(kv_count, owners, column, skip, scal, part_ref, back_ref, *rest):
    bufs = rest[skip:][:owners]
    scr, sems = rest[-2:]
    tok_local = part_ref.shape[0]
    chunk = tok_local // owners
    step = pl.program_id(0)
    me = scal[0]
    plain = tok_local - WINDOW_LENGTH
    scr[step, :plain] = part_ref[:plain].astype(jnp.bfloat16)
    scr[step, plain:] = (part_ref[plain:] + back_ref[...].astype(jnp.float32)).astype(jnp.bfloat16)

    def copies(index):
        result = []
        for flip in range(owners):
            owner = jnp.bitwise_xor(me, flip)
            rows = pl.ds(pl.multiple_of(owner * chunk, chunk), chunk)
            for kind in range(2):
                place = column + (kind * kv_count + index) * HEAD_SIZE
                result.append(
                    pltpu.make_async_copy(
                        scr.at[index, rows, pl.ds(kind * HEAD_SIZE, HEAD_SIZE)],
                        bufs[flip].at[:, pl.ds(place, HEAD_SIZE)],
                        sems.at[index, flip, kind],
                    )
                )
        return result

    for index in range(kv_count):

        @pl.when(step == index)
        def _(index=index):
            for copy in copies(index):
                copy.start()

    @pl.when(step == kv_count - 1)
    def _():
        for index in range(kv_count):
            for copy in copies(index):
                copy.wait()


def finish_call(kv_count, owners, column, scal, part, back, bufs, after):
    tok_local = part.shape[0]
    chunk = tok_local // owners
    aliased = bufs is not None
    shape = jax.ShapeDtypeStruct((chunk, column + kv_count * 2 * HEAD_SIZE), jnp.bfloat16)
    any_spec = pl.BlockSpec(memory_space=pl.ANY)
    return pl.pallas_call(
        functools.partial(
            finish_kernel, kv_count, owners, column, len(after) + (owners if aliased else 0)
        ),
        grid=(kv_count,),
        in_specs=[
            pl.BlockSpec(memory_space=pltpu.SMEM),
            pl.BlockSpec((tok_local, 2 * HEAD_SIZE), lambda g: (0, g)),
            pl.BlockSpec((WINDOW_LENGTH, 2 * HEAD_SIZE), lambda g: (0, g)),
        ]
        + [any_spec] * ((owners if aliased else 0) + len(after)),
        out_specs=[any_spec] * owners,
        out_shape=[shape] * owners,
        input_output_aliases={3 + i: i for i in range(owners)} if aliased else {},
        scratch_shapes=[
            pltpu.VMEM((kv_count, tok_local, 2 * HEAD_SIZE), jnp.bfloat16),
            pltpu.SemaphoreType.DMA((kv_count, owners, 2)),
        ],
        compiler_params=pltpu.CompilerParams(vmem_limit_bytes=32 * 1024 * 1024),
        cost_estimate=pl.CostEstimate(
            flops=0, bytes_accessed=16 * tok_local * kv_count * HEAD_SIZE, transcendentals=0
        ),
        name="finish",
    )(scal, part, back, *(bufs if aliased else ()), *after)


def place_kernel(plan, owners, group, kv_local, aliased, scal, *rest):
    blocks = rest[:owners]
    outs = rest[owners + (3 if aliased else 0) :][:3]
    scr, in_sems, out_sems = rest[-3:]
    me = scal[0]
    loads = [
        pltpu.make_async_copy(blocks[flip], scr.at[flip], in_sems.at[flip])
        for flip in range(owners)
    ]
    for load in loads:
        load.start()
    stores = []
    for flip in range(owners):
        loads[flip].wait()
        source = jnp.bitwise_xor(me, flip)
        column = 0
        for which, (layer, kv_first, kv_count) in plan:
            heads = kv_count * group if which == 0 else kv_count
            home = kv_local * group if which == 0 else kv_local
            first = kv_first * group if which == 0 else kv_first
            place = pl.multiple_of((source * home + first) * HEAD_SIZE, HEAD_SIZE)
            store = pltpu.make_async_copy(
                scr.at[flip, :, pl.ds(column, heads * HEAD_SIZE)],
                outs[which].at[layer, :, pl.ds(place, heads * HEAD_SIZE)],
                out_sems.at[len(stores)],
            )
            store.start()
            stores.append(store)
            column += heads * HEAD_SIZE
    for store in stores:
        store.wait()


def place_call(plan, owners, group, kv_local, scal, blocks, outs):
    chunk, width = blocks[0].shape
    aliased = outs is not None
    any_spec = pl.BlockSpec(memory_space=pl.ANY)
    shapes = [
        jax.ShapeDtypeStruct(
            (SLIDING_LAYERS, chunk, owners * heads * HEAD_SIZE), jnp.bfloat16
        )
        for heads in (kv_local * group, kv_local, kv_local)
    ]
    return pl.pallas_call(
        functools.partial(place_kernel, plan, owners, group, kv_local, aliased),
        in_specs=[pl.BlockSpec(memory_space=pltpu.SMEM)]
        + [any_spec] * (owners + (3 if aliased else 0)),
        out_specs=[any_spec] * 3,
        out_shape=shapes,
        input_output_aliases={1 + owners + i: i for i in range(3)} if aliased else {},
        scratch_shapes=[
            pltpu.VMEM((owners, chunk, width), jnp.bfloat16),
            pltpu.SemaphoreType.DMA((owners,)),
            pltpu.SemaphoreType.DMA((owners * len(plan),)),
        ],
        compiler_params=pltpu.CompilerParams(vmem_limit_bytes=16 * 1024 * 1024),
        cost_estimate=pl.CostEstimate(
            flops=0, bytes_accessed=owners * chunk * width * 4, transcendentals=0
        ),
        name="place",
    )(scal, *blocks, *(outs if aliased else ()))


def shards(queries, layer_keys_input, layer_values_input, attn_out, grad_out, log_norm, window):
    tok_local = queries.shape[1]
    kv_local = layer_keys_input.shape[2] // HEAD_SIZE
    group = queries.shape[2] // layer_keys_input.shape[2]
    owners = lax.axis_size("head")
    shard = lax.axis_index("ctx")
    scal = jnp.concatenate(
        [
            jnp.stack([lax.axis_index("head"), (shard == 0).astype(jnp.int32)]).astype(jnp.int32),
            window.astype(jnp.int32),
        ]
    )
    pieces = []
    for layer in range(SLIDING_LAYERS):
        kv_first = 0
        while kv_first < kv_local:
            kv_count = 1 if layer == 0 and kv_first < 2 else min(2, kv_local - kv_first)
            pieces.append((layer, kv_first, kv_count))
            kv_first += kv_count

    plans = [[(0, 0, 1)], [(0, 1, kv_local - 1)], [(1, 0, kv_local)]]
    packed = pack_call(plans[0], layer_keys_input, layer_values_input)
    packed += pack_call(plans[1] + plans[2], layer_keys_input, layer_values_input)
    halos = [shifted(block, "ctx", 1) for block in packed]

    def halo_of(layer, kv_first):
        if layer == 1:
            return halos[2], kv_first
        return (halos[0], 0) if kv_first == 0 else (halos[1], kv_first - 1)

    outs = None
    waiting = None
    after = scal
    sent = []

    def send(plan, bufs):
        blocks = [bufs[0]] + [swapped(bufs[flip], "head", flip) for flip in range(1, owners)]
        sent.append((plan, blocks))

    for index, piece in enumerate(pieces):
        layer, kv_first, kv_count = piece
        halo, column = halo_of(layer, kv_first)
        extra = 0 if waiting is None else 2 * waiting[0][2]
        bufs, back, part = band_call(
            piece,
            extra,
            owners,
            scal,
            queries,
            grad_out,
            attn_out,
            log_norm,
            layer_keys_input,
            layer_values_input,
            halo,
            column,
            after,
        )
        after = part
        back = shifted(back, "ctx", -1)
        plan = [(0, piece)]
        if waiting is not None:
            old, old_part, old_back = waiting
            before = sent[-1][1][1:]
            bufs = finish_call(
                old[2], owners, kv_count * group * HEAD_SIZE, scal, old_part, old_back, bufs, before
            )
            after = bufs[0]
            plan += [(1, old), (2, old)]
        send(plan, bufs)
        waiting = (piece, part, back)
    old, old_part, old_back = waiting
    bufs = finish_call(old[2], owners, 0, scal, old_part, old_back, None, ())
    send([(1, old), (2, old)], bufs)
    for plan, blocks in sent:
        outs = place_call(plan, owners, group, kv_local, scal, blocks, outs)
    return tuple(outs)


def solution(mesh):
    in_specs = (
        P(None, "ctx", "head"),
        P(None, "ctx", "head"),
        P(None, "ctx", "head"),
        P(None, "ctx", "head"),
        P(None, "ctx", "head"),
        P(None, "head", "ctx"),
        P(),
    )
    out_specs = (
        P(None, ("ctx", "head"), None),
        P(None, ("ctx", "head"), None),
        P(None, ("ctx", "head"), None),
    )
    return jax.shard_map(shards, mesh=mesh, in_specs=in_specs, out_specs=out_specs, check_vma=False)
```

```python
import functools
import math

import jax
import jax.numpy as jnp
from jax import lax
from jax.experimental import pallas as pl
from jax.experimental.pallas import tpu as pltpu
from jax.sharding import PartitionSpec as P

HEAD_SIZE = 128
WINDOW_LENGTH = 1024
QUERY_PRE = 168
SLIDING_LAYERS = 2
TILE = 128
UNITS = 4
SCALE = QUERY_PRE ** (-0.5)
LOG2E = math.log2(math.e)
FAR = 1e30

NT = (((1,), (1,)), ((), ()))
NN = (((1,), (0,)), ((), ()))


def dot(a, b, dims=NN):
    return lax.dot_general(a, b, dims, preferred_element_type=jnp.float32)


def shifted(value, axis, steps):
    count = lax.axis_size(axis)
    first, last = (max(0, -steps), min(count, count - steps))
    return lax.ppermute(value, axis, [(source, source + steps) for source in range(first, last)])


def swapped(value, axis, flip):
    count = lax.axis_size(axis)
    return lax.ppermute(value, axis, [(source, source ^ flip) for source in range(count)])


def pack_kernel(plan, rows, *rest):
    count = len(plan)
    keys, values = rest[:2]
    outs = rest[2 : 2 + count]
    scrs = rest[2 + count : 2 + 2 * count]
    in_sems, out_sems = rest[2 + 2 * count :]
    loads = []
    for index, (layer, kv_first, kv_count) in enumerate(plan):
        width = kv_count * HEAD_SIZE
        for kind, array in enumerate((keys, values)):
            loads.append(
                pltpu.make_async_copy(
                    array.at[layer, rows, pl.ds(kv_first * HEAD_SIZE, width)],
                    scrs[index].at[:, pl.ds(kind * width, width)],
                    in_sems.at[index, kind],
                )
            )
    for load in loads:
        load.start()
    stores = []
    for index in range(count):
        loads[2 * index].wait()
        loads[2 * index + 1].wait()
        store = pltpu.make_async_copy(scrs[index], outs[index], out_sems.at[index])
        store.start()
        stores.append(store)
    for store in stores:
        store.wait()


def pack_call(plan, keys, values):
    tok_local = keys.shape[1]
    any_spec = pl.BlockSpec(memory_space=pl.ANY)
    sizes = [(WINDOW_LENGTH, 2 * kv_count * HEAD_SIZE) for _, _, kv_count in plan]
    return pl.pallas_call(
        functools.partial(pack_kernel, plan, pl.ds(tok_local - WINDOW_LENGTH, WINDOW_LENGTH)),
        in_specs=[any_spec] * 2,
        out_specs=[any_spec] * len(plan),
        out_shape=[jax.ShapeDtypeStruct(size, jnp.bfloat16) for size in sizes],
        scratch_shapes=[pltpu.VMEM(size, jnp.bfloat16) for size in sizes]
        + [pltpu.SemaphoreType.DMA((len(plan), 2)), pltpu.SemaphoreType.DMA((len(plan),))],
        compiler_params=pltpu.CompilerParams(vmem_limit_bytes=16 * 1024 * 1024),
        cost_estimate=pl.CostEstimate(
            flops=0, bytes_accessed=4 * sum(size[0] * size[1] for size in sizes), transcendentals=0
        ),
        name="pack",
    )(keys, values)


def band_kernel(
    layer,
    kv_first,
    kv_count,
    owners,
    scal,
    q_ref,
    do_ref,
    out_ref,
    lse_ref,
    k_ref,
    v_ref,
    k_halo,
    v_halo,
    after,
    *rest,
):
    dq_bufs = rest[:owners]
    back_ref, part_ref, kx, vx, kt, acc, lse2_scr, dq_scr, sems = rest[owners:]
    tok_local = q_ref.shape[1]
    group = q_ref.shape[2] // HEAD_SIZE
    chunk = tok_local // owners
    step = pl.program_id(0)
    me = scal[0]
    first_shard = scal[1]
    win = scal[2 + layer]
    wide = group * TILE

    rows_step = UNITS * TILE
    head = (kv_first + step) * group

    kx[0:WINDOW_LENGTH] = k_halo[...]
    vx[0:WINDOW_LENGTH] = v_halo[...]
    kx[WINDOW_LENGTH:] = k_ref[0]
    vx[WINDOW_LENGTH:] = v_ref[0]
    kt[:, 0:WINDOW_LENGTH] = k_halo[...].T
    for h in range(group):
        lse2_scr[h : h + 1, :] = lse_ref[0, pl.ds(head + h, 1), :] * LOG2E
    acc[0:WINDOW_LENGTH] = jnp.zeros((WINDOW_LENGTH, 2 * HEAD_SIZE), jnp.float32)

    rows = lax.broadcasted_iota(jnp.int32, (TILE, wide), 0)
    lanes = lax.broadcasted_iota(jnp.int32, (1, wide), 1) % TILE
    ones = jnp.ones((8, 2 * HEAD_SIZE), jnp.bfloat16)

    def stacked(ref, start):
        block = ref[0, pl.ds(start, TILE), :]
        return jnp.concatenate(
            [block[:, h * HEAD_SIZE : (h + 1) * HEAD_SIZE] for h in range(group)], 0
        )

    def sweep(reach):
        tiles = reach // TILE + 1
        skipped = WINDOW_LENGTH - reach

        def one_step(index, carry):
            start = pl.multiple_of(index * rows_step, rows_step)
            fresh = pl.ds(pl.multiple_of(start + WINDOW_LENGTH, TILE), rows_step)
            kt[:, fresh] = kx[fresh, :].T
            acc[fresh, :] = jnp.zeros((rows_step, 2 * HEAD_SIZE), jnp.float32)

            def products(unit):
                begin = pl.multiple_of(start + unit * TILE, TILE)
                q2 = stacked(q_ref, begin)
                do2 = stacked(do_ref, begin)
                span = pl.ds(pl.multiple_of(begin + skipped, TILE), tiles * TILE)
                scores = dot(kx[span, :], q2, NT)
                grad_prob = dot(vx[span, :], do2, NT)
                prod = do2.astype(jnp.float32) * stacked(out_ref, begin).astype(jnp.float32)
                high = prod.astype(jnp.bfloat16)
                low = (prod - high.astype(jnp.float32)).astype(jnp.bfloat16)
                delta = dot(ones, jnp.concatenate([high, low], 1), NT)[0:1]
                lse2 = jnp.concatenate(
                    [lse2_scr[h : h + 1, pl.ds(begin, TILE)] for h in range(group)], 1
                )
                return begin, q2, do2, scores, grad_prob, delta, lse2

            def weights(begin, q2, do2, scores, grad_prob, delta, lse2):
                probs, grads = [], []
                for tile in range(tiles):
                    part = slice(tile * TILE, (tile + 1) * TILE)
                    line = lse2
                    if tile < tiles - 1:
                        outside = jnp.logical_and(
                            first_shard == 1, begin + skipped + tile * TILE < WINDOW_LENGTH
                        )
                        line = jnp.where(outside, FAR, lse2)
                    prob = jnp.exp2(scores[part] * (SCALE * LOG2E) - line)
                    if tile == tiles - 1:
                        prob = jnp.where(rows <= lanes, prob, 0.0)
                    elif tile < 2:
                        prob = jnp.where(rows > lanes + (reach - win - tile * TILE), prob, 0.0)
                    probs.append(prob.astype(jnp.bfloat16))
                    grads.append((prob * (grad_prob[part] - delta)).astype(jnp.bfloat16))
                return begin, q2, do2, probs, grads

            def finish(first, second):
                begin = first[0]
                for lefts, rights, kind in ((3, 2, 1), (4, 1, 0)):
                    one, two = first[lefts], second[lefts]
                    side = slice(kind * HEAD_SIZE, (kind + 1) * HEAD_SIZE)
                    base = begin + skipped
                    middle = jnp.concatenate(
                        [jnp.concatenate(one[1:], 0), jnp.concatenate(two[:-1], 0)], 1
                    )
                    both = jnp.concatenate([first[rights], second[rights]], 0)
                    acc[pl.ds(pl.multiple_of(base, TILE), TILE), side] += dot(one[0], first[rights])
                    acc[pl.ds(pl.multiple_of(base + TILE, TILE), (tiles - 1) * TILE), side] += dot(
                        middle, both
                    )
                    acc[pl.ds(pl.multiple_of(base + tiles * TILE, TILE), TILE), side] += dot(
                        two[-1], second[rights]
                    )
                for begin, _, _, _, grads in (first, second):
                    span = pl.ds(pl.multiple_of(begin + skipped, TILE), tiles * TILE)
                    dq = (dot(kt[:, span], jnp.concatenate(grads, 0)).T * SCALE).astype(jnp.bfloat16)
                    for h in range(group):
                        dq_scr[step, pl.ds(begin, TILE), h * HEAD_SIZE : (h + 1) * HEAD_SIZE] = dq[
                            h * TILE : (h + 1) * TILE
                        ]

            held = products(0)
            done = []
            for unit in range(UNITS):
                coming = products(unit + 1) if unit + 1 < UNITS else None
                done.append(weights(*held))
                held = coming
                if unit % 2 == 1:
                    finish(done[unit - 1], done[unit])
            return carry

        lax.fori_loop(0, tok_local // rows_step, one_step, 0)

    low = 0
    for reach in range(WINDOW_LENGTH // 2 + TILE, WINDOW_LENGTH + 1, TILE):

        @pl.when(jnp.logical_and(win > low, win <= reach))
        def _(reach=reach):
            sweep(reach)

        low = reach

    back_ref[:, :HEAD_SIZE] = (acc[0:WINDOW_LENGTH, :HEAD_SIZE] * SCALE).astype(jnp.bfloat16)
    back_ref[:, HEAD_SIZE:] = acc[0:WINDOW_LENGTH, HEAD_SIZE:].astype(jnp.bfloat16)
    part_ref[:, :HEAD_SIZE] = acc[WINDOW_LENGTH:, :HEAD_SIZE] * SCALE
    part_ref[:, HEAD_SIZE:] = acc[WINDOW_LENGTH:, HEAD_SIZE:]

    def copies(index):
        result = []
        for flip in range(owners):
            owner = jnp.bitwise_xor(me, flip)
            source = dq_scr.at[index, pl.ds(pl.multiple_of(owner * chunk, chunk), chunk), :]
            target = dq_bufs[flip].at[:, pl.ds(index * group * HEAD_SIZE, group * HEAD_SIZE)]
            result.append(pltpu.make_async_copy(source, target, sems.at[index, flip]))
        return result

    for index in range(kv_count):

        @pl.when(step == index)
        def _(index=index):
            for copy in copies(index):
                copy.start()

    @pl.when(step == kv_count - 1)
    def _():
        for index in range(kv_count):
            for copy in copies(index):
                copy.wait()


def band_call(piece, extra, owners, scal, queries, grad_out, attn_out, log_norm, keys, values, halo, column, after):
    layer, kv_first, kv_count = piece
    tok_local = queries.shape[1]
    group = queries.shape[2] // keys.shape[2]
    span = WINDOW_LENGTH + tok_local
    chunk = tok_local // owners
    halo_kv = halo.shape[1] // (2 * HEAD_SIZE)
    q_spec = pl.BlockSpec((1, tok_local, group * HEAD_SIZE), lambda g: (layer, 0, kv_first + g))
    kv_spec = pl.BlockSpec((1, tok_local, HEAD_SIZE), lambda g: (layer, 0, kv_first + g))
    pairs = tok_local * (WINDOW_LENGTH + 2 * TILE) * group * kv_count
    outs = pl.pallas_call(
        functools.partial(band_kernel, layer, kv_first, kv_count, owners),
        grid=(kv_count,),
        in_specs=[
            pl.BlockSpec(memory_space=pltpu.SMEM),
            q_spec,
            q_spec,
            q_spec,
            pl.BlockSpec((1,) + log_norm.shape[1:], lambda g: (layer, 0, 0)),
            kv_spec,
            kv_spec,
            pl.BlockSpec((WINDOW_LENGTH, HEAD_SIZE), lambda g: (0, column + g)),
            pl.BlockSpec((WINDOW_LENGTH, HEAD_SIZE), lambda g: (0, halo_kv + column + g)),
            pl.BlockSpec(memory_space=pl.ANY),
        ],
        out_specs=[pl.BlockSpec(memory_space=pl.ANY)] * owners
        + [
            pl.BlockSpec((WINDOW_LENGTH, 2 * HEAD_SIZE), lambda g: (0, g)),
            pl.BlockSpec((tok_local, 2 * HEAD_SIZE), lambda g: (0, g)),
        ],
        out_shape=[
            jax.ShapeDtypeStruct((chunk, (kv_count * group + extra) * HEAD_SIZE), jnp.bfloat16)
        ]
        * owners
        + [
            jax.ShapeDtypeStruct((WINDOW_LENGTH, kv_count * 2 * HEAD_SIZE), jnp.bfloat16),
            jax.ShapeDtypeStruct((tok_local, kv_count * 2 * HEAD_SIZE), jnp.float32),
        ],
        scratch_shapes=[
            pltpu.VMEM((span, HEAD_SIZE), jnp.bfloat16),
            pltpu.VMEM((span, HEAD_SIZE), jnp.bfloat16),
            pltpu.VMEM((HEAD_SIZE, span), jnp.bfloat16),
            pltpu.VMEM((span, 2 * HEAD_SIZE), jnp.float32),
            pltpu.VMEM((8, tok_local), jnp.float32),
            pltpu.VMEM((kv_count, tok_local, group * HEAD_SIZE), jnp.bfloat16),
            pltpu.SemaphoreType.DMA((kv_count, owners)),
        ],
        compiler_params=pltpu.CompilerParams(vmem_limit_bytes=44 * 1024 * 1024),
        cost_estimate=pl.CostEstimate(
            flops=pairs * 2 * HEAD_SIZE * 5 * 4,
            bytes_accessed=8 * tok_local * group * kv_count * HEAD_SIZE,
            transcendentals=pairs,
        ),
        name="band",
    )(scal, queries, grad_out, attn_out, log_norm, keys, values, halo, halo, after)
    return outs[:owners], outs[owners], outs[owners + 1]


def finish_kernel(kv_count, owners, column, skip, scal, part_ref, back_ref, *rest):
    bufs = rest[skip:][:owners]
    scr, sems = rest[-2:]
    tok_local = part_ref.shape[0]
    chunk = tok_local // owners
    step = pl.program_id(0)
    me = scal[0]
    plain = tok_local - WINDOW_LENGTH
    scr[step, :plain] = part_ref[:plain].astype(jnp.bfloat16)
    scr[step, plain:] = (part_ref[plain:] + back_ref[...].astype(jnp.float32)).astype(jnp.bfloat16)

    def copies(index):
        result = []
        for flip in range(owners):
            owner = jnp.bitwise_xor(me, flip)
            rows = pl.ds(pl.multiple_of(owner * chunk, chunk), chunk)
            for kind in range(2):
                place = column + (kind * kv_count + index) * HEAD_SIZE
                result.append(
                    pltpu.make_async_copy(
                        scr.at[index, rows, pl.ds(kind * HEAD_SIZE, HEAD_SIZE)],
                        bufs[flip].at[:, pl.ds(place, HEAD_SIZE)],
                        sems.at[index, flip, kind],
                    )
                )
        return result

    for index in range(kv_count):

        @pl.when(step == index)
        def _(index=index):
            for copy in copies(index):
                copy.start()

    @pl.when(step == kv_count - 1)
    def _():
        for index in range(kv_count):
            for copy in copies(index):
                copy.wait()


def finish_call(kv_count, owners, column, scal, part, back, bufs, after):
    tok_local = part.shape[0]
    chunk = tok_local // owners
    aliased = bufs is not None
    shape = jax.ShapeDtypeStruct((chunk, column + kv_count * 2 * HEAD_SIZE), jnp.bfloat16)
    any_spec = pl.BlockSpec(memory_space=pl.ANY)
    return pl.pallas_call(
        functools.partial(
            finish_kernel, kv_count, owners, column, len(after) + (owners if aliased else 0)
        ),
        grid=(kv_count,),
        in_specs=[
            pl.BlockSpec(memory_space=pltpu.SMEM),
            pl.BlockSpec((tok_local, 2 * HEAD_SIZE), lambda g: (0, g)),
            pl.BlockSpec((WINDOW_LENGTH, 2 * HEAD_SIZE), lambda g: (0, g)),
        ]
        + [any_spec] * ((owners if aliased else 0) + len(after)),
        out_specs=[any_spec] * owners,
        out_shape=[shape] * owners,
        input_output_aliases={3 + i: i for i in range(owners)} if aliased else {},
        scratch_shapes=[
            pltpu.VMEM((kv_count, tok_local, 2 * HEAD_SIZE), jnp.bfloat16),
            pltpu.SemaphoreType.DMA((kv_count, owners, 2)),
        ],
        compiler_params=pltpu.CompilerParams(vmem_limit_bytes=32 * 1024 * 1024),
        cost_estimate=pl.CostEstimate(
            flops=0, bytes_accessed=16 * tok_local * kv_count * HEAD_SIZE, transcendentals=0
        ),
        name="finish",
    )(scal, part, back, *(bufs if aliased else ()), *after)


def place_kernel(plan, owners, group, kv_local, aliased, scal, *rest):
    blocks = rest[:owners]
    outs = rest[owners + (3 if aliased else 0) :][:3]
    scr, in_sems, out_sems = rest[-3:]
    me = scal[0]
    loads = [
        pltpu.make_async_copy(blocks[flip], scr.at[flip], in_sems.at[flip])
        for flip in range(owners)
    ]
    for load in loads:
        load.start()
    stores = []
    for flip in range(owners):
        loads[flip].wait()
        source = jnp.bitwise_xor(me, flip)
        column = 0
        for which, (layer, kv_first, kv_count) in plan:
            heads = kv_count * group if which == 0 else kv_count
            home = kv_local * group if which == 0 else kv_local
            first = kv_first * group if which == 0 else kv_first
            place = pl.multiple_of((source * home + first) * HEAD_SIZE, HEAD_SIZE)
            store = pltpu.make_async_copy(
                scr.at[flip, :, pl.ds(column, heads * HEAD_SIZE)],
                outs[which].at[layer, :, pl.ds(place, heads * HEAD_SIZE)],
                out_sems.at[len(stores)],
            )
            store.start()
            stores.append(store)
            column += heads * HEAD_SIZE
    for store in stores:
        store.wait()


def place_call(plan, owners, group, kv_local, scal, blocks, outs):
    chunk, width = blocks[0].shape
    aliased = outs is not None
    any_spec = pl.BlockSpec(memory_space=pl.ANY)
    shapes = [
        jax.ShapeDtypeStruct(
            (SLIDING_LAYERS, chunk, owners * heads * HEAD_SIZE), jnp.bfloat16
        )
        for heads in (kv_local * group, kv_local, kv_local)
    ]
    return pl.pallas_call(
        functools.partial(place_kernel, plan, owners, group, kv_local, aliased),
        in_specs=[pl.BlockSpec(memory_space=pltpu.SMEM)]
        + [any_spec] * (owners + (3 if aliased else 0)),
        out_specs=[any_spec] * 3,
        out_shape=shapes,
        input_output_aliases={1 + owners + i: i for i in range(3)} if aliased else {},
        scratch_shapes=[
            pltpu.VMEM((owners, chunk, width), jnp.bfloat16),
            pltpu.SemaphoreType.DMA((owners,)),
            pltpu.SemaphoreType.DMA((owners * len(plan),)),
        ],
        compiler_params=pltpu.CompilerParams(vmem_limit_bytes=16 * 1024 * 1024),
        cost_estimate=pl.CostEstimate(
            flops=0, bytes_accessed=owners * chunk * width * 4, transcendentals=0
        ),
        name="place",
    )(scal, *blocks, *(outs if aliased else ()))


def shards(queries, layer_keys_input, layer_values_input, attn_out, grad_out, log_norm, window):
    tok_local = queries.shape[1]
    kv_local = layer_keys_input.shape[2] // HEAD_SIZE
    group = queries.shape[2] // layer_keys_input.shape[2]
    owners = lax.axis_size("head")
    shard = lax.axis_index("ctx")
    scal = jnp.concatenate(
        [
            jnp.stack([lax.axis_index("head"), (shard == 0).astype(jnp.int32)]).astype(jnp.int32),
            window.astype(jnp.int32),
        ]
    )
    pieces = []
    for layer in range(SLIDING_LAYERS):
        kv_first = 0
        while kv_first < kv_local:
            kv_count = 1 if layer == 0 and kv_first < 2 else min(2, kv_local - kv_first)
            pieces.append((layer, kv_first, kv_count))
            kv_first += kv_count

    plans = [[(0, 0, 1)], [(0, 1, kv_local - 1)], [(1, 0, kv_local)]]
    packed = pack_call(plans[0], layer_keys_input, layer_values_input)
    packed += pack_call(plans[1] + plans[2], layer_keys_input, layer_values_input)
    halos = [shifted(block, "ctx", 1) for block in packed]

    def halo_of(layer, kv_first):
        if layer == 1:
            return halos[2], kv_first
        return (halos[0], 0) if kv_first == 0 else (halos[1], kv_first - 1)

    outs = None
    waiting = None
    after = scal
    sent = []

    def send(plan, bufs):
        blocks = [bufs[0]] + [swapped(bufs[flip], "head", flip) for flip in range(1, owners)]
        sent.append((plan, blocks))

    for index, piece in enumerate(pieces):
        layer, kv_first, kv_count = piece
        halo, column = halo_of(layer, kv_first)
        extra = 0 if waiting is None else 2 * waiting[0][2]
        bufs, back, part = band_call(
            piece,
            extra,
            owners,
            scal,
            queries,
            grad_out,
            attn_out,
            log_norm,
            layer_keys_input,
            layer_values_input,
            halo,
            column,
            after,
        )
        after = part
        back = shifted(back, "ctx", -1)
        plan = [(0, piece)]
        if waiting is not None:
            old, old_part, old_back = waiting
            before = sent[-1][1][1:]
            bufs = finish_call(
                old[2], owners, kv_count * group * HEAD_SIZE, scal, old_part, old_back, bufs, before
            )
            after = bufs[0]
            plan += [(1, old), (2, old)]
        send(plan, bufs)
        waiting = (piece, part, back)
    old, old_part, old_back = waiting
    bufs = finish_call(old[2], owners, 0, scal, old_part, old_back, None, ())
    send([(1, old), (2, old)], bufs)
    for plan, blocks in sent:
        outs = place_call(plan, owners, group, kv_local, scal, blocks, outs)
    return tuple(outs)


def solution(mesh):
    in_specs = (
        P(None, "ctx", "head"),
        P(None, "ctx", "head"),
        P(None, "ctx", "head"),
        P(None, "ctx", "head"),
        P(None, "ctx", "head"),
        P(None, "head", "ctx"),
        P(),
    )
    out_specs = (
        P(None, ("ctx", "head"), None),
        P(None, ("ctx", "head"), None),
        P(None, ("ctx", "head"), None),
    )
    return jax.shard_map(shards, mesh=mesh, in_specs=in_specs, out_specs=out_specs, check_vma=False)
```

```python
import functools
import math

import jax
import jax.numpy as jnp
from jax import lax
from jax.experimental import pallas as pl
from jax.experimental.pallas import tpu as pltpu
from jax.sharding import PartitionSpec as P

HEAD_SIZE = 128
WINDOW_LENGTH = 1024
QUERY_PRE = 168
SLIDING_LAYERS = 2
TILE = 128
SCALE = QUERY_PRE ** (-0.5)
LOG2E = math.log2(math.e)
FAR = 1e30
VMEM_LIMIT = 60 * 1024 * 1024

NT = (((1,), (1,)), ((), ()))
NN = (((1,), (0,)), ((), ()))


def dot(a, b, dims=NN):
    return lax.dot_general(a, b, dims, preferred_element_type=jnp.float32)


def shifted(value, axis, steps):
    count = lax.axis_size(axis)
    first, last = (max(0, -steps), min(count, count - steps))
    return lax.ppermute(value, axis, [(source, source + steps) for source in range(first, last)])


def swapped(value, axis, flip):
    count = lax.axis_size(axis)
    return lax.ppermute(value, axis, [(source, source ^ flip) for source in range(count)])


def pack_kernel(plan, rows, *rest):
    count = len(plan)
    keys, values = rest[:2]
    outs = rest[2 : 2 + count]
    scrs = rest[2 + count : 2 + 2 * count]
    in_sems, out_sems = rest[2 + 2 * count :]
    loads = []
    for index, (layer, kv_first, kv_count) in enumerate(plan):
        width = kv_count * HEAD_SIZE
        for kind, array in enumerate((keys, values)):
            loads.append(
                pltpu.make_async_copy(
                    array.at[layer, rows, pl.ds(kv_first * HEAD_SIZE, width)],
                    scrs[index].at[:, pl.ds(kind * width, width)],
                    in_sems.at[index, kind],
                )
            )
    for load in loads:
        load.start()
    stores = []
    for index in range(count):
        loads[2 * index].wait()
        loads[2 * index + 1].wait()
        store = pltpu.make_async_copy(scrs[index], outs[index], out_sems.at[index])
        store.start()
        stores.append(store)
    for store in stores:
        store.wait()


def pack_call(plan, keys, values):
    tok_local = keys.shape[1]
    any_spec = pl.BlockSpec(memory_space=pl.ANY)
    sizes = [(WINDOW_LENGTH, 2 * kv_count * HEAD_SIZE) for _, _, kv_count in plan]
    return pl.pallas_call(
        functools.partial(pack_kernel, plan, pl.ds(tok_local - WINDOW_LENGTH, WINDOW_LENGTH)),
        in_specs=[any_spec] * 2,
        out_specs=[any_spec] * len(plan),
        out_shape=[jax.ShapeDtypeStruct(size, jnp.bfloat16) for size in sizes],
        scratch_shapes=[pltpu.VMEM(size, jnp.bfloat16) for size in sizes]
        + [pltpu.SemaphoreType.DMA((len(plan), 2)), pltpu.SemaphoreType.DMA((len(plan),))],
        compiler_params=pltpu.CompilerParams(vmem_limit_bytes=VMEM_LIMIT),
        cost_estimate=pl.CostEstimate(
            flops=0, bytes_accessed=4 * sum(size[0] * size[1] for size in sizes), transcendentals=0
        ),
        name="pack",
    )(keys, values)


def band_kernel(
    layer,
    kv_first,
    kv_count,
    owners,
    scal,
    q_ref,
    do_ref,
    out_ref,
    lse_ref,
    k_ref,
    v_ref,
    k_halo,
    v_halo,
    after,
    *rest,
):
    dq_bufs = rest[:owners]
    back_ref, part_ref, kt, acc, lse2_scr, dq_scr, sems = rest[owners:]
    tok_local = q_ref.shape[1]
    group = q_ref.shape[2] // HEAD_SIZE
    chunk = tok_local // owners
    step = pl.program_id(0)
    me = scal[0]
    first_shard = scal[1]
    win = scal[2 + layer]
    wide = group * TILE

    head = (kv_first + step) * group
    for h in range(group):
        lse2_scr[h : h + 1, :] = lse_ref[0, pl.ds(head + h, 1), :] * LOG2E

    rows = lax.broadcasted_iota(jnp.int32, (TILE, wide), 0)
    lanes = lax.broadcasted_iota(jnp.int32, (1, wide), 1) % TILE
    left = lax.broadcasted_iota(jnp.int32, (1, HEAD_SIZE), 1) < HEAD_SIZE // 2

    def stacked(ref, start):
        block = ref[0, start : start + TILE, :]
        return jnp.concatenate(
            [block[:, h * HEAD_SIZE : (h + 1) * HEAD_SIZE] for h in range(group)], 0
        )

    def span_of(halo, own, low, high):
        pieces = []
        if low < WINDOW_LENGTH:
            pieces.append(halo[low : min(high, WINDOW_LENGTH), :])
        if high > WINDOW_LENGTH:
            pieces.append(own[0, max(low, WINDOW_LENGTH) - WINDOW_LENGTH : high - WINDOW_LENGTH, :])
        return jnp.concatenate(pieces, 0) if len(pieces) > 1 else pieces[0]

    def sweep(reach):
        tiles = reach // TILE + 1
        skipped = WINDOW_LENGTH - reach
        units = tok_local // TILE
        reached = {"keys": skipped, "touched": skipped, "flushed": skipped}
        minus = jnp.full((tiles * TILE, HEAD_SIZE), -1, jnp.bfloat16)
        if skipped:
            back_ref[0:skipped, :] = jnp.zeros((skipped, 2 * HEAD_SIZE), jnp.bfloat16)

        def transpose_to(high):
            low = reached["keys"]
            if high > low:
                kt[:, low:high] = span_of(k_halo, k_ref, low, high).T
                reached["keys"] = high

        def products(unit):
            begin = unit * TILE
            low = begin + skipped
            high = low + tiles * TILE
            q2 = stacked(q_ref, begin)
            do2 = stacked(do_ref, begin)
            prod = do2.astype(jnp.float32) * stacked(out_ref, begin).astype(jnp.float32)
            pair = prod + pltpu.roll(prod, HEAD_SIZE // 2, 1)
            coarse = pair.astype(jnp.bfloat16).astype(jnp.float32)
            terms = jnp.where(left, coarse, pair - coarse).astype(jnp.bfloat16)
            scores = dot(span_of(k_halo, k_ref, low, high), q2, NT)
            lead = jnp.concatenate([span_of(v_halo, v_ref, low, high), minus], 1)
            excess = dot(lead, jnp.concatenate([do2, terms], 1), NT)
            transpose_to(high)
            lse2 = jnp.concatenate(
                [lse2_scr[h : h + 1, begin : begin + TILE] for h in range(group)], 1
            )
            return begin, q2, do2, scores, excess, lse2

        def weights(begin, q2, do2, scores, excess, lse2):
            probs, grads = [], []
            away = jnp.where(first_shard == 1, FAR, lse2)
            for tile in range(tiles):
                part = slice(tile * TILE, (tile + 1) * TILE)
                line = away if begin + skipped + tile * TILE < WINDOW_LENGTH else lse2
                prob = jnp.exp2(scores[part] * (SCALE * LOG2E) - line)
                if tile == tiles - 1:
                    prob = jnp.where(rows <= lanes, prob, 0.0)
                elif tile < 3:
                    prob = jnp.where(rows > lanes + (reach - win - tile * TILE), prob, 0.0)
                probs.append(prob.astype(jnp.bfloat16))
                grads.append((prob * excess[part]).astype(jnp.bfloat16))
            return begin, q2, do2, probs, grads

        def add_rows(low, value, side):
            high = low + value.shape[0]
            edge = min(max(reached["touched"], low), high)
            if edge > low:
                acc[low:edge, side] += value[: edge - low]
            if edge < high:
                acc[edge:high, side] = value[edge - low :]

        def flush(high):
            low = reached["flushed"]
            edge = min(max(WINDOW_LENGTH, low), high)
            if edge > low:
                back_ref[low:edge, :HEAD_SIZE] = (acc[low:edge, :HEAD_SIZE] * SCALE).astype(jnp.bfloat16)
                back_ref[low:edge, HEAD_SIZE:] = acc[low:edge, HEAD_SIZE:].astype(jnp.bfloat16)
            if edge < high:
                place = slice(edge - WINDOW_LENGTH, high - WINDOW_LENGTH)
                part_ref[place, :HEAD_SIZE] = acc[edge:high, :HEAD_SIZE] * SCALE
                part_ref[place, HEAD_SIZE:] = acc[edge:high, HEAD_SIZE:]
            reached["flushed"] = high

        def finish(first, second):
            base = first[0] + skipped
            for lefts, rights, kind in ((3, 2, 1), (4, 1, 0)):
                one, two = first[lefts], second[lefts]
                side = slice(kind * HEAD_SIZE, (kind + 1) * HEAD_SIZE)
                middle = jnp.concatenate(
                    [jnp.concatenate(one[1:], 0), jnp.concatenate(two[:-1], 0)], 1
                )
                both = jnp.concatenate([first[rights], second[rights]], 0)
                add_rows(base, dot(one[0], first[rights]), side)
                add_rows(base + TILE, dot(middle, both), side)
                add_rows(base + tiles * TILE, dot(two[-1], second[rights]), side)
            reached["touched"] = base + (tiles + 1) * TILE
            for begin, _, _, _, grads in (first, second):
                keys_t = kt[:, begin + skipped : begin + skipped + tiles * TILE]
                dq = (dot(keys_t, jnp.concatenate(grads, 0)).T * SCALE).astype(jnp.bfloat16)
                for h in range(group):
                    dq_scr[step, begin : begin + TILE, h * HEAD_SIZE : (h + 1) * HEAD_SIZE] = dq[
                        h * TILE : (h + 1) * TILE
                    ]

        held = products(0)
        done = []
        for unit in range(units):
            coming = products(unit + 1) if unit + 1 < units else None
            done.append(weights(*held))
            held = coming
            if unit % 2 == 1:
                finish(done[unit - 1], done[unit])
                flush((unit + 1) * TILE + skipped)
        flush(WINDOW_LENGTH + tok_local)

    low = 0
    for reach in (WINDOW_LENGTH * 3 // 4, WINDOW_LENGTH):

        @pl.when(jnp.logical_and(win > low, win <= reach))
        def _(reach=reach):
            sweep(reach)

        low = reach

    def copies(index):
        result = []
        for flip in range(owners):
            owner = jnp.bitwise_xor(me, flip)
            source = dq_scr.at[index, pl.ds(pl.multiple_of(owner * chunk, chunk), chunk), :]
            target = dq_bufs[flip].at[:, pl.ds(index * group * HEAD_SIZE, group * HEAD_SIZE)]
            result.append(pltpu.make_async_copy(source, target, sems.at[index, flip]))
        return result

    for index in range(kv_count):

        @pl.when(step == index)
        def _(index=index):
            for copy in copies(index):
                copy.start()

    @pl.when(step == kv_count - 1)
    def _():
        for index in range(kv_count):
            for copy in copies(index):
                copy.wait()


def band_call(piece, extra, owners, scal, queries, grad_out, attn_out, log_norm, keys, values, halo, column, after):
    layer, kv_first, kv_count = piece
    tok_local = queries.shape[1]
    group = queries.shape[2] // keys.shape[2]
    span = WINDOW_LENGTH + tok_local
    chunk = tok_local // owners
    halo_kv = halo.shape[1] // (2 * HEAD_SIZE)
    q_spec = pl.BlockSpec((1, tok_local, group * HEAD_SIZE), lambda g: (layer, 0, kv_first + g))
    kv_spec = pl.BlockSpec((1, tok_local, HEAD_SIZE), lambda g: (layer, 0, kv_first + g))
    pairs = tok_local * (WINDOW_LENGTH + 2 * TILE) * group * kv_count
    outs = pl.pallas_call(
        functools.partial(band_kernel, layer, kv_first, kv_count, owners),
        grid=(kv_count,),
        in_specs=[
            pl.BlockSpec(memory_space=pltpu.SMEM),
            q_spec,
            q_spec,
            q_spec,
            pl.BlockSpec((1,) + log_norm.shape[1:], lambda g: (layer, 0, 0)),
            kv_spec,
            kv_spec,
            pl.BlockSpec((WINDOW_LENGTH, HEAD_SIZE), lambda g: (0, column + g)),
            pl.BlockSpec((WINDOW_LENGTH, HEAD_SIZE), lambda g: (0, halo_kv + column + g)),
            pl.BlockSpec(memory_space=pl.ANY),
        ],
        out_specs=[pl.BlockSpec(memory_space=pl.ANY)] * owners
        + [
            pl.BlockSpec((WINDOW_LENGTH, 2 * HEAD_SIZE), lambda g: (0, g)),
            pl.BlockSpec((tok_local, 2 * HEAD_SIZE), lambda g: (0, g)),
        ],
        out_shape=[
            jax.ShapeDtypeStruct((chunk, (kv_count * group + extra) * HEAD_SIZE), jnp.bfloat16)
        ]
        * owners
        + [
            jax.ShapeDtypeStruct((WINDOW_LENGTH, kv_count * 2 * HEAD_SIZE), jnp.bfloat16),
            jax.ShapeDtypeStruct((tok_local, kv_count * 2 * HEAD_SIZE), jnp.float32),
        ],
        scratch_shapes=[
            pltpu.VMEM((HEAD_SIZE, span), jnp.bfloat16),
            pltpu.VMEM((span, 2 * HEAD_SIZE), jnp.float32),
            pltpu.VMEM((8, tok_local), jnp.float32),
            pltpu.VMEM((kv_count, tok_local, group * HEAD_SIZE), jnp.bfloat16),
            pltpu.SemaphoreType.DMA((kv_count, owners)),
        ],
        compiler_params=pltpu.CompilerParams(vmem_limit_bytes=VMEM_LIMIT),
        cost_estimate=pl.CostEstimate(
            flops=pairs * 2 * HEAD_SIZE * 5 * 4,
            bytes_accessed=8 * tok_local * group * kv_count * HEAD_SIZE,
            transcendentals=pairs,
        ),
        name="band",
    )(scal, queries, grad_out, attn_out, log_norm, keys, values, halo, halo, after)
    return outs[:owners], outs[owners], outs[owners + 1]


def finish_kernel(kv_count, owners, column, skip, scal, part_ref, back_ref, *rest):
    bufs = rest[skip:][:owners]
    scr, sems = rest[-2:]
    tok_local = part_ref.shape[0]
    chunk = tok_local // owners
    step = pl.program_id(0)
    me = scal[0]
    plain = tok_local - WINDOW_LENGTH
    scr[step, :plain] = part_ref[:plain].astype(jnp.bfloat16)
    scr[step, plain:] = (part_ref[plain:] + back_ref[...].astype(jnp.float32)).astype(jnp.bfloat16)

    def copies(index):
        result = []
        for flip in range(owners):
            owner = jnp.bitwise_xor(me, flip)
            rows = pl.ds(pl.multiple_of(owner * chunk, chunk), chunk)
            for kind in range(2):
                place = column + (kind * kv_count + index) * HEAD_SIZE
                result.append(
                    pltpu.make_async_copy(
                        scr.at[index, rows, pl.ds(kind * HEAD_SIZE, HEAD_SIZE)],
                        bufs[flip].at[:, pl.ds(place, HEAD_SIZE)],
                        sems.at[index, flip, kind],
                    )
                )
        return result

    for index in range(kv_count):

        @pl.when(step == index)
        def _(index=index):
            for copy in copies(index):
                copy.start()

    @pl.when(step == kv_count - 1)
    def _():
        for index in range(kv_count):
            for copy in copies(index):
                copy.wait()


def finish_call(kv_count, owners, column, scal, part, back, bufs, after):
    tok_local = part.shape[0]
    chunk = tok_local // owners
    aliased = bufs is not None
    shape = jax.ShapeDtypeStruct((chunk, column + kv_count * 2 * HEAD_SIZE), jnp.bfloat16)
    any_spec = pl.BlockSpec(memory_space=pl.ANY)
    return pl.pallas_call(
        functools.partial(
            finish_kernel, kv_count, owners, column, len(after) + (owners if aliased else 0)
        ),
        grid=(kv_count,),
        in_specs=[
            pl.BlockSpec(memory_space=pltpu.SMEM),
            pl.BlockSpec((tok_local, 2 * HEAD_SIZE), lambda g: (0, g)),
            pl.BlockSpec((WINDOW_LENGTH, 2 * HEAD_SIZE), lambda g: (0, g)),
        ]
        + [any_spec] * ((owners if aliased else 0) + len(after)),
        out_specs=[any_spec] * owners,
        out_shape=[shape] * owners,
        input_output_aliases={3 + i: i for i in range(owners)} if aliased else {},
        scratch_shapes=[
            pltpu.VMEM((kv_count, tok_local, 2 * HEAD_SIZE), jnp.bfloat16),
            pltpu.SemaphoreType.DMA((kv_count, owners, 2)),
        ],
        compiler_params=pltpu.CompilerParams(vmem_limit_bytes=VMEM_LIMIT),
        cost_estimate=pl.CostEstimate(
            flops=0, bytes_accessed=16 * tok_local * kv_count * HEAD_SIZE, transcendentals=0
        ),
        name="finish",
    )(scal, part, back, *(bufs if aliased else ()), *after)


def place_kernel(plan, owners, group, kv_local, aliased, scal, *rest):
    blocks = rest[:owners]
    outs = rest[owners + (3 if aliased else 0) :][:3]
    scr, in_sems, out_sems = rest[-3:]
    me = scal[0]
    loads = [
        pltpu.make_async_copy(blocks[flip], scr.at[flip], in_sems.at[flip])
        for flip in range(owners)
    ]
    for load in loads:
        load.start()
    stores = []
    for flip in range(owners):
        loads[flip].wait()
        source = jnp.bitwise_xor(me, flip)
        column = 0
        for which, (layer, kv_first, kv_count) in plan:
            heads = kv_count * group if which == 0 else kv_count
            home = kv_local * group if which == 0 else kv_local
            first = kv_first * group if which == 0 else kv_first
            place = pl.multiple_of((source * home + first) * HEAD_SIZE, HEAD_SIZE)
            store = pltpu.make_async_copy(
                scr.at[flip, :, pl.ds(column, heads * HEAD_SIZE)],
                outs[which].at[layer, :, pl.ds(place, heads * HEAD_SIZE)],
                out_sems.at[len(stores)],
            )
            store.start()
            stores.append(store)
            column += heads * HEAD_SIZE
    for store in stores:
        store.wait()


def place_call(plan, owners, group, kv_local, scal, blocks, outs):
    chunk, width = blocks[0].shape
    aliased = outs is not None
    any_spec = pl.BlockSpec(memory_space=pl.ANY)
    shapes = [
        jax.ShapeDtypeStruct(
            (SLIDING_LAYERS, chunk, owners * heads * HEAD_SIZE), jnp.bfloat16
        )
        for heads in (kv_local * group, kv_local, kv_local)
    ]
    return pl.pallas_call(
        functools.partial(place_kernel, plan, owners, group, kv_local, aliased),
        in_specs=[pl.BlockSpec(memory_space=pltpu.SMEM)]
        + [any_spec] * (owners + (3 if aliased else 0)),
        out_specs=[any_spec] * 3,
        out_shape=shapes,
        input_output_aliases={1 + owners + i: i for i in range(3)} if aliased else {},
        scratch_shapes=[
            pltpu.VMEM((owners, chunk, width), jnp.bfloat16),
            pltpu.SemaphoreType.DMA((owners,)),
            pltpu.SemaphoreType.DMA((owners * len(plan),)),
        ],
        compiler_params=pltpu.CompilerParams(vmem_limit_bytes=VMEM_LIMIT),
        cost_estimate=pl.CostEstimate(
            flops=0, bytes_accessed=owners * chunk * width * 4, transcendentals=0
        ),
        name="place",
    )(scal, *blocks, *(outs if aliased else ()))


def shards(queries, layer_keys_input, layer_values_input, attn_out, grad_out, log_norm, window):
    tok_local = queries.shape[1]
    kv_local = layer_keys_input.shape[2] // HEAD_SIZE
    group = queries.shape[2] // layer_keys_input.shape[2]
    owners = lax.axis_size("head")
    shard = lax.axis_index("ctx")
    scal = jnp.concatenate(
        [
            jnp.stack([lax.axis_index("head"), (shard == 0).astype(jnp.int32)]).astype(jnp.int32),
            window.astype(jnp.int32),
        ]
    )
    pieces = []
    for layer in range(SLIDING_LAYERS):
        kv_first = 0
        while kv_first < kv_local:
            kv_count = 1 if layer == 0 and kv_first < 2 else min(2, kv_local - kv_first)
            pieces.append((layer, kv_first, kv_count))
            kv_first += kv_count

    plans = [[(0, 0, 1)], [(0, 1, kv_local - 1)], [(1, 0, kv_local)]]
    packed = pack_call(plans[0], layer_keys_input, layer_values_input)
    packed += pack_call(plans[1] + plans[2], layer_keys_input, layer_values_input)
    halos = [shifted(block, "ctx", 1) for block in packed]

    def halo_of(layer, kv_first):
        if layer == 1:
            return halos[2], kv_first
        return (halos[0], 0) if kv_first == 0 else (halos[1], kv_first - 1)

    outs = None
    waiting = None
    after = scal
    sent = []

    def send(plan, bufs):
        blocks = [bufs[0]] + [swapped(bufs[flip], "head", flip) for flip in range(1, owners)]
        sent.append((plan, blocks))

    for index, piece in enumerate(pieces):
        layer, kv_first, kv_count = piece
        halo, column = halo_of(layer, kv_first)
        extra = 0 if waiting is None else 2 * waiting[0][2]
        bufs, back, part = band_call(
            piece,
            extra,
            owners,
            scal,
            queries,
            grad_out,
            attn_out,
            log_norm,
            layer_keys_input,
            layer_values_input,
            halo,
            column,
            after,
        )
        after = part
        back = shifted(back, "ctx", -1)
        plan = [(0, piece)]
        if waiting is not None:
            old, old_part, old_back = waiting
            before = sent[-1][1][1:]
            bufs = finish_call(
                old[2], owners, kv_count * group * HEAD_SIZE, scal, old_part, old_back, bufs, before
            )
            after = bufs[0]
            plan += [(1, old), (2, old)]
        send(plan, bufs)
        waiting = (piece, part, back)
    old, old_part, old_back = waiting
    bufs = finish_call(old[2], owners, 0, scal, old_part, old_back, None, ())
    send([(1, old), (2, old)], bufs)
    for plan, blocks in sent:
        outs = place_call(plan, owners, group, kv_local, scal, blocks, outs)
    return tuple(outs)


def solution(mesh):
    in_specs = (
        P(None, "ctx", "head"),
        P(None, "ctx", "head"),
        P(None, "ctx", "head"),
        P(None, "ctx", "head"),
        P(None, "ctx", "head"),
        P(None, "head", "ctx"),
        P(),
    )
    out_specs = (
        P(None, ("ctx", "head"), None),
        P(None, ("ctx", "head"), None),
        P(None, ("ctx", "head"), None),
    )
    return jax.shard_map(shards, mesh=mesh, in_specs=in_specs, out_specs=out_specs, check_vma=False)
```

```python
import functools
import math

import jax
import jax.numpy as jnp
from jax import lax
from jax.experimental import pallas as pl
from jax.experimental.pallas import tpu as pltpu
from jax.sharding import PartitionSpec as P

HEAD_SIZE = 128
WINDOW_LENGTH = 1024
QUERY_PRE = 168
SLIDING_LAYERS = 2
TILE = 128
SCALE = QUERY_PRE ** (-0.5)
LOG2E = math.log2(math.e)
FAR = 1e30
MIB = 1024 * 1024

NT = (((1,), (1,)), ((), ()))
NN = (((1,), (0,)), ((), ()))


def dot(a, b, dims=NN):
    return lax.dot_general(a, b, dims, preferred_element_type=jnp.float32)


def shifted(value, axis, steps):
    count = lax.axis_size(axis)
    first, last = (max(0, -steps), min(count, count - steps))
    return lax.ppermute(value, axis, [(source, source + steps) for source in range(first, last)])


def swapped(value, axis, flip):
    count = lax.axis_size(axis)
    return lax.ppermute(value, axis, [(source, source ^ flip) for source in range(count)])


def pack_kernel(plan, rows, *rest):
    count = len(plan)
    keys, values = rest[:2]
    outs = rest[2 : 2 + count]
    scrs = rest[2 + count : 2 + 2 * count]
    in_sems, out_sems = rest[2 + 2 * count :]
    loads = []
    for index, (layer, kv_first, kv_count) in enumerate(plan):
        width = kv_count * HEAD_SIZE
        for kind, array in enumerate((keys, values)):
            loads.append(
                pltpu.make_async_copy(
                    array.at[layer, rows, pl.ds(kv_first * HEAD_SIZE, width)],
                    scrs[index].at[:, pl.ds(kind * width, width)],
                    in_sems.at[index, kind],
                )
            )
    for load in loads:
        load.start()
    stores = []
    for index in range(count):
        loads[2 * index].wait()
        loads[2 * index + 1].wait()
        store = pltpu.make_async_copy(scrs[index], outs[index], out_sems.at[index])
        store.start()
        stores.append(store)
    for store in stores:
        store.wait()


def pack_call(plan, keys, values):
    tok_local = keys.shape[1]
    any_spec = pl.BlockSpec(memory_space=pl.ANY)
    sizes = [(WINDOW_LENGTH, 2 * kv_count * HEAD_SIZE) for _, _, kv_count in plan]
    return pl.pallas_call(
        functools.partial(pack_kernel, plan, pl.ds(tok_local - WINDOW_LENGTH, WINDOW_LENGTH)),
        in_specs=[any_spec] * 2,
        out_specs=[any_spec] * len(plan),
        out_shape=[jax.ShapeDtypeStruct(size, jnp.bfloat16) for size in sizes],
        scratch_shapes=[pltpu.VMEM(size, jnp.bfloat16) for size in sizes]
        + [pltpu.SemaphoreType.DMA((len(plan), 2)), pltpu.SemaphoreType.DMA((len(plan),))],
        compiler_params=pltpu.CompilerParams(vmem_limit_bytes=60 * MIB),
        cost_estimate=pl.CostEstimate(
            flops=0, bytes_accessed=4 * sum(size[0] * size[1] for size in sizes), transcendentals=0
        ),
        name="pack",
    )(keys, values)


def band_kernel(
    layer,
    kv_first,
    kv_count,
    owners,
    scal,
    q_ref,
    do_ref,
    out_ref,
    lse_ref,
    k_ref,
    v_ref,
    k_halo,
    v_halo,
    after,
    *rest,
):
    dq_bufs = rest[:owners]
    back_ref, part_ref, kt, acc, lse2_scr, dq_scr, sems = rest[owners:]
    tok_local = q_ref.shape[1]
    group = q_ref.shape[2] // HEAD_SIZE
    chunk = tok_local // owners
    step = pl.program_id(0)
    me = scal[0]
    first_shard = scal[1]
    win = scal[2 + layer]
    wide = group * TILE

    head = (kv_first + step) * group
    for h in range(group):
        lse2_scr[h : h + 1, :] = lse_ref[0, pl.ds(head + h, 1), :] * LOG2E

    rows = lax.broadcasted_iota(jnp.int32, (TILE, wide), 0)
    lanes = lax.broadcasted_iota(jnp.int32, (1, wide), 1) % TILE
    left = lax.broadcasted_iota(jnp.int32, (1, HEAD_SIZE), 1) < HEAD_SIZE // 2

    def stacked(ref, start):
        block = ref[0, start : start + TILE, :]
        return jnp.concatenate(
            [block[:, h * HEAD_SIZE : (h + 1) * HEAD_SIZE] for h in range(group)], 0
        )

    def span_of(halo, own, low, high):
        pieces = []
        if low < WINDOW_LENGTH:
            pieces.append(halo[low : min(high, WINDOW_LENGTH), :])
        if high > WINDOW_LENGTH:
            pieces.append(own[0, max(low, WINDOW_LENGTH) - WINDOW_LENGTH : high - WINDOW_LENGTH, :])
        return jnp.concatenate(pieces, 0) if len(pieces) > 1 else pieces[0]

    def sweep(reach):
        tiles = reach // TILE + 1
        skipped = WINDOW_LENGTH - reach
        units = tok_local // TILE
        reached = {"keys": skipped, "touched": skipped, "flushed": skipped}
        minus = jnp.full((tiles * TILE, HEAD_SIZE), -1, jnp.bfloat16)
        if skipped:
            back_ref[0:skipped, :] = jnp.zeros((skipped, 2 * HEAD_SIZE), jnp.bfloat16)

        def transpose_to(high):
            low = reached["keys"]
            if high > low:
                kt[:, low:high] = span_of(k_halo, k_ref, low, high).T
                reached["keys"] = high

        def products(unit):
            begin = unit * TILE
            low = begin + skipped
            high = low + tiles * TILE
            q2 = stacked(q_ref, begin)
            do2 = stacked(do_ref, begin)
            prod = do2.astype(jnp.float32) * stacked(out_ref, begin).astype(jnp.float32)
            pair = prod + pltpu.roll(prod, HEAD_SIZE // 2, 1)
            coarse = pair.astype(jnp.bfloat16).astype(jnp.float32)
            terms = jnp.where(left, coarse, pair - coarse).astype(jnp.bfloat16)
            scores = dot(span_of(k_halo, k_ref, low, high), q2, NT)
            lead = jnp.concatenate([span_of(v_halo, v_ref, low, high), minus], 1)
            excess = dot(lead, jnp.concatenate([do2, terms], 1), NT)
            transpose_to(high)
            lse2 = jnp.concatenate(
                [lse2_scr[h : h + 1, begin : begin + TILE] for h in range(group)], 1
            )
            return begin, q2, do2, scores, excess, lse2

        def weights(begin, q2, do2, scores, excess, lse2):
            probs, grads = [], []
            away = jnp.where(first_shard == 1, FAR, lse2)
            for tile in range(tiles):
                part = slice(tile * TILE, (tile + 1) * TILE)
                line = away if begin + skipped + tile * TILE < WINDOW_LENGTH else lse2
                prob = jnp.exp2(scores[part] * (SCALE * LOG2E) - line)
                if tile == tiles - 1:
                    prob = jnp.where(rows <= lanes, prob, 0.0)
                elif tile < 3:
                    prob = jnp.where(rows > lanes + (reach - win - tile * TILE), prob, 0.0)
                probs.append(prob.astype(jnp.bfloat16))
                grads.append((prob * excess[part]).astype(jnp.bfloat16))
            return begin, q2, do2, probs, grads

        def add_rows(low, value, side):
            high = low + value.shape[0]
            edge = min(max(reached["touched"], low), high)
            if edge > low:
                acc[low:edge, side] += value[: edge - low]
            if edge < high:
                acc[edge:high, side] = value[edge - low :]

        def flush(high):
            low = reached["flushed"]
            edge = min(max(WINDOW_LENGTH, low), high)
            if edge > low:
                back_ref[low:edge, :HEAD_SIZE] = (acc[low:edge, :HEAD_SIZE] * SCALE).astype(jnp.bfloat16)
                back_ref[low:edge, HEAD_SIZE:] = acc[low:edge, HEAD_SIZE:].astype(jnp.bfloat16)
            if edge < high:
                place = slice(edge - WINDOW_LENGTH, high - WINDOW_LENGTH)
                part_ref[place, :HEAD_SIZE] = acc[edge:high, :HEAD_SIZE] * SCALE
                part_ref[place, HEAD_SIZE:] = acc[edge:high, HEAD_SIZE:]
            reached["flushed"] = high

        def finish(first, second):
            base = first[0] + skipped
            for lefts, rights, kind in ((3, 2, 1), (4, 1, 0)):
                one, two = first[lefts], second[lefts]
                side = slice(kind * HEAD_SIZE, (kind + 1) * HEAD_SIZE)
                middle = jnp.concatenate(
                    [jnp.concatenate(one[1:], 0), jnp.concatenate(two[:-1], 0)], 1
                )
                both = jnp.concatenate([first[rights], second[rights]], 0)
                add_rows(base, dot(one[0], first[rights]), side)
                add_rows(base + TILE, dot(middle, both), side)
                add_rows(base + tiles * TILE, dot(two[-1], second[rights]), side)
            reached["touched"] = base + (tiles + 1) * TILE
            for begin, _, _, _, grads in (first, second):
                keys_t = kt[:, begin + skipped : begin + skipped + tiles * TILE]
                dq = (dot(keys_t, jnp.concatenate(grads, 0)).T * SCALE).astype(jnp.bfloat16)
                for h in range(group):
                    dq_scr[step, begin : begin + TILE, h * HEAD_SIZE : (h + 1) * HEAD_SIZE] = dq[
                        h * TILE : (h + 1) * TILE
                    ]

        held = products(0)
        done = []
        for unit in range(units):
            coming = products(unit + 1) if unit + 1 < units else None
            done.append(weights(*held))
            held = coming
            if unit % 2 == 1:
                finish(done[unit - 1], done[unit])
                flush((unit + 1) * TILE + skipped)
        flush(WINDOW_LENGTH + tok_local)

    low = 0
    for reach in (WINDOW_LENGTH * 3 // 4, WINDOW_LENGTH):

        @pl.when(jnp.logical_and(win > low, win <= reach))
        def _(reach=reach):
            sweep(reach)

        low = reach

    def copies(index):
        result = []
        for flip in range(owners):
            owner = jnp.bitwise_xor(me, flip)
            source = dq_scr.at[index, pl.ds(pl.multiple_of(owner * chunk, chunk), chunk), :]
            target = dq_bufs[flip].at[:, pl.ds(index * group * HEAD_SIZE, group * HEAD_SIZE)]
            result.append(pltpu.make_async_copy(source, target, sems.at[index, flip]))
        return result

    for index in range(kv_count):

        @pl.when(step == index)
        def _(index=index):
            for copy in copies(index):
                copy.start()

    @pl.when(step == kv_count - 1)
    def _():
        for index in range(kv_count):
            for copy in copies(index):
                copy.wait()


def band_call(piece, extra, owners, scal, queries, grad_out, attn_out, log_norm, keys, values, halo, column, after):
    layer, kv_first, kv_count = piece
    tok_local = queries.shape[1]
    group = queries.shape[2] // keys.shape[2]
    span = WINDOW_LENGTH + tok_local
    chunk = tok_local // owners
    halo_kv = halo.shape[1] // (2 * HEAD_SIZE)
    q_spec = pl.BlockSpec((1, tok_local, group * HEAD_SIZE), lambda g: (layer, 0, kv_first + g))
    kv_spec = pl.BlockSpec((1, tok_local, HEAD_SIZE), lambda g: (layer, 0, kv_first + g))
    pairs = tok_local * (WINDOW_LENGTH + 2 * TILE) * group * kv_count
    outs = pl.pallas_call(
        functools.partial(band_kernel, layer, kv_first, kv_count, owners),
        grid=(kv_count,),
        in_specs=[
            pl.BlockSpec(memory_space=pltpu.SMEM),
            q_spec,
            q_spec,
            q_spec,
            pl.BlockSpec((1,) + log_norm.shape[1:], lambda g: (layer, 0, 0)),
            kv_spec,
            kv_spec,
            pl.BlockSpec((WINDOW_LENGTH, HEAD_SIZE), lambda g: (0, column + g)),
            pl.BlockSpec((WINDOW_LENGTH, HEAD_SIZE), lambda g: (0, halo_kv + column + g)),
            pl.BlockSpec(memory_space=pl.ANY),
        ],
        out_specs=[pl.BlockSpec(memory_space=pl.ANY)] * owners
        + [
            pl.BlockSpec((WINDOW_LENGTH, 2 * HEAD_SIZE), lambda g: (0, g)),
            pl.BlockSpec((tok_local, 2 * HEAD_SIZE), lambda g: (0, g)),
        ],
        out_shape=[
            jax.ShapeDtypeStruct((chunk, (kv_count * group + extra) * HEAD_SIZE), jnp.bfloat16)
        ]
        * owners
        + [
            jax.ShapeDtypeStruct((WINDOW_LENGTH, kv_count * 2 * HEAD_SIZE), jnp.bfloat16),
            jax.ShapeDtypeStruct((tok_local, kv_count * 2 * HEAD_SIZE), jnp.float32),
        ],
        scratch_shapes=[
            pltpu.VMEM((HEAD_SIZE, span), jnp.bfloat16),
            pltpu.VMEM((span, 2 * HEAD_SIZE), jnp.float32),
            pltpu.VMEM((8, tok_local), jnp.float32),
            pltpu.VMEM((kv_count, tok_local, group * HEAD_SIZE), jnp.bfloat16),
            pltpu.SemaphoreType.DMA((kv_count, owners)),
        ],
        compiler_params=pltpu.CompilerParams(vmem_limit_bytes=40 * MIB),
        cost_estimate=pl.CostEstimate(
            flops=pairs * 2 * HEAD_SIZE * 5 * 4,
            bytes_accessed=8 * tok_local * group * kv_count * HEAD_SIZE,
            transcendentals=pairs,
        ),
        name="band",
    )(scal, queries, grad_out, attn_out, log_norm, keys, values, halo, halo, after)
    return outs[:owners], outs[owners], outs[owners + 1]


def finish_kernel(kv_count, owners, column, skip, scal, part_ref, back_ref, *rest):
    bufs = rest[skip:][:owners]
    scr, sems = rest[-2:]
    tok_local = part_ref.shape[0]
    chunk = tok_local // owners
    step = pl.program_id(0)
    me = scal[0]
    plain = tok_local - WINDOW_LENGTH
    scr[step, :plain] = part_ref[:plain].astype(jnp.bfloat16)
    scr[step, plain:] = (part_ref[plain:] + back_ref[...].astype(jnp.float32)).astype(jnp.bfloat16)

    def copies(index):
        result = []
        for flip in range(owners):
            owner = jnp.bitwise_xor(me, flip)
            rows = pl.ds(pl.multiple_of(owner * chunk, chunk), chunk)
            for kind in range(2):
                place = column + (kind * kv_count + index) * HEAD_SIZE
                result.append(
                    pltpu.make_async_copy(
                        scr.at[index, rows, pl.ds(kind * HEAD_SIZE, HEAD_SIZE)],
                        bufs[flip].at[:, pl.ds(place, HEAD_SIZE)],
                        sems.at[index, flip, kind],
                    )
                )
        return result

    for index in range(kv_count):

        @pl.when(step == index)
        def _(index=index):
            for copy in copies(index):
                copy.start()

    @pl.when(step == kv_count - 1)
    def _():
        for index in range(kv_count):
            for copy in copies(index):
                copy.wait()


def finish_call(kv_count, owners, column, scal, part, back, bufs, after):
    tok_local = part.shape[0]
    chunk = tok_local // owners
    aliased = bufs is not None
    shape = jax.ShapeDtypeStruct((chunk, column + kv_count * 2 * HEAD_SIZE), jnp.bfloat16)
    any_spec = pl.BlockSpec(memory_space=pl.ANY)
    return pl.pallas_call(
        functools.partial(
            finish_kernel, kv_count, owners, column, len(after) + (owners if aliased else 0)
        ),
        grid=(kv_count,),
        in_specs=[
            pl.BlockSpec(memory_space=pltpu.SMEM),
            pl.BlockSpec((tok_local, 2 * HEAD_SIZE), lambda g: (0, g)),
            pl.BlockSpec((WINDOW_LENGTH, 2 * HEAD_SIZE), lambda g: (0, g)),
        ]
        + [any_spec] * ((owners if aliased else 0) + len(after)),
        out_specs=[any_spec] * owners,
        out_shape=[shape] * owners,
        input_output_aliases={3 + i: i for i in range(owners)} if aliased else {},
        scratch_shapes=[
            pltpu.VMEM((kv_count, tok_local, 2 * HEAD_SIZE), jnp.bfloat16),
            pltpu.SemaphoreType.DMA((kv_count, owners, 2)),
        ],
        compiler_params=pltpu.CompilerParams(vmem_limit_bytes=16 * MIB),
        cost_estimate=pl.CostEstimate(
            flops=0, bytes_accessed=16 * tok_local * kv_count * HEAD_SIZE, transcendentals=0
        ),
        name="finish",
    )(scal, part, back, *(bufs if aliased else ()), *after)


def place_kernel(plan, owners, group, kv_local, aliased, scal, *rest):
    blocks = rest[:owners]
    outs = rest[owners + (3 if aliased else 0) :][:3]
    scr, in_sems, out_sems = rest[-3:]
    me = scal[0]
    loads = [
        pltpu.make_async_copy(blocks[flip], scr.at[flip], in_sems.at[flip])
        for flip in range(owners)
    ]
    for load in loads:
        load.start()
    stores = []
    for flip in range(owners):
        loads[flip].wait()
        source = jnp.bitwise_xor(me, flip)
        column = 0
        for which, (layer, kv_first, kv_count) in plan:
            heads = kv_count * group if which == 0 else kv_count
            home = kv_local * group if which == 0 else kv_local
            first = kv_first * group if which == 0 else kv_first
            place = pl.multiple_of((source * home + first) * HEAD_SIZE, HEAD_SIZE)
            store = pltpu.make_async_copy(
                scr.at[flip, :, pl.ds(column, heads * HEAD_SIZE)],
                outs[which].at[layer, :, pl.ds(place, heads * HEAD_SIZE)],
                out_sems.at[len(stores)],
            )
            store.start()
            stores.append(store)
            column += heads * HEAD_SIZE
    for store in stores:
        store.wait()


def place_call(plan, owners, group, kv_local, scal, blocks, outs):
    chunk, width = blocks[0].shape
    aliased = outs is not None
    any_spec = pl.BlockSpec(memory_space=pl.ANY)
    shapes = [
        jax.ShapeDtypeStruct(
            (SLIDING_LAYERS, chunk, owners * heads * HEAD_SIZE), jnp.bfloat16
        )
        for heads in (kv_local * group, kv_local, kv_local)
    ]
    return pl.pallas_call(
        functools.partial(place_kernel, plan, owners, group, kv_local, aliased),
        in_specs=[pl.BlockSpec(memory_space=pltpu.SMEM)]
        + [any_spec] * (owners + (3 if aliased else 0)),
        out_specs=[any_spec] * 3,
        out_shape=shapes,
        input_output_aliases={1 + owners + i: i for i in range(3)} if aliased else {},
        scratch_shapes=[
            pltpu.VMEM((owners, chunk, width), jnp.bfloat16),
            pltpu.SemaphoreType.DMA((owners,)),
            pltpu.SemaphoreType.DMA((owners * len(plan),)),
        ],
        compiler_params=pltpu.CompilerParams(vmem_limit_bytes=16 * MIB),
        cost_estimate=pl.CostEstimate(
            flops=0, bytes_accessed=owners * chunk * width * 4, transcendentals=0
        ),
        name="place",
    )(scal, *blocks, *(outs if aliased else ()))


def shards(queries, layer_keys_input, layer_values_input, attn_out, grad_out, log_norm, window):
    tok_local = queries.shape[1]
    kv_local = layer_keys_input.shape[2] // HEAD_SIZE
    group = queries.shape[2] // layer_keys_input.shape[2]
    owners = lax.axis_size("head")
    shard = lax.axis_index("ctx")
    scal = jnp.concatenate(
        [
            jnp.stack([lax.axis_index("head"), (shard == 0).astype(jnp.int32)]).astype(jnp.int32),
            window.astype(jnp.int32),
        ]
    )
    pieces = []
    for layer in range(SLIDING_LAYERS):
        kv_first = 0
        while kv_first < kv_local:
            kv_count = 1
            pieces.append((layer, kv_first, kv_count))
            kv_first += kv_count

    plans = [[(0, 0, 1)], [(0, 1, kv_local - 1)], [(1, 0, kv_local)]]
    packed = pack_call(plans[0], layer_keys_input, layer_values_input)
    packed += pack_call(plans[1] + plans[2], layer_keys_input, layer_values_input)
    halos = [shifted(block, "ctx", 1) for block in packed]

    def halo_of(layer, kv_first):
        if layer == 1:
            return halos[2], kv_first
        return (halos[0], 0) if kv_first == 0 else (halos[1], kv_first - 1)

    outs = None
    waiting = None
    after = scal
    sent = []

    def send(plan, bufs):
        blocks = [bufs[0]] + [swapped(bufs[flip], "head", flip) for flip in range(1, owners)]
        sent.append((plan, blocks))

    for index, piece in enumerate(pieces):
        layer, kv_first, kv_count = piece
        halo, column = halo_of(layer, kv_first)
        extra = 0 if waiting is None else 2 * waiting[0][2]
        bufs, back, part = band_call(
            piece,
            extra,
            owners,
            scal,
            queries,
            grad_out,
            attn_out,
            log_norm,
            layer_keys_input,
            layer_values_input,
            halo,
            column,
            after,
        )
        after = part
        back = shifted(back, "ctx", -1)
        plan = [(0, piece)]
        if waiting is not None:
            old, old_part, old_back = waiting
            before = sent[-1][1][1:]
            bufs = finish_call(
                old[2], owners, kv_count * group * HEAD_SIZE, scal, old_part, old_back, bufs, before
            )
            after = bufs[0]
            plan += [(1, old), (2, old)]
        send(plan, bufs)
        waiting = (piece, part, back)
    old, old_part, old_back = waiting
    bufs = finish_call(old[2], owners, 0, scal, old_part, old_back, None, ())
    send([(1, old), (2, old)], bufs)
    for plan, blocks in sent:
        outs = place_call(plan, owners, group, kv_local, scal, blocks, outs)
    return tuple(outs)


def solution(mesh):
    in_specs = (
        P(None, "ctx", "head"),
        P(None, "ctx", "head"),
        P(None, "ctx", "head"),
        P(None, "ctx", "head"),
        P(None, "ctx", "head"),
        P(None, "head", "ctx"),
        P(),
    )
    out_specs = (
        P(None, ("ctx", "head"), None),
        P(None, ("ctx", "head"), None),
        P(None, ("ctx", "head"), None),
    )
    return jax.shard_map(shards, mesh=mesh, in_specs=in_specs, out_specs=out_specs, check_vma=False)
```

```python
import functools
import math

import jax
import jax.numpy as jnp
from jax import lax
from jax.experimental import pallas as pl
from jax.experimental.pallas import tpu as pltpu
from jax.sharding import PartitionSpec as P

HEAD_SIZE = 128
WINDOW_LENGTH = 1024
QUERY_PRE = 168
SLIDING_LAYERS = 2
TILE = 128
UNITS = 4
SCALE = QUERY_PRE ** (-0.5)
LOG2E = math.log2(math.e)
FAR = 1e30
MIB = 1024 * 1024

NT = (((1,), (1,)), ((), ()))
NN = (((1,), (0,)), ((), ()))


def dot(a, b, dims=NN):
    return lax.dot_general(a, b, dims, preferred_element_type=jnp.float32)


def shifted(value, axis, steps):
    count = lax.axis_size(axis)
    first, last = (max(0, -steps), min(count, count - steps))
    return lax.ppermute(value, axis, [(source, source + steps) for source in range(first, last)])


def swapped(value, axis, flip):
    count = lax.axis_size(axis)
    return lax.ppermute(value, axis, [(source, source ^ flip) for source in range(count)])


def pack_kernel(plan, rows, *rest):
    count = len(plan)
    keys, values = rest[:2]
    outs = rest[2 : 2 + count]
    scrs = rest[2 + count : 2 + 2 * count]
    in_sems, out_sems = rest[2 + 2 * count :]
    loads = []
    for index, (layer, kv_first, kv_count) in enumerate(plan):
        width = kv_count * HEAD_SIZE
        for kind, array in enumerate((keys, values)):
            loads.append(
                pltpu.make_async_copy(
                    array.at[layer, rows, pl.ds(kv_first * HEAD_SIZE, width)],
                    scrs[index].at[:, pl.ds(kind * width, width)],
                    in_sems.at[index, kind],
                )
            )
    for load in loads:
        load.start()
    stores = []
    for index in range(count):
        loads[2 * index].wait()
        loads[2 * index + 1].wait()
        store = pltpu.make_async_copy(scrs[index], outs[index], out_sems.at[index])
        store.start()
        stores.append(store)
    for store in stores:
        store.wait()


def pack_call(plan, keys, values):
    tok_local = keys.shape[1]
    any_spec = pl.BlockSpec(memory_space=pl.ANY)
    sizes = [(WINDOW_LENGTH, 2 * kv_count * HEAD_SIZE) for _, _, kv_count in plan]
    return pl.pallas_call(
        functools.partial(pack_kernel, plan, pl.ds(tok_local - WINDOW_LENGTH, WINDOW_LENGTH)),
        in_specs=[any_spec] * 2,
        out_specs=[any_spec] * len(plan),
        out_shape=[jax.ShapeDtypeStruct(size, jnp.bfloat16) for size in sizes],
        scratch_shapes=[pltpu.VMEM(size, jnp.bfloat16) for size in sizes]
        + [pltpu.SemaphoreType.DMA((len(plan), 2)), pltpu.SemaphoreType.DMA((len(plan),))],
        compiler_params=pltpu.CompilerParams(vmem_limit_bytes=60 * MIB),
        cost_estimate=pl.CostEstimate(
            flops=0, bytes_accessed=4 * sum(size[0] * size[1] for size in sizes), transcendentals=0
        ),
        name="pack",
    )(keys, values)


def band_kernel(
    layer,
    kv_first,
    kv_count,
    owners,
    scal,
    q_ref,
    do_ref,
    out_ref,
    lse_ref,
    k_ref,
    v_ref,
    k_halo,
    v_halo,
    after,
    *rest,
):
    dq_bufs = rest[:owners]
    back_ref, part_ref, kx, vx, kt, acc, lse2_scr, dq_scr, sems = rest[owners:]
    tok_local = q_ref.shape[1]
    group = q_ref.shape[2] // HEAD_SIZE
    chunk = tok_local // owners
    step = pl.program_id(0)
    me = scal[0]
    first_shard = scal[1]
    win = scal[2 + layer]
    wide = group * TILE

    rows_step = UNITS * TILE
    head = (kv_first + step) * group

    kx[0:WINDOW_LENGTH] = k_halo[...]
    vx[0:WINDOW_LENGTH] = v_halo[...]
    kx[WINDOW_LENGTH:] = k_ref[0]
    vx[WINDOW_LENGTH:] = v_ref[0]
    kt[:, 0:WINDOW_LENGTH] = k_halo[...].T
    for h in range(group):
        lse2_scr[h : h + 1, :] = lse_ref[0, pl.ds(head + h, 1), :] * LOG2E
    acc[0:WINDOW_LENGTH] = jnp.zeros((WINDOW_LENGTH, 2 * HEAD_SIZE), jnp.float32)

    rows = lax.broadcasted_iota(jnp.int32, (TILE, wide), 0)
    lanes = lax.broadcasted_iota(jnp.int32, (1, wide), 1) % TILE
    left = lax.broadcasted_iota(jnp.int32, (1, HEAD_SIZE), 1) < HEAD_SIZE // 2

    def stacked(ref, start):
        block = ref[0, pl.ds(start, TILE), :]
        return jnp.concatenate(
            [block[:, h * HEAD_SIZE : (h + 1) * HEAD_SIZE] for h in range(group)], 0
        )

    def sweep(reach):
        tiles = reach // TILE + 1
        skipped = WINDOW_LENGTH - reach
        minus = jnp.full((tiles * TILE, HEAD_SIZE), -1, jnp.bfloat16)

        def one_step(index, carry):
            start = pl.multiple_of(index * rows_step, rows_step)
            fresh = pl.ds(pl.multiple_of(start + WINDOW_LENGTH, TILE), rows_step)
            kt[:, fresh] = kx[fresh, :].T
            acc[fresh, :] = jnp.zeros((rows_step, 2 * HEAD_SIZE), jnp.float32)

            def products(unit):
                begin = pl.multiple_of(start + unit * TILE, TILE)
                q2 = stacked(q_ref, begin)
                do2 = stacked(do_ref, begin)
                span = pl.ds(pl.multiple_of(begin + skipped, TILE), tiles * TILE)
                prod = do2.astype(jnp.float32) * stacked(out_ref, begin).astype(jnp.float32)
                pair = prod + pltpu.roll(prod, HEAD_SIZE // 2, 1)
                coarse = pair.astype(jnp.bfloat16).astype(jnp.float32)
                terms = jnp.where(left, coarse, pair - coarse).astype(jnp.bfloat16)
                scores = dot(kx[span, :], q2, NT)
                lead = jnp.concatenate([vx[span, :], minus], 1)
                excess = dot(lead, jnp.concatenate([do2, terms], 1), NT)
                lse2 = jnp.concatenate(
                    [lse2_scr[h : h + 1, pl.ds(begin, TILE)] for h in range(group)], 1
                )
                return begin, q2, do2, scores, excess, lse2

            def weights(begin, q2, do2, scores, excess, lse2):
                probs, grads = [], []
                for tile in range(tiles):
                    part = slice(tile * TILE, (tile + 1) * TILE)
                    line = lse2
                    if tile < tiles - 1:
                        outside = jnp.logical_and(
                            first_shard == 1, begin + skipped + tile * TILE < WINDOW_LENGTH
                        )
                        line = jnp.where(outside, FAR, lse2)
                    prob = jnp.exp2(scores[part] * (SCALE * LOG2E) - line)
                    if tile == tiles - 1:
                        prob = jnp.where(rows <= lanes, prob, 0.0)
                    elif tile < 3:
                        prob = jnp.where(rows > lanes + (reach - win - tile * TILE), prob, 0.0)
                    probs.append(prob.astype(jnp.bfloat16))
                    grads.append((prob * excess[part]).astype(jnp.bfloat16))
                return begin, q2, do2, probs, grads

            def finish(first, second):
                begin = first[0]
                for lefts, rights, kind in ((3, 2, 1), (4, 1, 0)):
                    one, two = first[lefts], second[lefts]
                    side = slice(kind * HEAD_SIZE, (kind + 1) * HEAD_SIZE)
                    base = begin + skipped
                    middle = jnp.concatenate(
                        [jnp.concatenate(one[1:], 0), jnp.concatenate(two[:-1], 0)], 1
                    )
                    both = jnp.concatenate([first[rights], second[rights]], 0)
                    acc[pl.ds(pl.multiple_of(base, TILE), TILE), side] += dot(one[0], first[rights])
                    acc[pl.ds(pl.multiple_of(base + TILE, TILE), (tiles - 1) * TILE), side] += dot(
                        middle, both
                    )
                    acc[pl.ds(pl.multiple_of(base + tiles * TILE, TILE), TILE), side] += dot(
                        two[-1], second[rights]
                    )
                for begin, _, _, _, grads in (first, second):
                    span = pl.ds(pl.multiple_of(begin + skipped, TILE), tiles * TILE)
                    dq = (dot(kt[:, span], jnp.concatenate(grads, 0)).T * SCALE).astype(jnp.bfloat16)
                    for h in range(group):
                        dq_scr[step, pl.ds(begin, TILE), h * HEAD_SIZE : (h + 1) * HEAD_SIZE] = dq[
                            h * TILE : (h + 1) * TILE
                        ]

            held = products(0)
            done = []
            for unit in range(UNITS):
                coming = products(unit + 1) if unit + 1 < UNITS else None
                done.append(weights(*held))
                held = coming
                if unit % 2 == 1:
                    finish(done[unit - 1], done[unit])
            return carry

        lax.fori_loop(0, tok_local // rows_step, one_step, 0)

    low = 0
    for reach in (WINDOW_LENGTH * 3 // 4, WINDOW_LENGTH):

        @pl.when(jnp.logical_and(win > low, win <= reach))
        def _(reach=reach):
            sweep(reach)

        low = reach

    back_ref[:, :HEAD_SIZE] = (acc[0:WINDOW_LENGTH, :HEAD_SIZE] * SCALE).astype(jnp.bfloat16)
    back_ref[:, HEAD_SIZE:] = acc[0:WINDOW_LENGTH, HEAD_SIZE:].astype(jnp.bfloat16)
    part_ref[:, :HEAD_SIZE] = acc[WINDOW_LENGTH:, :HEAD_SIZE] * SCALE
    part_ref[:, HEAD_SIZE:] = acc[WINDOW_LENGTH:, HEAD_SIZE:]

    def copies(index):
        result = []
        for flip in range(owners):
            owner = jnp.bitwise_xor(me, flip)
            source = dq_scr.at[index, pl.ds(pl.multiple_of(owner * chunk, chunk), chunk), :]
            target = dq_bufs[flip].at[:, pl.ds(index * group * HEAD_SIZE, group * HEAD_SIZE)]
            result.append(pltpu.make_async_copy(source, target, sems.at[index, flip]))
        return result

    for index in range(kv_count):

        @pl.when(step == index)
        def _(index=index):
            for copy in copies(index):
                copy.start()

    @pl.when(step == kv_count - 1)
    def _():
        for index in range(kv_count):
            for copy in copies(index):
                copy.wait()


def band_call(piece, extra, owners, scal, queries, grad_out, attn_out, log_norm, keys, values, halo, column, after):
    layer, kv_first, kv_count = piece
    tok_local = queries.shape[1]
    group = queries.shape[2] // keys.shape[2]
    span = WINDOW_LENGTH + tok_local
    chunk = tok_local // owners
    halo_kv = halo.shape[1] // (2 * HEAD_SIZE)
    q_spec = pl.BlockSpec((1, tok_local, group * HEAD_SIZE), lambda g: (layer, 0, kv_first + g))
    kv_spec = pl.BlockSpec((1, tok_local, HEAD_SIZE), lambda g: (layer, 0, kv_first + g))
    pairs = tok_local * (WINDOW_LENGTH + 2 * TILE) * group * kv_count
    outs = pl.pallas_call(
        functools.partial(band_kernel, layer, kv_first, kv_count, owners),
        grid=(kv_count,),
        in_specs=[
            pl.BlockSpec(memory_space=pltpu.SMEM),
            q_spec,
            q_spec,
            q_spec,
            pl.BlockSpec((1,) + log_norm.shape[1:], lambda g: (layer, 0, 0)),
            kv_spec,
            kv_spec,
            pl.BlockSpec((WINDOW_LENGTH, HEAD_SIZE), lambda g: (0, column + g)),
            pl.BlockSpec((WINDOW_LENGTH, HEAD_SIZE), lambda g: (0, halo_kv + column + g)),
            pl.BlockSpec(memory_space=pl.ANY),
        ],
        out_specs=[pl.BlockSpec(memory_space=pl.ANY)] * owners
        + [
            pl.BlockSpec((WINDOW_LENGTH, 2 * HEAD_SIZE), lambda g: (0, g)),
            pl.BlockSpec((tok_local, 2 * HEAD_SIZE), lambda g: (0, g)),
        ],
        out_shape=[
            jax.ShapeDtypeStruct((chunk, (kv_count * group + extra) * HEAD_SIZE), jnp.bfloat16)
        ]
        * owners
        + [
            jax.ShapeDtypeStruct((WINDOW_LENGTH, kv_count * 2 * HEAD_SIZE), jnp.bfloat16),
            jax.ShapeDtypeStruct((tok_local, kv_count * 2 * HEAD_SIZE), jnp.float32),
        ],
        scratch_shapes=[
            pltpu.VMEM((span, HEAD_SIZE), jnp.bfloat16),
            pltpu.VMEM((span, HEAD_SIZE), jnp.bfloat16),
            pltpu.VMEM((HEAD_SIZE, span), jnp.bfloat16),
            pltpu.VMEM((span, 2 * HEAD_SIZE), jnp.float32),
            pltpu.VMEM((8, tok_local), jnp.float32),
            pltpu.VMEM((kv_count, tok_local, group * HEAD_SIZE), jnp.bfloat16),
            pltpu.SemaphoreType.DMA((kv_count, owners)),
        ],
        compiler_params=pltpu.CompilerParams(vmem_limit_bytes=40 * MIB),
        cost_estimate=pl.CostEstimate(
            flops=pairs * 2 * HEAD_SIZE * 5 * 4,
            bytes_accessed=8 * tok_local * group * kv_count * HEAD_SIZE,
            transcendentals=pairs,
        ),
        name="band",
    )(scal, queries, grad_out, attn_out, log_norm, keys, values, halo, halo, after)
    return outs[:owners], outs[owners], outs[owners + 1]


def finish_kernel(kv_count, owners, column, skip, scal, part_ref, back_ref, *rest):
    bufs = rest[skip:][:owners]
    scr, sems = rest[-2:]
    tok_local = part_ref.shape[0]
    chunk = tok_local // owners
    step = pl.program_id(0)
    me = scal[0]
    plain = tok_local - WINDOW_LENGTH
    scr[step, :plain] = part_ref[:plain].astype(jnp.bfloat16)
    scr[step, plain:] = (part_ref[plain:] + back_ref[...].astype(jnp.float32)).astype(jnp.bfloat16)

    def copies(index):
        result = []
        for flip in range(owners):
            owner = jnp.bitwise_xor(me, flip)
            rows = pl.ds(pl.multiple_of(owner * chunk, chunk), chunk)
            for kind in range(2):
                place = column + (kind * kv_count + index) * HEAD_SIZE
                result.append(
                    pltpu.make_async_copy(
                        scr.at[index, rows, pl.ds(kind * HEAD_SIZE, HEAD_SIZE)],
                        bufs[flip].at[:, pl.ds(place, HEAD_SIZE)],
                        sems.at[index, flip, kind],
                    )
                )
        return result

    for index in range(kv_count):

        @pl.when(step == index)
        def _(index=index):
            for copy in copies(index):
                copy.start()

    @pl.when(step == kv_count - 1)
    def _():
        for index in range(kv_count):
            for copy in copies(index):
                copy.wait()


def finish_call(kv_count, owners, column, scal, part, back, bufs, after):
    tok_local = part.shape[0]
    chunk = tok_local // owners
    aliased = bufs is not None
    shape = jax.ShapeDtypeStruct((chunk, column + kv_count * 2 * HEAD_SIZE), jnp.bfloat16)
    any_spec = pl.BlockSpec(memory_space=pl.ANY)
    return pl.pallas_call(
        functools.partial(
            finish_kernel, kv_count, owners, column, len(after) + (owners if aliased else 0)
        ),
        grid=(kv_count,),
        in_specs=[
            pl.BlockSpec(memory_space=pltpu.SMEM),
            pl.BlockSpec((tok_local, 2 * HEAD_SIZE), lambda g: (0, g)),
            pl.BlockSpec((WINDOW_LENGTH, 2 * HEAD_SIZE), lambda g: (0, g)),
        ]
        + [any_spec] * ((owners if aliased else 0) + len(after)),
        out_specs=[any_spec] * owners,
        out_shape=[shape] * owners,
        input_output_aliases={3 + i: i for i in range(owners)} if aliased else {},
        scratch_shapes=[
            pltpu.VMEM((kv_count, tok_local, 2 * HEAD_SIZE), jnp.bfloat16),
            pltpu.SemaphoreType.DMA((kv_count, owners, 2)),
        ],
        compiler_params=pltpu.CompilerParams(vmem_limit_bytes=16 * MIB),
        cost_estimate=pl.CostEstimate(
            flops=0, bytes_accessed=16 * tok_local * kv_count * HEAD_SIZE, transcendentals=0
        ),
        name="finish",
    )(scal, part, back, *(bufs if aliased else ()), *after)


def place_kernel(plan, owners, group, kv_local, aliased, scal, *rest):
    blocks = rest[:owners]
    outs = rest[owners + (3 if aliased else 0) :][:3]
    scr, in_sems, out_sems = rest[-3:]
    me = scal[0]
    loads = [
        pltpu.make_async_copy(blocks[flip], scr.at[flip], in_sems.at[flip])
        for flip in range(owners)
    ]
    for load in loads:
        load.start()
    stores = []
    for flip in range(owners):
        loads[flip].wait()
        source = jnp.bitwise_xor(me, flip)
        column = 0
        for which, (layer, kv_first, kv_count) in plan:
            heads = kv_count * group if which == 0 else kv_count
            home = kv_local * group if which == 0 else kv_local
            first = kv_first * group if which == 0 else kv_first
            place = pl.multiple_of((source * home + first) * HEAD_SIZE, HEAD_SIZE)
            store = pltpu.make_async_copy(
                scr.at[flip, :, pl.ds(column, heads * HEAD_SIZE)],
                outs[which].at[layer, :, pl.ds(place, heads * HEAD_SIZE)],
                out_sems.at[len(stores)],
            )
            store.start()
            stores.append(store)
            column += heads * HEAD_SIZE
    for store in stores:
        store.wait()


def place_call(plan, owners, group, kv_local, scal, blocks, outs):
    chunk, width = blocks[0].shape
    aliased = outs is not None
    any_spec = pl.BlockSpec(memory_space=pl.ANY)
    shapes = [
        jax.ShapeDtypeStruct(
            (SLIDING_LAYERS, chunk, owners * heads * HEAD_SIZE), jnp.bfloat16
        )
        for heads in (kv_local * group, kv_local, kv_local)
    ]
    return pl.pallas_call(
        functools.partial(place_kernel, plan, owners, group, kv_local, aliased),
        in_specs=[pl.BlockSpec(memory_space=pltpu.SMEM)]
        + [any_spec] * (owners + (3 if aliased else 0)),
        out_specs=[any_spec] * 3,
        out_shape=shapes,
        input_output_aliases={1 + owners + i: i for i in range(3)} if aliased else {},
        scratch_shapes=[
            pltpu.VMEM((owners, chunk, width), jnp.bfloat16),
            pltpu.SemaphoreType.DMA((owners,)),
            pltpu.SemaphoreType.DMA((owners * len(plan),)),
        ],
        compiler_params=pltpu.CompilerParams(vmem_limit_bytes=16 * MIB),
        cost_estimate=pl.CostEstimate(
            flops=0, bytes_accessed=owners * chunk * width * 4, transcendentals=0
        ),
        name="place",
    )(scal, *blocks, *(outs if aliased else ()))


def shards(queries, layer_keys_input, layer_values_input, attn_out, grad_out, log_norm, window):
    tok_local = queries.shape[1]
    kv_local = layer_keys_input.shape[2] // HEAD_SIZE
    group = queries.shape[2] // layer_keys_input.shape[2]
    owners = lax.axis_size("head")
    shard = lax.axis_index("ctx")
    scal = jnp.concatenate(
        [
            jnp.stack([lax.axis_index("head"), (shard == 0).astype(jnp.int32)]).astype(jnp.int32),
            window.astype(jnp.int32),
        ]
    )
    pieces = []
    for layer in range(SLIDING_LAYERS):
        kv_first = 0
        while kv_first < kv_local:
            kv_count = 1
            pieces.append((layer, kv_first, kv_count))
            kv_first += kv_count

    plans = [[(0, 0, 1)], [(0, 1, kv_local - 1)], [(1, 0, kv_local)]]
    packed = pack_call(plans[0], layer_keys_input, layer_values_input)
    packed += pack_call(plans[1] + plans[2], layer_keys_input, layer_values_input)
    halos = [shifted(block, "ctx", 1) for block in packed]

    def halo_of(layer, kv_first):
        if layer == 1:
            return halos[2], kv_first
        return (halos[0], 0) if kv_first == 0 else (halos[1], kv_first - 1)

    outs = None
    waiting = None
    after = scal
    sent = []

    def send(plan, bufs):
        blocks = [bufs[0]] + [swapped(bufs[flip], "head", flip) for flip in range(1, owners)]
        sent.append((plan, blocks))

    for index, piece in enumerate(pieces):
        layer, kv_first, kv_count = piece
        halo, column = halo_of(layer, kv_first)
        extra = 0 if waiting is None else 2 * waiting[0][2]
        bufs, back, part = band_call(
            piece,
            extra,
            owners,
            scal,
            queries,
            grad_out,
            attn_out,
            log_norm,
            layer_keys_input,
            layer_values_input,
            halo,
            column,
            after,
        )
        after = part
        back = shifted(back, "ctx", -1)
        plan = [(0, piece)]
        if waiting is not None:
            old, old_part, old_back = waiting
            before = sent[-1][1][1:]
            bufs = finish_call(
                old[2], owners, kv_count * group * HEAD_SIZE, scal, old_part, old_back, bufs, before
            )
            after = bufs[0]
            plan += [(1, old), (2, old)]
        send(plan, bufs)
        waiting = (piece, part, back)
    old, old_part, old_back = waiting
    bufs = finish_call(old[2], owners, 0, scal, old_part, old_back, None, ())
    send([(1, old), (2, old)], bufs)
    for plan, blocks in sent:
        outs = place_call(plan, owners, group, kv_local, scal, blocks, outs)
    return tuple(outs)


def solution(mesh):
    in_specs = (
        P(None, "ctx", "head"),
        P(None, "ctx", "head"),
        P(None, "ctx", "head"),
        P(None, "ctx", "head"),
        P(None, "ctx", "head"),
        P(None, "head", "ctx"),
        P(),
    )
    out_specs = (
        P(None, ("ctx", "head"), None),
        P(None, ("ctx", "head"), None),
        P(None, ("ctx", "head"), None),
    )
    return jax.shard_map(shards, mesh=mesh, in_specs=in_specs, out_specs=out_specs, check_vma=False)
```

```python
import functools
import math

import jax
import jax.numpy as jnp
from jax import lax
from jax.experimental import pallas as pl
from jax.experimental.pallas import tpu as pltpu
from jax.sharding import PartitionSpec as P

HEAD_SIZE = 128
WINDOW_LENGTH = 1024
QUERY_PRE = 168
SLIDING_LAYERS = 2
TILE = 128
UNITS = 4
SCALE = QUERY_PRE ** (-0.5)
LOG2E = math.log2(math.e)
FAR = 1e30
MIB = 1024 * 1024

NT = (((1,), (1,)), ((), ()))
NN = (((1,), (0,)), ((), ()))


def dot(a, b, dims=NN):
    return lax.dot_general(a, b, dims, preferred_element_type=jnp.float32)


def shifted(value, axis, steps):
    count = lax.axis_size(axis)
    first, last = (max(0, -steps), min(count, count - steps))
    return lax.ppermute(value, axis, [(source, source + steps) for source in range(first, last)])


def swapped(value, axis, flip):
    count = lax.axis_size(axis)
    return lax.ppermute(value, axis, [(source, source ^ flip) for source in range(count)])


def pack_kernel(plan, rows, *rest):
    count = len(plan)
    keys, values = rest[:2]
    outs = rest[2 : 2 + count]
    scrs = rest[2 + count : 2 + 2 * count]
    in_sems, out_sems = rest[2 + 2 * count :]
    loads = []
    for index, (layer, kv_first, kv_count) in enumerate(plan):
        width = kv_count * HEAD_SIZE
        for kind, array in enumerate((keys, values)):
            loads.append(
                pltpu.make_async_copy(
                    array.at[layer, rows, pl.ds(kv_first * HEAD_SIZE, width)],
                    scrs[index].at[:, pl.ds(kind * width, width)],
                    in_sems.at[index, kind],
                )
            )
    for load in loads:
        load.start()
    stores = []
    for index in range(count):
        loads[2 * index].wait()
        loads[2 * index + 1].wait()
        store = pltpu.make_async_copy(scrs[index], outs[index], out_sems.at[index])
        store.start()
        stores.append(store)
    for store in stores:
        store.wait()


def pack_call(plan, keys, values):
    tok_local = keys.shape[1]
    any_spec = pl.BlockSpec(memory_space=pl.ANY)
    sizes = [(WINDOW_LENGTH, 2 * kv_count * HEAD_SIZE) for _, _, kv_count in plan]
    return pl.pallas_call(
        functools.partial(pack_kernel, plan, pl.ds(tok_local - WINDOW_LENGTH, WINDOW_LENGTH)),
        in_specs=[any_spec] * 2,
        out_specs=[any_spec] * len(plan),
        out_shape=[jax.ShapeDtypeStruct(size, jnp.bfloat16) for size in sizes],
        scratch_shapes=[pltpu.VMEM(size, jnp.bfloat16) for size in sizes]
        + [pltpu.SemaphoreType.DMA((len(plan), 2)), pltpu.SemaphoreType.DMA((len(plan),))],
        compiler_params=pltpu.CompilerParams(vmem_limit_bytes=60 * MIB),
        cost_estimate=pl.CostEstimate(
            flops=0, bytes_accessed=4 * sum(size[0] * size[1] for size in sizes), transcendentals=0
        ),
        name="pack",
    )(keys, values)


def band_kernel(
    layer,
    kv_first,
    kv_count,
    owners,
    skip,
    scal,
    q_ref,
    do_ref,
    out_ref,
    lse_ref,
    k_ref,
    v_ref,
    k_halo,
    v_halo,
    *rest,
):
    dq_bufs = rest[skip:][:owners]
    back_ref, part_ref, kx, vx, kt, acc, lse2_scr, dq_scr, sems = rest[skip + owners :]
    tok_local = q_ref.shape[1]
    group = q_ref.shape[2] // HEAD_SIZE
    chunk = tok_local // owners
    step = pl.program_id(0)
    me = scal[0]
    first_shard = scal[1]
    win = scal[2 + layer]
    wide = group * TILE

    rows_step = UNITS * TILE
    head = (kv_first + step) * group

    kx[0:WINDOW_LENGTH] = k_halo[...]
    vx[0:WINDOW_LENGTH] = v_halo[...]
    kx[WINDOW_LENGTH:] = k_ref[0]
    vx[WINDOW_LENGTH:] = v_ref[0]
    kt[:, 0:WINDOW_LENGTH] = k_halo[...].T
    for h in range(group):
        lse2_scr[h : h + 1, :] = lse_ref[0, pl.ds(head + h, 1), :] * LOG2E
    acc[0:WINDOW_LENGTH] = jnp.zeros((WINDOW_LENGTH, 2 * HEAD_SIZE), jnp.float32)

    rows = lax.broadcasted_iota(jnp.int32, (TILE, wide), 0)
    lanes = lax.broadcasted_iota(jnp.int32, (1, wide), 1) % TILE
    left = lax.broadcasted_iota(jnp.int32, (1, HEAD_SIZE), 1) < HEAD_SIZE // 2

    def stacked(ref, start):
        block = ref[0, pl.ds(start, TILE), :]
        return jnp.concatenate(
            [block[:, h * HEAD_SIZE : (h + 1) * HEAD_SIZE] for h in range(group)], 0
        )

    def sweep(reach):
        tiles = reach // TILE + 1
        skipped = WINDOW_LENGTH - reach
        minus = jnp.full((tiles * TILE, HEAD_SIZE), -1, jnp.bfloat16)

        def one_step(index, carry):
            start = pl.multiple_of(index * rows_step, rows_step)
            fresh = pl.ds(pl.multiple_of(start + WINDOW_LENGTH, TILE), rows_step)
            kt[:, fresh] = kx[fresh, :].T
            acc[fresh, :] = jnp.zeros((rows_step, 2 * HEAD_SIZE), jnp.float32)

            def products(unit):
                begin = pl.multiple_of(start + unit * TILE, TILE)
                q2 = stacked(q_ref, begin)
                do2 = stacked(do_ref, begin)
                span = pl.ds(pl.multiple_of(begin + skipped, TILE), tiles * TILE)
                prod = do2.astype(jnp.float32) * stacked(out_ref, begin).astype(jnp.float32)
                pair = prod + pltpu.roll(prod, HEAD_SIZE // 2, 1)
                coarse = pair.astype(jnp.bfloat16).astype(jnp.float32)
                terms = jnp.where(left, coarse, pair - coarse).astype(jnp.bfloat16)
                scores = dot(kx[span, :], q2, NT)
                lead = jnp.concatenate([vx[span, :], minus], 1)
                excess = dot(lead, jnp.concatenate([do2, terms], 1), NT)
                lse2 = jnp.concatenate(
                    [lse2_scr[h : h + 1, pl.ds(begin, TILE)] for h in range(group)], 1
                )
                return begin, q2, do2, scores, excess, lse2

            def weights(begin, q2, do2, scores, excess, lse2):
                probs, grads = [], []
                for tile in range(tiles):
                    part = slice(tile * TILE, (tile + 1) * TILE)
                    line = lse2
                    if tile < tiles - 1:
                        outside = jnp.logical_and(
                            first_shard == 1, begin + skipped + tile * TILE < WINDOW_LENGTH
                        )
                        line = jnp.where(outside, FAR, lse2)
                    prob = jnp.exp2(scores[part] * (SCALE * LOG2E) - line)
                    if tile == tiles - 1:
                        prob = jnp.where(rows <= lanes, prob, 0.0)
                    elif tile < 3:
                        prob = jnp.where(rows > lanes + (reach - win - tile * TILE), prob, 0.0)
                    probs.append(prob.astype(jnp.bfloat16))
                    grads.append((prob * excess[part]).astype(jnp.bfloat16))
                return begin, q2, do2, probs, grads

            def finish(first, second):
                begin = first[0]
                for lefts, rights, kind in ((3, 2, 1), (4, 1, 0)):
                    one, two = first[lefts], second[lefts]
                    side = slice(kind * HEAD_SIZE, (kind + 1) * HEAD_SIZE)
                    base = begin + skipped
                    middle = jnp.concatenate(
                        [jnp.concatenate(one[1:], 0), jnp.concatenate(two[:-1], 0)], 1
                    )
                    both = jnp.concatenate([first[rights], second[rights]], 0)
                    acc[pl.ds(pl.multiple_of(base, TILE), TILE), side] += dot(one[0], first[rights])
                    acc[pl.ds(pl.multiple_of(base + TILE, TILE), (tiles - 1) * TILE), side] += dot(
                        middle, both
                    )
                    acc[pl.ds(pl.multiple_of(base + tiles * TILE, TILE), TILE), side] += dot(
                        two[-1], second[rights]
                    )
                for begin, _, _, _, grads in (first, second):
                    span = pl.ds(pl.multiple_of(begin + skipped, TILE), tiles * TILE)
                    dq = (dot(kt[:, span], jnp.concatenate(grads, 0)).T * SCALE).astype(jnp.bfloat16)
                    for h in range(group):
                        dq_scr[step, pl.ds(begin, TILE), h * HEAD_SIZE : (h + 1) * HEAD_SIZE] = dq[
                            h * TILE : (h + 1) * TILE
                        ]

            held = products(0)
            done = []
            for unit in range(UNITS):
                coming = products(unit + 1) if unit + 1 < UNITS else None
                done.append(weights(*held))
                held = coming
                if unit % 2 == 1:
                    finish(done[unit - 1], done[unit])
            return carry

        lax.fori_loop(0, tok_local // rows_step, one_step, 0)

    low = 0
    for reach in (WINDOW_LENGTH * 3 // 4, WINDOW_LENGTH):

        @pl.when(jnp.logical_and(win > low, win <= reach))
        def _(reach=reach):
            sweep(reach)

        low = reach

    back_ref[:, :HEAD_SIZE] = (acc[0:WINDOW_LENGTH, :HEAD_SIZE] * SCALE).astype(jnp.bfloat16)
    back_ref[:, HEAD_SIZE:] = acc[0:WINDOW_LENGTH, HEAD_SIZE:].astype(jnp.bfloat16)
    part_ref[:, :HEAD_SIZE] = acc[WINDOW_LENGTH:, :HEAD_SIZE] * SCALE
    part_ref[:, HEAD_SIZE:] = acc[WINDOW_LENGTH:, HEAD_SIZE:]

    def copies(index):
        result = []
        for flip in range(owners):
            owner = jnp.bitwise_xor(me, flip)
            source = dq_scr.at[index, pl.ds(pl.multiple_of(owner * chunk, chunk), chunk), :]
            target = dq_bufs[flip].at[:, pl.ds(index * group * HEAD_SIZE, group * HEAD_SIZE)]
            result.append(pltpu.make_async_copy(source, target, sems.at[index, flip]))
        return result

    for index in range(kv_count):

        @pl.when(step == index)
        def _(index=index):
            for copy in copies(index):
                copy.start()

    @pl.when(step == kv_count - 1)
    def _():
        for index in range(kv_count):
            for copy in copies(index):
                copy.wait()


def band_call(piece, extra, owners, scal, queries, grad_out, attn_out, log_norm, keys, values, halo, column, after):
    layer, kv_first, kv_count = piece
    tok_local = queries.shape[1]
    group = queries.shape[2] // keys.shape[2]
    span = WINDOW_LENGTH + tok_local
    chunk = tok_local // owners
    halo_kv = halo.shape[1] // (2 * HEAD_SIZE)
    q_spec = pl.BlockSpec((1, tok_local, group * HEAD_SIZE), lambda g: (layer, 0, kv_first + g))
    kv_spec = pl.BlockSpec((1, tok_local, HEAD_SIZE), lambda g: (layer, 0, kv_first + g))
    pairs = tok_local * (WINDOW_LENGTH + 2 * TILE) * group * kv_count
    outs = pl.pallas_call(
        functools.partial(band_kernel, layer, kv_first, kv_count, owners, len(after)),
        grid=(kv_count,),
        in_specs=[
            pl.BlockSpec(memory_space=pltpu.SMEM),
            q_spec,
            q_spec,
            q_spec,
            pl.BlockSpec((1,) + log_norm.shape[1:], lambda g: (layer, 0, 0)),
            kv_spec,
            kv_spec,
            pl.BlockSpec((WINDOW_LENGTH, HEAD_SIZE), lambda g: (0, column + g)),
            pl.BlockSpec((WINDOW_LENGTH, HEAD_SIZE), lambda g: (0, halo_kv + column + g)),
        ]
        + [pl.BlockSpec(memory_space=pl.ANY)] * len(after),
        out_specs=[pl.BlockSpec(memory_space=pl.ANY)] * owners
        + [
            pl.BlockSpec((WINDOW_LENGTH, 2 * HEAD_SIZE), lambda g: (0, g)),
            pl.BlockSpec((tok_local, 2 * HEAD_SIZE), lambda g: (0, g)),
        ],
        out_shape=[
            jax.ShapeDtypeStruct((chunk, (kv_count * group + extra) * HEAD_SIZE), jnp.bfloat16)
        ]
        * owners
        + [
            jax.ShapeDtypeStruct((WINDOW_LENGTH, kv_count * 2 * HEAD_SIZE), jnp.bfloat16),
            jax.ShapeDtypeStruct((tok_local, kv_count * 2 * HEAD_SIZE), jnp.float32),
        ],
        scratch_shapes=[
            pltpu.VMEM((span, HEAD_SIZE), jnp.bfloat16),
            pltpu.VMEM((span, HEAD_SIZE), jnp.bfloat16),
            pltpu.VMEM((HEAD_SIZE, span), jnp.bfloat16),
            pltpu.VMEM((span, 2 * HEAD_SIZE), jnp.float32),
            pltpu.VMEM((8, tok_local), jnp.float32),
            pltpu.VMEM((kv_count, tok_local, group * HEAD_SIZE), jnp.bfloat16),
            pltpu.SemaphoreType.DMA((kv_count, owners)),
        ],
        compiler_params=pltpu.CompilerParams(vmem_limit_bytes=40 * MIB),
        cost_estimate=pl.CostEstimate(
            flops=pairs * 2 * HEAD_SIZE * 5 * 4,
            bytes_accessed=8 * tok_local * group * kv_count * HEAD_SIZE,
            transcendentals=pairs,
        ),
        name="band",
    )(scal, queries, grad_out, attn_out, log_norm, keys, values, halo, halo, *after)
    return outs[:owners], outs[owners], outs[owners + 1]


def finish_kernel(kv_count, owners, column, skip, scal, part_ref, back_ref, *rest):
    bufs = rest[skip:][:owners]
    scr, sems = rest[-2:]
    tok_local = part_ref.shape[0]
    chunk = tok_local // owners
    step = pl.program_id(0)
    me = scal[0]
    plain = tok_local - WINDOW_LENGTH
    scr[step, :plain] = part_ref[:plain].astype(jnp.bfloat16)
    scr[step, plain:] = (part_ref[plain:] + back_ref[...].astype(jnp.float32)).astype(jnp.bfloat16)

    def copies(index):
        result = []
        for flip in range(owners):
            owner = jnp.bitwise_xor(me, flip)
            rows = pl.ds(pl.multiple_of(owner * chunk, chunk), chunk)
            for kind in range(2):
                place = column + (kind * kv_count + index) * HEAD_SIZE
                result.append(
                    pltpu.make_async_copy(
                        scr.at[index, rows, pl.ds(kind * HEAD_SIZE, HEAD_SIZE)],
                        bufs[flip].at[:, pl.ds(place, HEAD_SIZE)],
                        sems.at[index, flip, kind],
                    )
                )
        return result

    for index in range(kv_count):

        @pl.when(step == index)
        def _(index=index):
            for copy in copies(index):
                copy.start()

    @pl.when(step == kv_count - 1)
    def _():
        for index in range(kv_count):
            for copy in copies(index):
                copy.wait()


def finish_call(kv_count, owners, column, scal, part, back, bufs, after=()):
    tok_local = part.shape[0]
    chunk = tok_local // owners
    aliased = bufs is not None
    shape = jax.ShapeDtypeStruct((chunk, column + kv_count * 2 * HEAD_SIZE), jnp.bfloat16)
    any_spec = pl.BlockSpec(memory_space=pl.ANY)
    return pl.pallas_call(
        functools.partial(
            finish_kernel, kv_count, owners, column, len(after) + (owners if aliased else 0)
        ),
        grid=(kv_count,),
        in_specs=[
            pl.BlockSpec(memory_space=pltpu.SMEM),
            pl.BlockSpec((tok_local, 2 * HEAD_SIZE), lambda g: (0, g)),
            pl.BlockSpec((WINDOW_LENGTH, 2 * HEAD_SIZE), lambda g: (0, g)),
        ]
        + [any_spec] * ((owners if aliased else 0) + len(after)),
        out_specs=[any_spec] * owners,
        out_shape=[shape] * owners,
        input_output_aliases={3 + i: i for i in range(owners)} if aliased else {},
        scratch_shapes=[
            pltpu.VMEM((kv_count, tok_local, 2 * HEAD_SIZE), jnp.bfloat16),
            pltpu.SemaphoreType.DMA((kv_count, owners, 2)),
        ],
        compiler_params=pltpu.CompilerParams(vmem_limit_bytes=16 * MIB),
        cost_estimate=pl.CostEstimate(
            flops=0, bytes_accessed=16 * tok_local * kv_count * HEAD_SIZE, transcendentals=0
        ),
        name="finish",
    )(scal, part, back, *(bufs if aliased else ()), *after)


def place_kernel(plans, owners, group, kv_local, skip, scal, *rest):
    blocks = rest[: owners * len(plans)]
    outs = rest[skip:][:3]
    scrs = rest[skip + 3 : skip + 3 + len(plans)]
    in_sems, out_sems = rest[skip + 3 + len(plans) :]
    me = scal[0]
    loads = [
        pltpu.make_async_copy(
            blocks[number * owners + flip], scrs[number].at[flip], in_sems.at[number, flip]
        )
        for number in range(len(plans))
        for flip in range(owners)
    ]
    for load in loads:
        load.start()
    stores = []
    for number, plan in enumerate(plans):
        for flip in range(owners):
            loads[number * owners + flip].wait()
            source = jnp.bitwise_xor(me, flip)
            column = 0
            for which, (layer, kv_first, kv_count) in plan:
                heads = kv_count * group if which == 0 else kv_count
                home = kv_local * group if which == 0 else kv_local
                first = kv_first * group if which == 0 else kv_first
                place = pl.multiple_of((source * home + first) * HEAD_SIZE, HEAD_SIZE)
                store = pltpu.make_async_copy(
                    scrs[number].at[flip, :, pl.ds(column, heads * HEAD_SIZE)],
                    outs[which].at[layer, :, pl.ds(place, heads * HEAD_SIZE)],
                    out_sems.at[len(stores)],
                )
                store.start()
                stores.append(store)
                column += heads * HEAD_SIZE
    for store in stores:
        store.wait()


def place_call(sends, owners, group, kv_local, scal, outs):
    plans = [plan for plan, _ in sends]
    blocks = [block for _, some in sends for block in some]
    aliased = outs is not None
    any_spec = pl.BlockSpec(memory_space=pl.ANY)
    chunk = blocks[0].shape[0]
    shapes = [
        jax.ShapeDtypeStruct(
            (SLIDING_LAYERS, chunk, owners * heads * HEAD_SIZE), jnp.bfloat16
        )
        for heads in (kv_local * group, kv_local, kv_local)
    ]
    skip = len(blocks) + (3 if aliased else 0)
    return pl.pallas_call(
        functools.partial(place_kernel, plans, owners, group, kv_local, skip),
        in_specs=[pl.BlockSpec(memory_space=pltpu.SMEM)] + [any_spec] * skip,
        out_specs=[any_spec] * 3,
        out_shape=shapes,
        input_output_aliases={1 + len(blocks) + i: i for i in range(3)} if aliased else {},
        scratch_shapes=[
            pltpu.VMEM((owners,) + some[0].shape, jnp.bfloat16) for _, some in sends
        ]
        + [
            pltpu.SemaphoreType.DMA((len(plans), owners)),
            pltpu.SemaphoreType.DMA((owners * sum(len(plan) for plan in plans),)),
        ],
        compiler_params=pltpu.CompilerParams(vmem_limit_bytes=24 * MIB),
        cost_estimate=pl.CostEstimate(
            flops=0,
            bytes_accessed=sum(block.shape[0] * block.shape[1] * 4 for block in blocks),
            transcendentals=0,
        ),
        name="place",
    )(scal, *blocks, *(outs if aliased else ()))


def shards(queries, layer_keys_input, layer_values_input, attn_out, grad_out, log_norm, window):
    tok_local = queries.shape[1]
    kv_local = layer_keys_input.shape[2] // HEAD_SIZE
    group = queries.shape[2] // layer_keys_input.shape[2]
    owners = lax.axis_size("head")
    shard = lax.axis_index("ctx")
    scal = jnp.concatenate(
        [
            jnp.stack([lax.axis_index("head"), (shard == 0).astype(jnp.int32)]).astype(jnp.int32),
            window.astype(jnp.int32),
        ]
    )
    pieces = []
    for layer in range(SLIDING_LAYERS):
        kv_first = 0
        while kv_first < kv_local:
            kv_count = 1
            pieces.append((layer, kv_first, kv_count))
            kv_first += kv_count

    plans = [[(0, 0, 1)], [(0, 1, kv_local - 1)], [(1, 0, kv_local)]]
    packed = pack_call(plans[0], layer_keys_input, layer_values_input)
    packed += pack_call(plans[1] + plans[2], layer_keys_input, layer_values_input)
    halos = [shifted(block, "ctx", 1) for block in packed]

    def halo_of(layer, kv_first):
        if layer == 1:
            return halos[2], kv_first
        return (halos[0], 0) if kv_first == 0 else (halos[1], kv_first - 1)

    waiting = None
    token = scal
    sent = []

    def send(plan, bufs):
        blocks = [bufs[0]] + [swapped(bufs[flip], "head", flip) for flip in range(1, owners)]
        sent.append((plan, blocks))

    for index, piece in enumerate(pieces):
        layer, kv_first, kv_count = piece
        halo, column = halo_of(layer, kv_first)
        extra = 0 if waiting is None else 2 * waiting[0][2]
        after = [token]
        if index >= 2:
            after += sent[index - 2][1][1:]
        if index == 2:
            after.append(halos[2])
        bufs, back, part = band_call(
            piece,
            extra,
            owners,
            scal,
            queries,
            grad_out,
            attn_out,
            log_norm,
            layer_keys_input,
            layer_values_input,
            halo,
            column,
            after,
        )
        token = part
        back = shifted(back, "ctx", -1)
        plan = [(0, piece)]
        if waiting is not None:
            old, old_part, old_back = waiting
            last = sent[-1][1][1:] if index == len(pieces) - 1 else ()
            bufs = finish_call(
                old[2], owners, kv_count * group * HEAD_SIZE, scal, old_part, old_back, bufs, last
            )
            token = bufs[0]
            plan += [(1, old), (2, old)]
        send(plan, bufs)
        waiting = (piece, part, back)
    old, old_part, old_back = waiting
    bufs = finish_call(old[2], owners, 0, scal, old_part, old_back, None)
    send([(1, old), (2, old)], bufs)
    outs = place_call(sent[:-2], owners, group, kv_local, scal, None)
    outs = place_call(sent[-2:], owners, group, kv_local, scal, outs)
    return tuple(outs)


def solution(mesh):
    in_specs = (
        P(None, "ctx", "head"),
        P(None, "ctx", "head"),
        P(None, "ctx", "head"),
        P(None, "ctx", "head"),
        P(None, "ctx", "head"),
        P(None, "head", "ctx"),
        P(),
    )
    out_specs = (
        P(None, ("ctx", "head"), None),
        P(None, ("ctx", "head"), None),
        P(None, ("ctx", "head"), None),
    )
    return jax.shard_map(shards, mesh=mesh, in_specs=in_specs, out_specs=out_specs, check_vma=False)
```

```python
import functools
import math

import jax
import jax.numpy as jnp
from jax import lax
from jax.experimental import pallas as pl
from jax.experimental.pallas import tpu as pltpu
from jax.sharding import PartitionSpec as P

HEAD_SIZE = 128
WINDOW_LENGTH = 1024
QUERY_PRE = 168
SLIDING_LAYERS = 2
TILE = 128
UNITS = 4
SCALE = QUERY_PRE ** (-0.5)
LOG2E = math.log2(math.e)
FAR = 1e30
MIB = 1024 * 1024

NT = (((1,), (1,)), ((), ()))
NN = (((1,), (0,)), ((), ()))


def dot(a, b, dims=NN):
    return lax.dot_general(a, b, dims, preferred_element_type=jnp.float32)


def shifted(value, axis, steps):
    count = lax.axis_size(axis)
    first, last = (max(0, -steps), min(count, count - steps))
    return lax.ppermute(value, axis, [(source, source + steps) for source in range(first, last)])


def swapped(value, axis, flip):
    count = lax.axis_size(axis)
    return lax.ppermute(value, axis, [(source, source ^ flip) for source in range(count)])


def pack_kernel(plan, rows, *rest):
    count = len(plan)
    keys, values = rest[:2]
    outs = rest[2 : 2 + count]
    scrs = rest[2 + count : 2 + 2 * count]
    in_sems, out_sems = rest[2 + 2 * count :]
    loads = []
    for index, (layer, kv_first, kv_count) in enumerate(plan):
        width = kv_count * HEAD_SIZE
        for kind, array in enumerate((keys, values)):
            loads.append(
                pltpu.make_async_copy(
                    array.at[layer, rows, pl.ds(kv_first * HEAD_SIZE, width)],
                    scrs[index].at[:, pl.ds(kind * width, width)],
                    in_sems.at[index, kind],
                )
            )
    for load in loads:
        load.start()
    stores = []
    for index in range(count):
        loads[2 * index].wait()
        loads[2 * index + 1].wait()
        store = pltpu.make_async_copy(scrs[index], outs[index], out_sems.at[index])
        store.start()
        stores.append(store)
    for store in stores:
        store.wait()


def pack_call(plan, keys, values):
    tok_local = keys.shape[1]
    any_spec = pl.BlockSpec(memory_space=pl.ANY)
    sizes = [(WINDOW_LENGTH, 2 * kv_count * HEAD_SIZE) for _, _, kv_count in plan]
    return pl.pallas_call(
        functools.partial(pack_kernel, plan, pl.ds(tok_local - WINDOW_LENGTH, WINDOW_LENGTH)),
        in_specs=[any_spec] * 2,
        out_specs=[any_spec] * len(plan),
        out_shape=[jax.ShapeDtypeStruct(size, jnp.bfloat16) for size in sizes],
        scratch_shapes=[pltpu.VMEM(size, jnp.bfloat16) for size in sizes]
        + [pltpu.SemaphoreType.DMA((len(plan), 2)), pltpu.SemaphoreType.DMA((len(plan),))],
        compiler_params=pltpu.CompilerParams(vmem_limit_bytes=60 * MIB),
        cost_estimate=pl.CostEstimate(
            flops=0, bytes_accessed=4 * sum(size[0] * size[1] for size in sizes), transcendentals=0
        ),
        name="pack",
    )(keys, values)


def band_kernel(
    layer,
    kv_first,
    kv_count,
    owners,
    skip,
    scal,
    q_ref,
    do_ref,
    out_ref,
    lse_ref,
    k_ref,
    v_ref,
    k_halo,
    v_halo,
    *rest,
):
    dq_bufs = rest[skip:][:owners]
    back_ref, part_ref, kx, vx, kt, acc, lse2_scr, dq_scr, sems = rest[skip + owners :]
    tok_local = q_ref.shape[1]
    group = q_ref.shape[2] // HEAD_SIZE
    chunk = tok_local // owners
    step = pl.program_id(0)
    me = scal[0]
    first_shard = scal[1]
    win = scal[2 + layer]
    wide = group * TILE

    rows_step = UNITS * TILE
    head = (kv_first + step) * group

    kx[0:WINDOW_LENGTH] = k_halo[...]
    vx[0:WINDOW_LENGTH] = v_halo[...]
    kx[WINDOW_LENGTH:] = k_ref[0]
    vx[WINDOW_LENGTH:] = v_ref[0]
    kt[:, 0:WINDOW_LENGTH] = k_halo[...].T
    for h in range(group):
        lse2_scr[h : h + 1, :] = lse_ref[0, pl.ds(head + h, 1), :] * LOG2E
    acc[0:WINDOW_LENGTH] = jnp.zeros((WINDOW_LENGTH, 2 * HEAD_SIZE), jnp.float32)

    rows = lax.broadcasted_iota(jnp.int32, (TILE, wide), 0)
    lanes = lax.broadcasted_iota(jnp.int32, (1, wide), 1) % TILE
    left = lax.broadcasted_iota(jnp.int32, (1, HEAD_SIZE), 1) < HEAD_SIZE // 2

    def stacked(ref, start):
        block = ref[0, pl.ds(start, TILE), :]
        return jnp.concatenate(
            [block[:, h * HEAD_SIZE : (h + 1) * HEAD_SIZE] for h in range(group)], 0
        )

    def sweep(reach):
        tiles = reach // TILE + 1
        skipped = WINDOW_LENGTH - reach
        minus = jnp.full((tiles * TILE, HEAD_SIZE), -1, jnp.bfloat16)

        def one_step(index, carry):
            start = pl.multiple_of(index * rows_step, rows_step)
            fresh = pl.ds(pl.multiple_of(start + WINDOW_LENGTH, TILE), rows_step)
            kt[:, fresh] = kx[fresh, :].T
            acc[fresh, :] = jnp.zeros((rows_step, 2 * HEAD_SIZE), jnp.float32)

            def products(unit):
                begin = pl.multiple_of(start + unit * TILE, TILE)
                q2 = stacked(q_ref, begin)
                do2 = stacked(do_ref, begin)
                span = pl.ds(pl.multiple_of(begin + skipped, TILE), tiles * TILE)
                prod = do2.astype(jnp.float32) * stacked(out_ref, begin).astype(jnp.float32)
                pair = prod + pltpu.roll(prod, HEAD_SIZE // 2, 1)
                coarse = pair.astype(jnp.bfloat16).astype(jnp.float32)
                terms = jnp.where(left, coarse, pair - coarse).astype(jnp.bfloat16)
                scores = dot(kx[span, :], q2, NT)
                lead = jnp.concatenate([vx[span, :], minus], 1)
                excess = dot(lead, jnp.concatenate([do2, terms], 1), NT)
                lse2 = jnp.concatenate(
                    [lse2_scr[h : h + 1, pl.ds(begin, TILE)] for h in range(group)], 1
                )
                return begin, q2, do2, scores, excess, lse2

            def weights(begin, q2, do2, scores, excess, lse2):
                probs, grads = [], []
                for tile in range(tiles):
                    part = slice(tile * TILE, (tile + 1) * TILE)
                    line = lse2
                    if tile < tiles - 1:
                        outside = jnp.logical_and(
                            first_shard == 1, begin + skipped + tile * TILE < WINDOW_LENGTH
                        )
                        line = jnp.where(outside, FAR, lse2)
                    prob = jnp.exp2(scores[part] * (SCALE * LOG2E) - line)
                    if tile == tiles - 1:
                        prob = jnp.where(rows <= lanes, prob, 0.0)
                    elif tile < 3:
                        prob = jnp.where(rows > lanes + (reach - win - tile * TILE), prob, 0.0)
                    probs.append(prob.astype(jnp.bfloat16))
                    grads.append((prob * excess[part]).astype(jnp.bfloat16))
                return begin, q2, do2, probs, grads

            def finish(first, second):
                begin = first[0]
                for lefts, rights, kind in ((3, 2, 1), (4, 1, 0)):
                    one, two = first[lefts], second[lefts]
                    side = slice(kind * HEAD_SIZE, (kind + 1) * HEAD_SIZE)
                    base = begin + skipped
                    middle = jnp.concatenate(
                        [jnp.concatenate(one[1:], 0), jnp.concatenate(two[:-1], 0)], 1
                    )
                    both = jnp.concatenate([first[rights], second[rights]], 0)
                    acc[pl.ds(pl.multiple_of(base, TILE), TILE), side] += dot(one[0], first[rights])
                    acc[pl.ds(pl.multiple_of(base + TILE, TILE), (tiles - 1) * TILE), side] += dot(
                        middle, both
                    )
                    acc[pl.ds(pl.multiple_of(base + tiles * TILE, TILE), TILE), side] += dot(
                        two[-1], second[rights]
                    )
                for begin, _, _, _, grads in (first, second):
                    span = pl.ds(pl.multiple_of(begin + skipped, TILE), tiles * TILE)
                    dq = (dot(kt[:, span], jnp.concatenate(grads, 0)).T * SCALE).astype(jnp.bfloat16)
                    for h in range(group):
                        dq_scr[step, pl.ds(begin, TILE), h * HEAD_SIZE : (h + 1) * HEAD_SIZE] = dq[
                            h * TILE : (h + 1) * TILE
                        ]

            held = products(0)
            done = []
            for unit in range(UNITS):
                coming = products(unit + 1) if unit + 1 < UNITS else None
                done.append(weights(*held))
                held = coming
                if unit % 2 == 1:
                    finish(done[unit - 1], done[unit])
            return carry

        lax.fori_loop(0, tok_local // rows_step, one_step, 0)

    low = 0
    for reach in (WINDOW_LENGTH * 3 // 4, WINDOW_LENGTH):

        @pl.when(jnp.logical_and(win > low, win <= reach))
        def _(reach=reach):
            sweep(reach)

        low = reach

    back_ref[:, :HEAD_SIZE] = (acc[0:WINDOW_LENGTH, :HEAD_SIZE] * SCALE).astype(jnp.bfloat16)
    back_ref[:, HEAD_SIZE:] = acc[0:WINDOW_LENGTH, HEAD_SIZE:].astype(jnp.bfloat16)
    part_ref[:, :HEAD_SIZE] = acc[WINDOW_LENGTH:, :HEAD_SIZE] * SCALE
    part_ref[:, HEAD_SIZE:] = acc[WINDOW_LENGTH:, HEAD_SIZE:]

    def copies(index):
        result = []
        for flip in range(owners):
            owner = jnp.bitwise_xor(me, flip)
            source = dq_scr.at[index, pl.ds(pl.multiple_of(owner * chunk, chunk), chunk), :]
            target = dq_bufs[flip].at[:, pl.ds(index * group * HEAD_SIZE, group * HEAD_SIZE)]
            result.append(pltpu.make_async_copy(source, target, sems.at[index, flip]))
        return result

    for index in range(kv_count):

        @pl.when(step == index)
        def _(index=index):
            for copy in copies(index):
                copy.start()

    @pl.when(step == kv_count - 1)
    def _():
        for index in range(kv_count):
            for copy in copies(index):
                copy.wait()


def band_call(piece, extra, owners, scal, queries, grad_out, attn_out, log_norm, keys, values, halo, column, after):
    layer, kv_first, kv_count = piece
    tok_local = queries.shape[1]
    group = queries.shape[2] // keys.shape[2]
    span = WINDOW_LENGTH + tok_local
    chunk = tok_local // owners
    halo_kv = halo.shape[1] // (2 * HEAD_SIZE)
    q_spec = pl.BlockSpec((1, tok_local, group * HEAD_SIZE), lambda g: (layer, 0, kv_first + g))
    kv_spec = pl.BlockSpec((1, tok_local, HEAD_SIZE), lambda g: (layer, 0, kv_first + g))
    pairs = tok_local * (WINDOW_LENGTH + 2 * TILE) * group * kv_count
    outs = pl.pallas_call(
        functools.partial(band_kernel, layer, kv_first, kv_count, owners, len(after)),
        grid=(kv_count,),
        in_specs=[
            pl.BlockSpec(memory_space=pltpu.SMEM),
            q_spec,
            q_spec,
            q_spec,
            pl.BlockSpec((1,) + log_norm.shape[1:], lambda g: (layer, 0, 0)),
            kv_spec,
            kv_spec,
            pl.BlockSpec((WINDOW_LENGTH, HEAD_SIZE), lambda g: (0, column + g)),
            pl.BlockSpec((WINDOW_LENGTH, HEAD_SIZE), lambda g: (0, halo_kv + column + g)),
        ]
        + [pl.BlockSpec(memory_space=pl.ANY)] * len(after),
        out_specs=[pl.BlockSpec(memory_space=pl.ANY)] * owners
        + [
            pl.BlockSpec((WINDOW_LENGTH, 2 * HEAD_SIZE), lambda g: (0, g)),
            pl.BlockSpec((tok_local, 2 * HEAD_SIZE), lambda g: (0, g)),
        ],
        out_shape=[
            jax.ShapeDtypeStruct((chunk, (kv_count * group + extra) * HEAD_SIZE), jnp.bfloat16)
        ]
        * owners
        + [
            jax.ShapeDtypeStruct((WINDOW_LENGTH, kv_count * 2 * HEAD_SIZE), jnp.bfloat16),
            jax.ShapeDtypeStruct((tok_local, kv_count * 2 * HEAD_SIZE), jnp.float32),
        ],
        scratch_shapes=[
            pltpu.VMEM((span, HEAD_SIZE), jnp.bfloat16),
            pltpu.VMEM((span, HEAD_SIZE), jnp.bfloat16),
            pltpu.VMEM((HEAD_SIZE, span), jnp.bfloat16),
            pltpu.VMEM((span, 2 * HEAD_SIZE), jnp.float32),
            pltpu.VMEM((8, tok_local), jnp.float32),
            pltpu.VMEM((kv_count, tok_local, group * HEAD_SIZE), jnp.bfloat16),
            pltpu.SemaphoreType.DMA((kv_count, owners)),
        ],
        compiler_params=pltpu.CompilerParams(vmem_limit_bytes=40 * MIB),
        cost_estimate=pl.CostEstimate(
            flops=pairs * 2 * HEAD_SIZE * 5 * 4,
            bytes_accessed=8 * tok_local * group * kv_count * HEAD_SIZE,
            transcendentals=pairs,
        ),
        name="band",
    )(scal, queries, grad_out, attn_out, log_norm, keys, values, halo, halo, *after)
    return outs[:owners], outs[owners], outs[owners + 1]


def finish_kernel(kv_count, owners, column, skip, scal, part_ref, back_ref, *rest):
    bufs = rest[skip:][:owners]
    scr, sems = rest[-2:]
    tok_local = part_ref.shape[0]
    chunk = tok_local // owners
    step = pl.program_id(0)
    me = scal[0]
    plain = tok_local - WINDOW_LENGTH
    scr[step, :plain] = part_ref[:plain].astype(jnp.bfloat16)
    scr[step, plain:] = (part_ref[plain:] + back_ref[...].astype(jnp.float32)).astype(jnp.bfloat16)

    def copies(index):
        result = []
        for flip in range(owners):
            owner = jnp.bitwise_xor(me, flip)
            rows = pl.ds(pl.multiple_of(owner * chunk, chunk), chunk)
            for kind in range(2):
                place = column + (kind * kv_count + index) * HEAD_SIZE
                result.append(
                    pltpu.make_async_copy(
                        scr.at[index, rows, pl.ds(kind * HEAD_SIZE, HEAD_SIZE)],
                        bufs[flip].at[:, pl.ds(place, HEAD_SIZE)],
                        sems.at[index, flip, kind],
                    )
                )
        return result

    for index in range(kv_count):

        @pl.when(step == index)
        def _(index=index):
            for copy in copies(index):
                copy.start()

    @pl.when(step == kv_count - 1)
    def _():
        for index in range(kv_count):
            for copy in copies(index):
                copy.wait()


def finish_call(kv_count, owners, column, scal, part, back, bufs, after=()):
    tok_local = part.shape[0]
    chunk = tok_local // owners
    aliased = bufs is not None
    shape = jax.ShapeDtypeStruct((chunk, column + kv_count * 2 * HEAD_SIZE), jnp.bfloat16)
    any_spec = pl.BlockSpec(memory_space=pl.ANY)
    return pl.pallas_call(
        functools.partial(
            finish_kernel, kv_count, owners, column, len(after) + (owners if aliased else 0)
        ),
        grid=(kv_count,),
        in_specs=[
            pl.BlockSpec(memory_space=pltpu.SMEM),
            pl.BlockSpec((tok_local, 2 * HEAD_SIZE), lambda g: (0, g)),
            pl.BlockSpec((WINDOW_LENGTH, 2 * HEAD_SIZE), lambda g: (0, g)),
        ]
        + [any_spec] * ((owners if aliased else 0) + len(after)),
        out_specs=[any_spec] * owners,
        out_shape=[shape] * owners,
        input_output_aliases={3 + i: i for i in range(owners)} if aliased else {},
        scratch_shapes=[
            pltpu.VMEM((kv_count, tok_local, 2 * HEAD_SIZE), jnp.bfloat16),
            pltpu.SemaphoreType.DMA((kv_count, owners, 2)),
        ],
        compiler_params=pltpu.CompilerParams(vmem_limit_bytes=16 * MIB),
        cost_estimate=pl.CostEstimate(
            flops=0, bytes_accessed=16 * tok_local * kv_count * HEAD_SIZE, transcendentals=0
        ),
        name="finish",
    )(scal, part, back, *(bufs if aliased else ()), *after)


def place_kernel(plans, owners, group, kv_local, skip, scal, *rest):
    blocks = rest[: owners * len(plans)]
    outs = rest[skip:][:3]
    scrs = rest[skip + 3 : skip + 3 + len(plans)]
    in_sems, out_sems = rest[skip + 3 + len(plans) :]
    me = scal[0]
    loads = [
        pltpu.make_async_copy(
            blocks[number * owners + flip], scrs[number].at[flip], in_sems.at[number, flip]
        )
        for number in range(len(plans))
        for flip in range(owners)
    ]
    for load in loads:
        load.start()
    stores = []
    for number, plan in enumerate(plans):
        for flip in range(owners):
            loads[number * owners + flip].wait()
            source = jnp.bitwise_xor(me, flip)
            column = 0
            for which, (layer, kv_first, kv_count) in plan:
                heads = kv_count * group if which == 0 else kv_count
                home = kv_local * group if which == 0 else kv_local
                first = kv_first * group if which == 0 else kv_first
                place = pl.multiple_of((source * home + first) * HEAD_SIZE, HEAD_SIZE)
                store = pltpu.make_async_copy(
                    scrs[number].at[flip, :, pl.ds(column, heads * HEAD_SIZE)],
                    outs[which].at[layer, :, pl.ds(place, heads * HEAD_SIZE)],
                    out_sems.at[len(stores)],
                )
                store.start()
                stores.append(store)
                column += heads * HEAD_SIZE
    for store in stores:
        store.wait()


def place_call(sends, owners, group, kv_local, scal, outs):
    plans = [plan for plan, _ in sends]
    blocks = [block for _, some in sends for block in some]
    aliased = outs is not None
    any_spec = pl.BlockSpec(memory_space=pl.ANY)
    chunk = blocks[0].shape[0]
    shapes = [
        jax.ShapeDtypeStruct(
            (SLIDING_LAYERS, chunk, owners * heads * HEAD_SIZE), jnp.bfloat16
        )
        for heads in (kv_local * group, kv_local, kv_local)
    ]
    skip = len(blocks) + (3 if aliased else 0)
    return pl.pallas_call(
        functools.partial(place_kernel, plans, owners, group, kv_local, skip),
        in_specs=[pl.BlockSpec(memory_space=pltpu.SMEM)] + [any_spec] * skip,
        out_specs=[any_spec] * 3,
        out_shape=shapes,
        input_output_aliases={1 + len(blocks) + i: i for i in range(3)} if aliased else {},
        scratch_shapes=[
            pltpu.VMEM((owners,) + some[0].shape, jnp.bfloat16) for _, some in sends
        ]
        + [
            pltpu.SemaphoreType.DMA((len(plans), owners)),
            pltpu.SemaphoreType.DMA((owners * sum(len(plan) for plan in plans),)),
        ],
        compiler_params=pltpu.CompilerParams(vmem_limit_bytes=24 * MIB),
        cost_estimate=pl.CostEstimate(
            flops=0,
            bytes_accessed=sum(block.shape[0] * block.shape[1] * 4 for block in blocks),
            transcendentals=0,
        ),
        name="place",
    )(scal, *blocks, *(outs if aliased else ()))


def shards(queries, layer_keys_input, layer_values_input, attn_out, grad_out, log_norm, window):
    tok_local = queries.shape[1]
    kv_local = layer_keys_input.shape[2] // HEAD_SIZE
    group = queries.shape[2] // layer_keys_input.shape[2]
    owners = lax.axis_size("head")
    shard = lax.axis_index("ctx")
    scal = jnp.concatenate(
        [
            jnp.stack([lax.axis_index("head"), (shard == 0).astype(jnp.int32)]).astype(jnp.int32),
            window.astype(jnp.int32),
        ]
    )
    pieces = []
    for layer in range(SLIDING_LAYERS):
        kv_first = 0
        while kv_first < kv_local:
            kv_count = 1
            pieces.append((layer, kv_first, kv_count))
            kv_first += kv_count

    plans = [[(0, 0, 1)], [(0, 1, kv_local - 1)], [(1, 0, kv_local)]]
    packed = pack_call(plans[0], layer_keys_input, layer_values_input)
    packed += pack_call(plans[1] + plans[2], layer_keys_input, layer_values_input)
    halos = [shifted(block, "ctx", 1) for block in packed]

    def halo_of(layer, kv_first):
        if layer == 1:
            return halos[2], kv_first
        return (halos[0], 0) if kv_first == 0 else (halos[1], kv_first - 1)

    waiting = None
    token = scal
    sent = []

    def send(plan, bufs):
        blocks = [bufs[0]] + [swapped(bufs[flip], "head", flip) for flip in range(1, owners)]
        sent.append((plan, blocks))

    for index, piece in enumerate(pieces):
        layer, kv_first, kv_count = piece
        halo, column = halo_of(layer, kv_first)
        extra = 0 if waiting is None else 2 * waiting[0][2]
        after = [token]
        if index >= 2:
            after += sent[index - 2][1][1:]
        if index == 2:
            after.append(halos[2])
        bufs, back, part = band_call(
            piece,
            extra,
            owners,
            scal,
            queries,
            grad_out,
            attn_out,
            log_norm,
            layer_keys_input,
            layer_values_input,
            halo,
            column,
            after,
        )
        token = part
        back = shifted(back, "ctx", -1)
        plan = [(0, piece)]
        if waiting is not None:
            old, old_part, old_back = waiting
            last = sent[-1][1][1:] if index == len(pieces) - 1 else ()
            bufs = finish_call(
                old[2], owners, kv_count * group * HEAD_SIZE, scal, old_part, old_back, bufs, last
            )
            token = bufs[0]
            plan += [(1, old), (2, old)]
        send(plan, bufs)
        waiting = (piece, part, back)
    old, old_part, old_back = waiting
    bufs = finish_call(
        old[2], owners, 0, scal, old_part, old_back, None, sent[-1][1][1:2]
    )
    send([(1, old), (2, old)], bufs)
    outs = place_call(sent[:-2], owners, group, kv_local, scal, None)
    outs = place_call(sent[-2:-1], owners, group, kv_local, scal, outs)
    outs = place_call(sent[-1:], owners, group, kv_local, scal, outs)
    return tuple(outs)


def solution(mesh):
    in_specs = (
        P(None, "ctx", "head"),
        P(None, "ctx", "head"),
        P(None, "ctx", "head"),
        P(None, "ctx", "head"),
        P(None, "ctx", "head"),
        P(None, "head", "ctx"),
        P(),
    )
    out_specs = (
        P(None, ("ctx", "head"), None),
        P(None, ("ctx", "head"), None),
        P(None, ("ctx", "head"), None),
    )
    return jax.shard_map(shards, mesh=mesh, in_specs=in_specs, out_specs=out_specs, check_vma=False)
```
